256 devices in a mesh: ctx: 16 (over y, z_lo), head: 8 (over x, core), grp: 2 (over z_hi).
Axes of the slice: x: 4, y: 4, z: 8 (z_hi: 2, z_lo: 4; z = z_hi * 4 + z_lo), core: 2. Of those that a mesh axis runs over, the one named last changes fastest.
Arguments:
- span_q: bfloat16 [2, 2048, 8192], P('grp', 'ctx', 'head'), may hold values from -6 to 6
- span_kv: bfloat16 [2, 2, 2048, 1024], P('grp', None, 'ctx', 'head'), may hold values from -6 to 6
- prefix_kv: bfloat16 [2, 2, 14336, 1024], P('grp', None, 'ctx', 'head'), may hold values from -6 to 6
- prefix_len: int32 [2], P('grp'), may hold values from 7168 to 14336, as said below
- dec_q: bfloat16 [2, 256, 4, 8192], P('grp', 'ctx', None, 'head'), may hold values from -6 to 6
- dec_new_kv: bfloat16 [2, 2, 256, 4, 1024], P('grp', None, 'ctx', None, 'head'), may hold values from -6 to 6
- dec_cache: bfloat16 [2, 2, 256, 512, 1024], P('grp', None, 'ctx', None, 'head'), may hold values from -6 to 6
- cache_len: int32 [2, 256], P('grp', 'ctx'), may hold values from 32 to 512, as said below
- prompt_row: int32 [2], P('grp'), may hold values from 0 to 255
- out_weight: bfloat16 [8192, 8192], P('head', 'ctx'), may hold values from -0.0625 to 0.0625
Outputs:
- prefill_out: bfloat16 [2, 2048, 8192], P('grp', 'ctx', 'head')
- decode_out: bfloat16 [2, 256, 4, 8192], P('grp', 'head', None, 'ctx')
The draws below stay inside these ranges and needn't reach their ends.
Inputs may be any that keep to these rules, and one draw needn't show every extreme that they name: `prefix_len`: some group uses all 14336 prefix slots. `cache_len`: some row of each group uses all 512 slots.
All inputs are finite; a program needn't handle non-finite values.
Results may differ from the reference program's by a relative error of at most 0.019.
Values may be sent and summed in bfloat16 or wider, within the bound.
A program may use at most 192 MiB of HBM per device.

```python
import math
import jax
import jax.numpy as jnp
from jax import lax

D = 8192
QH = 64
KVH = 8
HD = 128
CACHE = 512
STEPS = 4
GROUPS = 2
GQ = 8
SPAN = 2048
PRE = 14336
ROWS = 256


def draw_span_q(key, part):
    key = jax.random.fold_in(key, 1)
    shape = (GROUPS, SPAN, QH * HD)
    values = 1.6 * jax.random.truncated_normal(key, -3.75, 3.75, shape, jnp.float32)
    return values.astype(jnp.bfloat16)


def draw_prefix_kv(key, part):
    key = jax.random.fold_in(key, 2)
    shape = (GROUPS, 2, PRE, KVH * HD)
    values = 1.6 * jax.random.truncated_normal(key, -3.75, 3.75, shape, jnp.float32)
    return values.astype(jnp.bfloat16)


def draw_dec_q(key, part):
    key = jax.random.fold_in(key, 3)
    shape = (GROUPS, ROWS, STEPS, QH * HD)
    values = 1.6 * jax.random.truncated_normal(key, -3.75, 3.75, shape, jnp.float32)
    return values.astype(jnp.bfloat16)


def draw_dec_cache(key, part):
    key = jax.random.fold_in(key, 4)
    shape = (GROUPS, 2, ROWS, CACHE, KVH * HD)
    values = 1.6 * jax.random.truncated_normal(key, -3.75, 3.75, shape, jnp.float32)
    return values.astype(jnp.bfloat16)


def draw_prefix_len(key, part):
    key = jax.random.fold_in(key, 5)
    first_key, second_key = jax.random.split(key)
    lengths = jax.random.randint(first_key, (GROUPS,), PRE // 2, PRE + 1)
    full_group = jax.random.randint(second_key, (), 0, GROUPS)
    return jnp.where(jnp.arange(GROUPS) == full_group, PRE, lengths).astype(jnp.int32)


def draw_cache_len(key, part):
    key = jax.random.fold_in(key, 6)
    first_key, second_key = jax.random.split(key)
    lengths = jax.random.randint(first_key, (GROUPS, ROWS), max(2, CACHE // 16), CACHE + 1)
    full_row = jax.random.randint(second_key, (GROUPS, 1), 0, ROWS)
    return jnp.where(jnp.arange(ROWS)[None, :] == full_row, CACHE, lengths).astype(jnp.int32)


def block_scale(key, dims, shards, low, top_value):
    def one(axis_at, blocks):
        heights = jax.random.uniform(jax.random.fold_in(jax.random.fold_in(key, 6), axis_at), (blocks,), jnp.float32, low / len(shards), top_value / len(shards))
        return jnp.repeat(jnp.exp(heights), dims[axis_at] // blocks).reshape((-1,) + (1,) * (len(dims) - axis_at - 1))

    factor_of = one(*shards[0])
    for cut in shards[1:]:
        factor_of = factor_of * one(*cut)
    return factor_of


def normal_values(own_key, extent, scale, most, shards=(), held_as=jnp.bfloat16):
    level = block_scale(own_key, extent, shards, -0.22, 0.18) if shards else 1.0
    result = jax.random.normal(own_key, extent, jnp.float32) * scale * level
    return jnp.minimum(jnp.maximum(result, -most), most).astype(held_as)


def setup_inputs(seed: int = 0) -> dict:
    splits = jax.random.split(jax.random.key(seed), 11)
    return {
        "span_q": draw_span_q(jax.random.fold_in(splits[10], 71), 0),
        "span_kv": normal_values(splits[1], (GROUPS, 2, SPAN, KVH * HD), 1.6, 6.0, ((0, 2), (2, 16), (3, 8))),
        "prefix_kv": draw_prefix_kv(jax.random.fold_in(splits[10], 71), 0),
        "prefix_len": draw_prefix_len(jax.random.fold_in(splits[10], 71), 0),
        "dec_q": draw_dec_q(jax.random.fold_in(splits[10], 71), 0),
        "dec_new_kv": normal_values(splits[5], (GROUPS, 2, ROWS, STEPS, KVH * HD), 1.6, 6.0, ((0, 2), (2, 16), (4, 8))),
        "dec_cache": draw_dec_cache(jax.random.fold_in(splits[10], 71), 0),
        "cache_len": draw_cache_len(jax.random.fold_in(splits[10], 71), 0),
        "prompt_row": jax.random.randint(splits[8], (GROUPS,), 0, ROWS).astype(jnp.int32),
        "out_weight": normal_values(splits[9], (QH * HD, D), (QH * HD) ** -0.5, 0.0625, ((0, 8), (1, 16))),
    }


MASKED_SCORE = -1e+30

def prefill_group(queries, prefix, span, prefix_valid):
    score_scale = 1.0 / math.sqrt(HD)
    key_rows = jnp.concatenate([prefix[0], span[0]], axis=0)
    value_rows = jnp.concatenate([prefix[1], span[1]], axis=0)
    key_count = PRE + SPAN
    slot_ids = jnp.arange(key_count, dtype=jnp.int32)
    block_rows = math.gcd(SPAN, 256)

    def one_head(kv_head):
        head_keys = lax.dynamic_slice_in_dim(key_rows, kv_head * HD, HD, 1)
        head_values = lax.dynamic_slice_in_dim(value_rows, kv_head * HD, HD, 1)
        head_queries = lax.dynamic_slice_in_dim(queries, kv_head * GQ * HD, GQ * HD, 1)

        def one_block(block_id):
            query_rows = lax.dynamic_slice_in_dim(head_queries, block_id * block_rows, block_rows, 0)
            query_rows = query_rows.reshape(block_rows * GQ, HD)
            positions = block_id * block_rows + jnp.arange(block_rows, dtype=jnp.int32)
            usable = jnp.where(slot_ids[None, :] < PRE, slot_ids[None, :] < prefix_valid, slot_ids[None, :] - PRE <= positions[:, None])
            scores = jnp.dot(query_rows, head_keys.T, preferred_element_type=jnp.float32) * score_scale
            scores = scores.reshape(block_rows, GQ, key_count)
            masked = jnp.where(usable[:, None, :], scores, MASKED_SCORE)
            row_max = lax.optimization_barrier(jnp.max(masked, axis=-1, keepdims=True))
            weights = jnp.where(usable[:, None, :], jnp.exp(masked - row_max), 0.0)
            row_total = lax.optimization_barrier(jnp.sum(weights, axis=-1, keepdims=True))
            mixed = jnp.dot(weights.astype(jnp.bfloat16).reshape(block_rows * GQ, key_count), head_values, preferred_element_type=jnp.float32).reshape(block_rows, GQ, HD)
            return (mixed / row_total).astype(jnp.bfloat16)
        blocks = lax.map(one_block, jnp.arange(SPAN // block_rows, dtype=jnp.int32))
        return blocks.reshape(SPAN, GQ * HD)
    heads = lax.map(one_head, jnp.arange(KVH, dtype=jnp.int32))
    return jnp.transpose(heads, (1, 0, 2)).reshape(SPAN, QH * HD)

def decode_group(queries, new_kv, cache, lengths, prompt_index, migrated):
    score_scale = 1.0 / math.sqrt(HD)
    key_count = CACHE + SPAN + STEPS
    slot_ids = jnp.arange(key_count, dtype=jnp.int32)
    step_ids = jnp.arange(STEPS, dtype=jnp.int32)

    def one_row(row_index):
        row_queries = queries[row_index].reshape(STEPS, KVH, GQ, HD).astype(jnp.float32)
        key_rows = jnp.concatenate([cache[0, row_index], migrated[0], new_kv[0, row_index]], axis=0)
        value_rows = jnp.concatenate([cache[1, row_index], migrated[1], new_kv[1, row_index]], axis=0)
        key_rows = key_rows.reshape(key_count, KVH, HD).astype(jnp.float32)
        value_rows = value_rows.reshape(key_count, KVH, HD).astype(jnp.float32)
        usable = jnp.where(slot_ids[None, :] < CACHE, slot_ids[None, :] < lengths[row_index], jnp.where(slot_ids[None, :] < CACHE + SPAN, row_index == prompt_index, slot_ids[None, :] - CACHE - SPAN <= step_ids[:, None]))
        usable = usable[:, None, None, :]
        scores = jnp.einsum('skgd,lkd->skgl', row_queries, key_rows) * score_scale
        masked = jnp.where(usable, scores, MASKED_SCORE)
        row_max = lax.optimization_barrier(jnp.max(masked, axis=-1, keepdims=True))
        weights = jnp.where(usable, jnp.exp(masked - row_max), 0.0)
        row_total = lax.optimization_barrier(jnp.sum(weights, axis=-1))
        rounded = lax.optimization_barrier(weights.astype(jnp.bfloat16)).astype(jnp.float32)
        mixed = jnp.einsum('skgl,lkd->skgd', rounded, value_rows)
        return (mixed / row_total[..., None]).astype(jnp.bfloat16).reshape(STEPS, QH * HD)
    return lax.map(one_row, jnp.arange(ROWS, dtype=jnp.int32))

def reference(span_q, span_kv, prefix_kv, prefix_len, dec_q, dec_new_kv, dec_cache, cache_len, prompt_row, out_weight):
    prefill_parts = []
    decode_parts = []
    for group_id in range(GROUPS):
        partner = 1 - group_id
        prefill_parts.append(prefill_group(span_q[group_id], prefix_kv[group_id], span_kv[group_id], prefix_len[group_id]))
        attended = decode_group(dec_q[group_id], dec_new_kv[group_id], dec_cache[group_id], cache_len[group_id], prompt_row[group_id], span_kv[partner])
        projected = jnp.dot(attended.reshape(ROWS * STEPS, QH * HD), out_weight, preferred_element_type=jnp.float32)
        decode_parts.append(projected.astype(jnp.bfloat16).reshape(ROWS, STEPS, D))
    return (jnp.stack(prefill_parts, axis=0), jnp.stack(decode_parts, axis=0))
```

```python
import math

import jax
import jax.numpy as jnp
from jax import lax
from jax.experimental import pallas as pl
from jax.experimental.pallas import tpu as pltpu
from jax.sharding import PartitionSpec as P

HD = 128
GQ = 8
RING = 4
PRE = 896
SPAN = 128
KEYS = PRE + SPAN
ROWS = 16
STEPS = 4
SLOTS = 512
QROWS = STEPS * GQ
COLS = 512
MASKED = -1e30
LOG2E = math.log2(math.e)
SCALE = LOG2E / math.sqrt(HD)
MESH = pl.DeviceIdType.MESH
F32 = jnp.float32
BF16 = jnp.bfloat16
BLOCK = 512
VMEM_BYTES = 40 * 1024 * 1024

PIECES = (0, 1, 1, 1, 2, 2, 2, 2, 3, 3, 3, 3, 1, 0, 0, 0)
CHUNKS = (0, 0, 1, 2, 0, 1, 2, 3, 0, 1, 2, 3, 3, 1, 2, 3)


def dot_nt(a, b):
    return lax.dot_general(a, b, (((1,), (1,)), ((), ())), preferred_element_type=F32)


def dot_nn(a, b):
    return lax.dot_general(a, b, (((1,), (0,)), ((), ())), preferred_element_type=F32)


def log2(v):
    return jnp.log(v) * LOG2E


def iota(shape, axis):
    return lax.broadcasted_iota(jnp.int32, shape, axis)


def lookup(table, index):
    value = jnp.int32(table[0])
    for at, entry in enumerate(table[1:], 1):
        value = jnp.where(index == at, jnp.int32(entry), value)
    return value


def to_row(column):
    shape = column.shape
    return jnp.sum(jnp.where(iota(shape, 0) == iota(shape, 1), column, 0.0), axis=0, keepdims=True)


def to_column(row, count):
    shape = (count, HD)
    spread = jnp.broadcast_to(row, shape)
    return jnp.sum(jnp.where(iota(shape, 0) == iota(shape, 1), spread, 0.0), axis=1, keepdims=True)


def merge(parts):
    top = parts[0][1]
    for _, level in parts[1:]:
        top = jnp.maximum(top, level)
    weights = [jnp.exp2(level - top) for _, level in parts]
    total = weights[0]
    for w in weights[1:]:
        total = total + w
    mixed = parts[0][0] * weights[0]
    for (out, _), w in zip(parts[1:], weights[1:]):
        mixed = mixed + out * w
    return mixed / total, top + log2(total)


SCRATCH = {
    "kl": pltpu.VMEM((KEYS, HD), BF16),
    "kb": pltpu.VMEM((RING, 2 * HD, KEYS), BF16),
    "vb": pltpu.VMEM((RING, KEYS, HD), BF16),
    "qb": pltpu.VMEM((RING, GQ * SPAN, HD), BF16),
    "ts0": pltpu.VMEM((BLOCK, KEYS), F32),
    "ts1": pltpu.VMEM((BLOCK, KEYS), F32),
    "mx0": pltpu.VMEM((BLOCK, HD), F32),
    "mx1": pltpu.VMEM((BLOCK, HD), F32),
    "dq": pltpu.VMEM((ROWS, STEPS, GQ * HD), BF16),
    "nkv": pltpu.VMEM((2, ROWS, STEPS, HD), BF16),
    "acc": pltpu.VMEM((RING, GQ * SPAN, HD), F32),
    "top": pltpu.VMEM((RING, GQ * SPAN, HD), F32),
    "tot": pltpu.VMEM((RING, GQ * SPAN, HD), F32),
    "os": pltpu.VMEM((RING, GQ, SPAN, HD), BF16),
    "ls": pltpu.VMEM((RING, GQ, SPAN), F32),
    "orb": pltpu.VMEM((RING, GQ, SPAN, HD), BF16),
    "lrb": pltpu.VMEM((RING, GQ, SPAN), F32),
    "ck": pltpu.VMEM((ROWS, SLOTS, HD), BF16),
    "cv": pltpu.VMEM((ROWS, SLOTS, HD), BF16),
    "wb": pltpu.VMEM((GQ * HD, COLS), BF16),
    "qf": pltpu.VMEM((ROWS * QROWS, HD), F32),
    "kn": pltpu.VMEM((HD, HD), F32),
    "vn": pltpu.VMEM((HD, HD), F32),
    "of": pltpu.VMEM((ROWS * QROWS, HD), F32),
    "mf": pltpu.VMEM((ROWS * QROWS, HD), F32),
    "lf": pltpu.VMEM((ROWS * QROWS, HD), F32),
    "sb": pltpu.VMEM((RING, QROWS, HD), BF16),
    "sx": pltpu.VMEM((QROWS, HD), BF16),
    "xb": pltpu.VMEM((RING, QROWS, HD), BF16),
    "hos": pltpu.VMEM((QROWS, HD), BF16),
    "hls": pltpu.VMEM((8, HD), F32),
    "ho": pltpu.VMEM((RING, QROWS, HD), BF16),
    "hl": pltpu.VMEM((RING, 8, HD), F32),
    "sl": pltpu.VMEM((RING, 8, HD), F32),
    "ho2": pltpu.VMEM((RING, QROWS, HD), BF16),
    "hl2": pltpu.VMEM((RING, 16, HD), F32),
    "wt": pltpu.VMEM((2 * QROWS, HD), F32),
    "ot": pltpu.VMEM((2 * QROWS, HD), F32),
    "ab": pltpu.VMEM((RING, RING, GQ, ROWS * STEPS, HD), BF16),
    "am": pltpu.VMEM((RING * ROWS * STEPS, GQ * HD), BF16),
    "pr": pltpu.VMEM((RING * ROWS * STEPS, COLS), F32),
    "pm": pltpu.VMEM((RING, 128, COLS), F32),
    "so": pltpu.VMEM((RING, 128, COLS), BF16),
    "si": pltpu.VMEM((RING, 128, COLS), BF16),
    "xo": pltpu.VMEM((RING, 128, COLS), BF16),
    "xi": pltpu.VMEM((RING, 128, COLS), BF16),
    "own": pltpu.VMEM((128, COLS), F32),
    "clen": pltpu.SMEM((1, ROWS), jnp.int32),
    "loc": pltpu.SemaphoreType.DMA((18,)),
    "kvs": pltpu.SemaphoreType.DMA((6,)),
    "kr": pltpu.SemaphoreType.DMA((RING,)),
    "vr": pltpu.SemaphoreType.DMA((RING,)),
    "qs": pltpu.SemaphoreType.DMA((6,)),
    "qr": pltpu.SemaphoreType.DMA((RING,)),
    "bs": pltpu.SemaphoreType.DMA((RING,)),
    "br": pltpu.SemaphoreType.DMA((RING,)),
    "xs": pltpu.SemaphoreType.DMA((RING,)),
    "xr": pltpu.SemaphoreType.DMA((RING,)),
    "hs": pltpu.SemaphoreType.DMA((RING,)),
    "hr": pltpu.SemaphoreType.DMA((RING,)),
    "hls_s": pltpu.SemaphoreType.DMA((RING,)),
    "hlr": pltpu.SemaphoreType.DMA((RING,)),
    "sls": pltpu.SemaphoreType.DMA((RING,)),
    "slr": pltpu.SemaphoreType.DMA((RING,)),
    "h2s": pltpu.SemaphoreType.DMA((RING,)),
    "h2r": pltpu.SemaphoreType.DMA((RING,)),
    "hl2s": pltpu.SemaphoreType.DMA((RING,)),
    "hl2r": pltpu.SemaphoreType.DMA((RING,)),
    "as_": pltpu.SemaphoreType.DMA((RING,)),
    "ar": pltpu.SemaphoreType.DMA((RING,)),
    "ays": pltpu.SemaphoreType.DMA((6,)),
    "ayr": pltpu.SemaphoreType.DMA((RING, 2)),
    "ops": pltpu.SemaphoreType.DMA((RING,)),
    "opr": pltpu.SemaphoreType.DMA((RING,)),
    "lps": pltpu.SemaphoreType.DMA((RING,)),
    "lpr": pltpu.SemaphoreType.DMA((RING,)),
    "sis": pltpu.SemaphoreType.DMA((RING,)),
    "sir": pltpu.SemaphoreType.DMA((RING,)),
    "xis": pltpu.SemaphoreType.DMA((RING,)),
    "xir": pltpu.SemaphoreType.DMA((RING,)),
}


class Names:
    pass


def kernel(plen, prow, clen_in, q_in, skv, pkv, dq, nkv, cache, w_in, out_p, out_d, *scratch):
    s = Names()
    for name, ref in zip(SCRATCH, scratch):
        setattr(s, name, ref)

    me = lax.axis_index("ctx")
    y, z = lax.div(me, RING), lax.rem(me, RING)
    head = lax.axis_index("head")
    x, core = lax.div(head, 2), lax.rem(head, 2)
    other = 1 - lax.axis_index("grp")

    def turned(j):
        return lax.rem(y + lax.div(j * (j + 1), 2), RING)

    def near(p):
        high = lax.rem(lax.div(z, 2) + lax.div(p, 2), 2)
        return 2 * high + lax.rem(z + p, 2)

    up, down, far = lax.rem(y + 1, RING), lax.rem(y + 3, RING), lax.rem(y + 2, RING)

    def at_y(yy):
        return {"ctx": yy * RING + z}

    def at_z(zz):
        return {"ctx": y * RING + zz}

    def across(zz):
        return {"ctx": y * RING + zz, "grp": other}

    def at_x(xx):
        return {"head": xx * 2 + core}

    sibling = {"head": x * 2 + 1 - core}

    def send(src, dst, ssem, rsem, device):
        return pltpu.make_async_remote_copy(
            src_ref=src, dst_ref=dst, send_sem=ssem, recv_sem=rsem, device_id=device, device_id_type=MESH
        )

    def arrived(dst, rsem):
        send(dst, dst, s.loc.at[0], rsem, sibling).wait_recv()

    pairs = [
        (pkv.at[0], s.kl.at[pl.ds(0, PRE)]),
        (skv.at[0], s.kl.at[pl.ds(PRE, SPAN)]),
        (pkv.at[1], s.vb.at[y, pl.ds(0, PRE)]),
        (skv.at[1], s.vb.at[y, pl.ds(PRE, SPAN)]),
    ]
    pairs += [(q_in.at[:, pl.ds(h * HD, HD)], s.qb.at[z, pl.ds(h * SPAN, SPAN)]) for h in range(GQ)]
    pairs += [(dq, s.dq), (nkv, s.nkv), (clen_in, s.clen), (cache.at[0], s.ck), (cache.at[1], s.cv), (w_in, s.wb)]
    loads = [pltpu.make_async_copy(src, dst, s.loc.at[at]) for at, (src, dst) in enumerate(pairs)]
    for load in loads:
        load.start()

    barrier = pltpu.get_barrier_semaphore()
    greeted = [at_y(lax.rem(y + d, RING)) for d in (1, 2, 3)] + [at_z(lax.rem(z + d, RING)) for d in (1, 2, 3)]
    greeted += [across(zz) for zz in range(RING)] + [sibling] + [at_x(lax.rem(x + d, RING)) for d in (1, 2, 3)]
    for device in greeted:
        pl.semaphore_signal(barrier, inc=1, device_id=device, device_id_type=MESH)

    def clear(p, carry):
        s.acc[p] = jnp.zeros((GQ * SPAN, HD), F32)
        s.tot[p] = jnp.zeros((GQ * SPAN, HD), F32)
        s.top[p] = jnp.full((GQ * SPAN, HD), MASKED, F32)
        slot = iota((HD, KEYS), 1)
        unused = ((p * RING + z) * PRE + slot >= plen[0]) & (slot < PRE) & (iota((HD, KEYS), 0) == 0)
        s.kb[p, HD : 2 * HD, :] = jnp.where(unused, MASKED, 0.0).astype(BF16)
        return carry

    lax.fori_loop(0, RING, clear, 0)


    for load in loads[2:12]:
        load.wait()
    pl.semaphore_wait(barrier, len(greeted))

    def keys_of(yy):
        return s.kb.at[yy, pl.ds(0, HD)]

    kv_own = [
        send(s.vb.at[y], s.vb.at[y], s.kvs.at[0], s.vr.at[y], at_y(up)),
        send(s.vb.at[y], s.vb.at[y], s.kvs.at[1], s.vr.at[y], at_y(down)),
        send(keys_of(y), keys_of(y), s.kvs.at[2], s.kr.at[y], at_y(up)),
        send(keys_of(y), keys_of(y), s.kvs.at[3], s.kr.at[y], at_y(down)),
    ]
    kv_on = [
        send(keys_of(down), keys_of(down), s.kvs.at[4], s.kr.at[down], at_y(up)),
        send(s.vb.at[up], s.vb.at[up], s.kvs.at[5], s.vr.at[up], at_y(down)),
    ]

    def q_copy(source, step, sem):
        return send(s.qb.at[source], s.qb.at[source], s.qs.at[sem], s.qr.at[source], at_z(z + step))

    q_first = [(z < 3, z, 1, 0), (z > 0, z, -1, 1)]
    q_second = [((z > 0) & (z < 3), z - 1, 1, 2), ((z > 0) & (z < 3), z + 1, -1, 3)]
    q_third = [(z == 2, z - 2, 1, 4), (z == 1, z + 2, -1, 5)]

    def q_start(group):
        for when, source, step, sem in group:

            @pl.when(when)
            def _(source=source, step=step, sem=sem):
                q_copy(source, step, sem).start()

    def q_wait(distance):
        @pl.when(z >= distance)
        def _():
            arrived(s.qb.at[z - distance], s.qr.at[z - distance])

        @pl.when(z + distance < RING)
        def _():
            arrived(s.qb.at[z + distance], s.qr.at[z + distance])

    def b_copy(d):
        return send(s.sb.at[y], s.sb.at[y], s.bs.at[d], s.br.at[y], at_y(lax.rem(y + d, RING)))

    for copy in kv_own[:2]:
        copy.start()
    q_start(q_first)
    for load in loads[:2]:
        load.wait()
    s.kb[y, 0:HD, :] = s.kl[...].T
    for copy in kv_own[2:]:
        copy.start()

    for load in loads[12:15]:
        load.wait()
    for r in range(ROWS):
        row = s.dq[r].astype(F32)
        for h in range(GQ):
            s.qf[pl.ds(r * QROWS + h, STEPS, stride=GQ), :] = row[:, h * HD : (h + 1) * HD]
    s.kn[...] = jnp.zeros((HD, HD), F32)
    s.vn[...] = jnp.zeros((HD, HD), F32)
    for r in range(ROWS):
        s.kn[pl.ds(r * STEPS, STEPS), :] = s.nkv[0, r].astype(F32)
        s.vn[pl.ds(r * STEPS, STEPS), :] = s.nkv[1, r].astype(F32)

    def picked(ref):
        def add(r, total):
            mine = jnp.where(me * ROWS + r == prow[0], 1.0, 0.0)
            return total + mine * ref[pl.ds(pl.multiple_of(r * QROWS, QROWS), QROWS), :]

        return lax.fori_loop(0, ROWS, add, jnp.zeros((QROWS, HD), F32))

    s.sb[y] = picked(s.qf).astype(BF16)

    for d in (1, 2, 3):
        b_copy(d).start()

    lanes = (ROWS * QROWS, HD)
    at_row, at_key = iota(lanes, 0), iota(lanes, 1)
    same = lax.shift_right_logical(at_row, 5) == lax.shift_right_logical(at_key, 2)
    early = jnp.bitwise_and(at_key, 3) <= jnp.bitwise_and(lax.shift_right_logical(at_row, 3), 3)
    new = jnp.where(same & early, dot_nt(s.qf[...].astype(BF16), s.kn[...].astype(BF16)) * SCALE, MASKED)
    new_top = jnp.max(new, axis=1, keepdims=True)
    new_weights = jnp.exp2(new - new_top)
    s.mf[...] = jnp.broadcast_to(new_top, lanes)
    s.lf[...] = jnp.broadcast_to(jnp.sum(new_weights, axis=1, keepdims=True), lanes)
    s.of[...] = dot_nn(new_weights.astype(BF16), s.vn[...].astype(BF16))

    for load in loads[15:]:
        load.wait()

    def cached(r):
        rows = pl.ds(pl.multiple_of(r * QROWS, QROWS), QROWS)
        scores = dot_nt(s.qf[rows, :].astype(BF16), s.ck[r]) * SCALE
        scores = jnp.where(iota((QROWS, SLOTS), 1) < s.clen[0, r], scores, MASKED)
        before = s.mf[rows, :]
        after = jnp.maximum(before, jnp.max(scores, axis=1, keepdims=True))
        weights = jnp.exp2(scores - after[:, :1])
        keep = jnp.exp2(before - after)
        total = s.lf[rows, :] * keep + jnp.sum(weights, axis=1, keepdims=True)
        mixed = s.of[rows, :] * keep + dot_nn(weights.astype(BF16), s.cv[r])
        s.of[rows, :] = mixed / total
        s.lf[rows, :] = after + log2(total)

    def first_queries():
        q_wait(1)
        q_start(q_second)

    def some_rows(i, carry):
        @pl.when(i == 2)
        def _():
            first_queries()

        for u in range(4):
            cached(i * 4 + u)
        return carry

    lax.fori_loop(0, ROWS // 4, some_rows, 0)
    for h in range(GQ):
        s.ab[y, z, h] = s.of[pl.ds(h, ROWS * STEPS, stride=GQ), :].astype(BF16)

    def a_copy(d):
        return send(s.ab.at[y, z], s.ab.at[y, z], s.as_.at[d], s.ar.at[z], at_z(lax.rem(z + d, RING)))

    for d in (1, 2, 3):
        a_copy(d).start()
    s.sl[z] = jnp.broadcast_to(to_row(picked(s.lf)), (8, HD))

    def x_copy(d):
        zz = lax.rem(z + d, RING)
        return send(s.sx, s.xb.at[z], s.xs.at[d], s.xr.at[z], across(zz))

    def pass_query():
        for d in (1, 2, 3):
            yy = lax.rem(y + d, RING)
            arrived(s.sb.at[yy], s.br.at[yy])
        total = s.sb[0].astype(F32)
        for yy in (1, 2, 3):
            total = total + s.sb[yy].astype(F32)
        s.sx[...] = total.astype(BF16)
        for d in range(RING):
            x_copy(d).start()

    def h_copies(d):
        zz = lax.rem(z + d, RING)
        copies = [
            send(s.hos, s.ho.at[z], s.hs.at[d], s.hr.at[z], across(zz)),
            send(s.hls, s.hl.at[z], s.hls_s.at[d], s.hlr.at[z], across(zz)),
        ]
        if d:
            copies.append(send(s.sl.at[z], s.sl.at[z], s.sls.at[d], s.slr.at[z], at_z(zz)))
        return copies

    def answer():
        for zz in range(RING):
            arrived(s.xb.at[zz], s.xr.at[zz])
        query = s.xb[0].astype(F32)
        for zz in (1, 2, 3):
            query = query + s.xb[zz].astype(F32)
        span = pl.ds(PRE, SPAN)
        scores = dot_nn(query.astype(BF16), s.kb[y, 0:HD, span]) * SCALE
        top = jnp.max(scores, axis=1, keepdims=True)
        weights = jnp.exp2(scores - top)
        total = jnp.sum(weights, axis=1, keepdims=True)
        s.hos[...] = (dot_nn(weights.astype(BF16), s.vb[y, span, :]) / total).astype(BF16)
        level = jnp.broadcast_to(top + log2(total), (QROWS, HD))
        s.hls[...] = jnp.broadcast_to(to_row(level), (8, HD))
        for d in range(RING):
            for copy in h_copies(d):
                copy.start()

    def h2_copies(d):
        yy = lax.rem(y + d, RING)
        return [
            send(s.ho2.at[y], s.ho2.at[y], s.h2s.at[d], s.h2r.at[y], at_y(yy)),
            send(s.hl2.at[y], s.hl2.at[y], s.hl2s.at[d], s.hl2r.at[y], at_y(yy)),
        ]

    def combine_z():
        for zz in range(RING):
            arrived(s.ho.at[zz], s.hr.at[zz])
            arrived(s.hl.at[zz], s.hlr.at[zz])
        for d in (1, 2, 3):
            zz = lax.rem(z + d, RING)
            arrived(s.sl.at[zz], s.slr.at[zz])
        out, level = merge([(s.ho[zz].astype(F32), to_column(s.hl[zz, 0:1, :], QROWS)) for zz in range(RING)])
        s.ho2[y] = out.astype(BF16)
        s.hl2[y, 0:8, :] = jnp.broadcast_to(to_row(jnp.broadcast_to(level, (QROWS, HD))), (8, HD))
        s.hl2[y, 8:16, :] = s.sl[0] + s.sl[1] + s.sl[2] + s.sl[3]
        for d in (1, 2, 3):
            for copy in h2_copies(d):
                copy.start()

    def combine_y():
        for d in (1, 2, 3):
            yy = lax.rem(y + d, RING)
            arrived(s.ho2.at[yy], s.h2r.at[yy])
            arrived(s.hl2.at[yy], s.hl2r.at[yy])
        out, level = merge([(s.ho2[yy].astype(F32), to_column(s.hl2[yy, 0:1, :], QROWS)) for yy in range(RING)])
        rows = s.hl2[0, 8:9, :] + s.hl2[1, 8:9, :] + s.hl2[2, 8:9, :] + s.hl2[3, 8:9, :]
        before = to_column(rows, QROWS)
        top = jnp.maximum(before, level)
        w_own, w_span = jnp.exp2(before - top), jnp.exp2(level - top)
        total = w_own + w_span
        keep = jnp.broadcast_to(w_own / total, (QROWS, HD))
        added = out * (w_span / total)
        for at in range(2):
            s.wt[pl.ds(at * QROWS, QROWS), :] = keep
            s.ot[pl.ds(at * QROWS, QROWS), :] = added

    def half(yy, i):
        return s.ab.at[yy, pl.ds(2 * i, 2)]

    def ay_copy(yy, i, sem, to):
        return send(half(yy, i), half(yy, i), s.ays.at[sem], s.ayr.at[yy, i], at_y(to))

    ay_own = [ay_copy(y, 0, 0, up), ay_copy(y, 1, 1, down), ay_copy(y, 1, 2, up), ay_copy(y, 0, 3, down)]
    ay_on = [ay_copy(down, 0, 4, up), ay_copy(up, 1, 5, down)]

    def spread_rows():
        for d in (1, 2, 3):
            zz = lax.rem(z + d, RING)
            arrived(s.ab.at[y, zz], s.ar.at[zz])
        for copy in ay_own:
            copy.start()

    def pass_rows():
        arrived(half(down, 0), s.ayr.at[down, 0])
        ay_on[0].start()
        arrived(half(up, 1), s.ayr.at[up, 1])
        ay_on[1].start()

    def rest_of_rows():
        arrived(half(down, 1), s.ayr.at[down, 1])
        arrived(half(up, 0), s.ayr.at[up, 0])

    def far_rows():
        for i in range(2):
            arrived(half(far, i), s.ayr.at[far, i])

    def si_copy(j):
        return send(s.so.at[j], s.si.at[j], s.sis.at[j], s.sir.at[j], sibling)

    def project(j):
        yc = turned(j)
        count = RING * ROWS * STEPS
        row = yc * (RING * ROWS) + lax.shift_right_logical(iota((count, HD), 0), 2)
        hit = row == prow[0]
        for h in range(GQ):
            block = jnp.concatenate([s.ab[yc, zz, h] for zz in range(RING)], axis=0).astype(F32)
            keep = s.wt[pl.ds(h, 2 * STEPS, stride=GQ), :]
            added = s.ot[pl.ds(h, 2 * STEPS, stride=GQ), :]
            keep = jnp.concatenate([keep] * (count // (2 * STEPS)), axis=0)
            added = jnp.concatenate([added] * (count // (2 * STEPS)), axis=0)
            block = jnp.where(hit, block * keep + added, block)
            s.am[:, h * HD : (h + 1) * HD] = block.astype(BF16)
        s.pr[...] = dot_nn(s.am[...], s.wb[...])
        s.pm[j] = s.pr[pl.ds(pl.multiple_of(core * 128, 128), 128), :]
        s.so[j] = s.pr[pl.ds(pl.multiple_of((1 - core) * 128, 128), 128), :].astype(BF16)
        si_copy(j).start()

    def xi_copy(j):
        return send(s.xo.at[j], s.xi.at[x], s.xis.at[j], s.xir.at[x], at_x(turned(j)))

    def join(j):
        arrived(s.si.at[j], s.sir.at[j])
        total = s.pm[j] + s.si[j].astype(F32)

        @pl.when(turned(j) == x)
        def _():
            s.own[...] = total

        @pl.when(turned(j) != x)
        def _():
            s.xo[j] = total.astype(BF16)
            xi_copy(j).start()

    count = BLOCK // SPAN
    first_lane = jnp.where(iota((BLOCK, HD), 1) == 0, 1.0, 0.0).astype(BF16)
    ones = jnp.ones((KEYS, HD), BF16)

    def scores_of(at, b, held, peak):
        p, yc = lookup(PIECES, at), turned(lookup(CHUNKS, at))
        zq = near(p)
        late = (y * RING + zq) * SPAN - (yc * RING + z) * SPAN
        shape = (SPAN, SPAN)
        ahead = jnp.where(iota(shape, 1) - iota(shape, 0) <= late, 0.0, MASKED)
        ahead = jnp.concatenate([ahead] * count, axis=0)
        queries = jnp.concatenate([s.qb[zq, b * BLOCK : (b + 1) * BLOCK, :], first_lane], axis=1)
        scores = dot_nn(queries, s.kb[yc])
        highest = None
        for k in range(KEYS // HD):
            cols = slice(k * HD, (k + 1) * HD)
            part = scores[:, cols] * SCALE
            if k == PRE // HD:
                part = part + ahead
            held[:, cols] = part
            highest = part if highest is None else jnp.maximum(highest, part)
        peak[...] = jnp.broadcast_to(jnp.max(highest, axis=1, keepdims=True), (BLOCK, HD))

    def weigh(at, b, held, peak):
        p, yc = lookup(PIECES, at), turned(lookup(CHUNKS, at))
        rows = slice(b * BLOCK, (b + 1) * BLOCK)
        before = s.top[p, rows, :]
        after = jnp.maximum(before, peak[...])
        keep = jnp.exp2(before - after)
        packed = []
        for k in range(KEYS // HD):
            packed.append(jnp.exp2(held[:, k * HD : (k + 1) * HD] - after).astype(BF16))
        mixed = dot_nn(jnp.concatenate(packed, axis=1), jnp.concatenate([s.vb[yc], ones], axis=1))
        s.top[p, rows, :] = after
        s.tot[p, rows, :] = s.tot[p, rows, :] * keep + mixed[:, HD:]
        s.acc[p, rows, :] = s.acc[p, rows, :] * keep + mixed[:, :HD]

    def o_copies(p):
        return [
            send(s.os.at[p], s.orb.at[p], s.ops.at[p], s.opr.at[p], at_z(near(p))),
            send(s.ls.at[p], s.lrb.at[p], s.lps.at[p], s.lpr.at[p], at_z(near(p))),
        ]

    def ship(p):
        def one(h, carry):
            rows = pl.ds(pl.multiple_of(h * SPAN, SPAN), SPAN)
            total = s.tot[p, rows, :]
            s.os[p, h] = (s.acc[p, rows, :] / total).astype(BF16)
            s.ls[p, pl.ds(h, 1), :] = to_row(s.top[p, rows, :] + log2(total))
            return carry

        lax.fori_loop(0, GQ, one, 0)
        for copy in o_copies(p):
            copy.start()

    def settle():
        def one(h, carry):
            rows = pl.ds(pl.multiple_of(h * SPAN, SPAN), SPAN)
            levels = [to_column(s.lrb[p, pl.ds(h, 1), :], SPAN) for p in (1, 2, 3)]
            top = s.top[0, rows, :]
            for level in levels:
                top = jnp.maximum(top, level)
            weight = jnp.exp2(s.top[0, rows, :] - top)
            total = s.tot[0, rows, :] * weight
            mixed = s.acc[0, rows, :] * weight
            for p, level in zip((1, 2, 3), levels):
                weight = jnp.exp2(level - top)
                total = total + weight
                mixed = mixed + s.orb[p, h].astype(F32) * weight
            out_p[:, pl.ds(pl.multiple_of(h * HD, HD), HD)] = (mixed / total).astype(BF16)
            return carry

        lax.fori_loop(0, GQ, one, 0)

    def keys_near():
        arrived(keys_of(down), s.kr.at[down])
        kv_on[0].start()
        arrived(s.vb.at[up], s.vr.at[up])
        kv_on[1].start()
        arrived(s.vb.at[down], s.vr.at[down])
        arrived(keys_of(up), s.kr.at[up])

    def keys_far():
        arrived(keys_of(far), s.kr.at[far])
        arrived(s.vb.at[far], s.vr.at[far])

    def second_queries():
        q_wait(2)
        q_start(q_third)

    actions = {
        0: [pass_query],
        2: [keys_near],
        3: [answer],
        4: [second_queries],
        6: [combine_z],
        7: [keys_far, spread_rows],
        8: [lambda: q_wait(3)],
        9: [combine_y],
        11: [pass_rows],
        14: [rest_of_rows],
        16: [far_rows],
    }

    def prepare(i):
        for at, todo in actions.items():

            @pl.when(i == at)
            def _(todo=todo):
                for action in todo:
                    action()

        @pl.when(i >= 14)
        def _():
            join(i - 14)

        @pl.when((i == 12) | (i >= 14))
        def _():
            project(jnp.maximum(i - 13, 0))

    def step(i, carry):
        scores_of(i, 1, s.ts1, s.mx1)
        weigh(i, 0, s.ts0, s.mx0)
        prepare(i + 1)
        scores_of(jnp.minimum(i + 1, 15), 0, s.ts0, s.mx0)
        weigh(i, 1, s.ts1, s.mx1)
        p, k = lookup(PIECES, i), lookup(CHUNKS, i)

        @pl.when((k == 3) & (p > 0))
        def _():
            ship(p)

        return carry

    for action in actions.pop(0):
        action()
    scores_of(0, 0, s.ts0, s.mx0)
    lax.fori_loop(0, 16, step, 0)
    join(RING - 1)

    for p in (1, 2, 3):
        arrived(s.orb.at[p], s.opr.at[p])
        arrived(s.lrb.at[p], s.lpr.at[p])
    settle()

    total = s.own[...]
    for d in (1, 2, 3):
        xx = lax.rem(x + d, RING)
        arrived(s.xi.at[xx], s.xir.at[xx])
        total = total + s.xi[xx].astype(F32)
    for r in range(32):
        out_d[r] = total[r * STEPS : (r + 1) * STEPS, :].astype(BF16)

    for copy in kv_own + kv_on + ay_own + ay_on:
        copy.wait_send()
    for when, source, step_z, sem in q_first + q_second + q_third:

        @pl.when(when)
        def _(source=source, step_z=step_z, sem=sem):
            q_copy(source, step_z, sem).wait_send()

    for d in range(RING):
        x_copy(d).wait_send()
        for copy in h_copies(d):
            copy.wait_send()
        if d:
            b_copy(d).wait_send()
            a_copy(d).wait_send()
            for copy in h2_copies(d):
                copy.wait_send()
            for copy in o_copies(d):
                copy.wait_send()
    for j in range(RING):
        si_copy(j).wait_send()

        @pl.when(turned(j) != x)
        def _(j=j):
            xi_copy(j).wait_send()


def shards(span_q, span_kv, prefix_kv, prefix_len, dec_q, dec_new_kv, dec_cache, cache_len, prompt_row, out_weight):
    vmem = pl.BlockSpec(memory_space=pltpu.VMEM)
    smem = pl.BlockSpec(memory_space=pltpu.SMEM)
    hbm = pl.BlockSpec(memory_space=pltpu.HBM)
    prefill, decode = pl.pallas_call(
        kernel,
        out_shape=(
            jax.ShapeDtypeStruct((SPAN, GQ * HD), BF16),
            jax.ShapeDtypeStruct((32, STEPS, COLS), BF16),
        ),
        in_specs=[smem] * 2 + [hbm] * 8,
        out_specs=(vmem, vmem),
        scratch_shapes=list(SCRATCH.values()),
        compiler_params=pltpu.CompilerParams(
            collective_id=0, has_side_effects=True, vmem_limit_bytes=VMEM_BYTES
        ),
        cost_estimate=pl.CostEstimate(flops=11_000_000_000, bytes_accessed=8_000_000, transcendentals=17_000_000),
    )(
        prefix_len,
        prompt_row,
        *[
            pltpu.with_memory_space_constraint(operand, pltpu.HBM)
            for operand in (
                cache_len,
                span_q[0],
                span_kv[0],
                prefix_kv[0],
                dec_q[0],
                dec_new_kv[0],
                dec_cache[0],
                out_weight,
            )
        ],
    )
    return prefill[None], decode[None]


def solution(mesh):
    placed = (
        P("grp", "ctx", "head"),
        P("grp", None, "ctx", "head"),
        P("grp", None, "ctx", "head"),
        P("grp"),
        P("grp", "ctx", None, "head"),
        P("grp", None, "ctx", None, "head"),
        P("grp", None, "ctx", None, "head"),
        P("grp", "ctx"),
        P("grp"),
        P("head", "ctx"),
    )
    return jax.shard_map(
        shards,
        mesh=mesh,
        in_specs=placed,
        out_specs=(P("grp", "ctx", "head"), P("grp", "head", None, "ctx")),
        check_vma=False,
    )
```

```python
import math

import jax
import jax.numpy as jnp
from jax import lax
from jax.experimental import pallas as pl
from jax.experimental.pallas import tpu as pltpu
from jax.sharding import PartitionSpec as P

HD = 128
GQ = 8
RING = 4
PRE = 896
SPAN = 128
KEYS = PRE + SPAN
ROWS = 16
STEPS = 4
SLOTS = 512
QROWS = STEPS * GQ
COLS = 512
MASKED = -1e30
LOG2E = math.log2(math.e)
SCALE = LOG2E / math.sqrt(HD)
MESH = pl.DeviceIdType.MESH
F32 = jnp.float32
BF16 = jnp.bfloat16
BLOCK = 512
VMEM_BYTES = 40 * 1024 * 1024

PIECES = (0, 1, 1, 1, 2, 2, 2, 2, 3, 3, 3, 3, 1, 0, 0, 0)
CHUNKS = (0, 0, 1, 2, 0, 1, 2, 3, 0, 1, 2, 3, 3, 1, 2, 3)


def dot_nt(a, b):
    return lax.dot_general(a, b, (((1,), (1,)), ((), ())), preferred_element_type=F32)


def dot_nn(a, b):
    return lax.dot_general(a, b, (((1,), (0,)), ((), ())), preferred_element_type=F32)


def log2(v):
    return jnp.log(v) * LOG2E


def iota(shape, axis):
    return lax.broadcasted_iota(jnp.int32, shape, axis)


def lookup(table, index):
    value = jnp.int32(table[0])
    for at, entry in enumerate(table[1:], 1):
        value = jnp.where(index == at, jnp.int32(entry), value)
    return value


def to_row(column):
    shape = column.shape
    return jnp.sum(jnp.where(iota(shape, 0) == iota(shape, 1), column, 0.0), axis=0, keepdims=True)


def to_column(row, count):
    shape = (count, HD)
    spread = jnp.broadcast_to(row, shape)
    return jnp.sum(jnp.where(iota(shape, 0) == iota(shape, 1), spread, 0.0), axis=1, keepdims=True)


def merge(parts):
    top = parts[0][1]
    for _, level in parts[1:]:
        top = jnp.maximum(top, level)
    weights = [jnp.exp2(level - top) for _, level in parts]
    total = weights[0]
    for w in weights[1:]:
        total = total + w
    mixed = parts[0][0] * weights[0]
    for (out, _), w in zip(parts[1:], weights[1:]):
        mixed = mixed + out * w
    return mixed / total, top + log2(total)


SCRATCH = {
    "kl": pltpu.VMEM((KEYS, HD), BF16),
    "kb": pltpu.VMEM((RING, 2 * HD, KEYS), BF16),
    "vb": pltpu.VMEM((RING, KEYS, HD), BF16),
    "qb": pltpu.VMEM((RING, GQ * SPAN, HD), BF16),
    "ts0": pltpu.VMEM((BLOCK, KEYS), F32),
    "ts1": pltpu.VMEM((BLOCK, KEYS), F32),
    "kp0": pltpu.VMEM((BLOCK, HD), F32),
    "kp1": pltpu.VMEM((BLOCK, HD), F32),
    "pk0": pltpu.VMEM((BLOCK, KEYS), BF16),
    "pk1": pltpu.VMEM((BLOCK, KEYS), BF16),
    "dq": pltpu.VMEM((ROWS, STEPS, GQ * HD), BF16),
    "nkv": pltpu.VMEM((2, ROWS, STEPS, HD), BF16),
    "acc": pltpu.VMEM((RING, GQ * SPAN, HD), F32),
    "top": pltpu.VMEM((RING, GQ * SPAN, HD), F32),
    "tot": pltpu.VMEM((RING, GQ * SPAN, HD), F32),
    "os": pltpu.VMEM((RING, GQ, SPAN, HD), BF16),
    "ls": pltpu.VMEM((RING, GQ, SPAN), F32),
    "orb": pltpu.VMEM((RING, GQ, SPAN, HD), BF16),
    "lrb": pltpu.VMEM((RING, GQ, SPAN), F32),
    "ck": pltpu.VMEM((ROWS, SLOTS, HD), BF16),
    "cv": pltpu.VMEM((ROWS, SLOTS, HD), BF16),
    "wb": pltpu.VMEM((GQ * HD, COLS), BF16),
    "qf": pltpu.VMEM((ROWS * QROWS, HD), F32),
    "kn": pltpu.VMEM((HD, HD), F32),
    "vn": pltpu.VMEM((HD, HD), F32),
    "of": pltpu.VMEM((ROWS * QROWS, HD), F32),
    "mf": pltpu.VMEM((ROWS * QROWS, HD), F32),
    "lf": pltpu.VMEM((ROWS * QROWS, HD), F32),
    "sb": pltpu.VMEM((RING, QROWS, HD), BF16),
    "sx": pltpu.VMEM((QROWS, HD), BF16),
    "xb": pltpu.VMEM((RING, QROWS, HD), BF16),
    "hos": pltpu.VMEM((QROWS, HD), BF16),
    "hls": pltpu.VMEM((8, HD), F32),
    "ho": pltpu.VMEM((RING, QROWS, HD), BF16),
    "hl": pltpu.VMEM((RING, 8, HD), F32),
    "sl": pltpu.VMEM((RING, 8, HD), F32),
    "ho2": pltpu.VMEM((RING, QROWS, HD), BF16),
    "hl2": pltpu.VMEM((RING, 16, HD), F32),
    "wt": pltpu.VMEM((2 * QROWS, HD), F32),
    "ot": pltpu.VMEM((2 * QROWS, HD), F32),
    "ab": pltpu.VMEM((RING, RING, GQ, ROWS * STEPS, HD), BF16),
    "am": pltpu.VMEM((RING * ROWS * STEPS, GQ * HD), BF16),
    "pr": pltpu.VMEM((RING * ROWS * STEPS, COLS), F32),
    "pm": pltpu.VMEM((RING, 128, COLS), F32),
    "so": pltpu.VMEM((RING, 128, COLS), BF16),
    "si": pltpu.VMEM((RING, 128, COLS), BF16),
    "xo": pltpu.VMEM((RING, 128, COLS), BF16),
    "xi": pltpu.VMEM((RING, 128, COLS), BF16),
    "own": pltpu.VMEM((128, COLS), F32),
    "clen": pltpu.SMEM((1, ROWS), jnp.int32),
    "loc": pltpu.SemaphoreType.DMA((18,)),
    "kvs": pltpu.SemaphoreType.DMA((6,)),
    "kr": pltpu.SemaphoreType.DMA((RING,)),
    "vr": pltpu.SemaphoreType.DMA((RING,)),
    "qs": pltpu.SemaphoreType.DMA((6,)),
    "qr": pltpu.SemaphoreType.DMA((RING,)),
    "bs": pltpu.SemaphoreType.DMA((RING,)),
    "br": pltpu.SemaphoreType.DMA((RING,)),
    "xs": pltpu.SemaphoreType.DMA((RING,)),
    "xr": pltpu.SemaphoreType.DMA((RING,)),
    "hs": pltpu.SemaphoreType.DMA((RING,)),
    "hr": pltpu.SemaphoreType.DMA((RING,)),
    "hls_s": pltpu.SemaphoreType.DMA((RING,)),
    "hlr": pltpu.SemaphoreType.DMA((RING,)),
    "sls": pltpu.SemaphoreType.DMA((RING,)),
    "slr": pltpu.SemaphoreType.DMA((RING,)),
    "h2s": pltpu.SemaphoreType.DMA((RING,)),
    "h2r": pltpu.SemaphoreType.DMA((RING,)),
    "hl2s": pltpu.SemaphoreType.DMA((RING,)),
    "hl2r": pltpu.SemaphoreType.DMA((RING,)),
    "as_": pltpu.SemaphoreType.DMA((RING,)),
    "ar": pltpu.SemaphoreType.DMA((RING,)),
    "ays": pltpu.SemaphoreType.DMA((6,)),
    "ayr": pltpu.SemaphoreType.DMA((RING, 2)),
    "ops": pltpu.SemaphoreType.DMA((RING,)),
    "opr": pltpu.SemaphoreType.DMA((RING,)),
    "lps": pltpu.SemaphoreType.DMA((RING,)),
    "lpr": pltpu.SemaphoreType.DMA((RING,)),
    "sis": pltpu.SemaphoreType.DMA((RING,)),
    "sir": pltpu.SemaphoreType.DMA((RING,)),
    "xis": pltpu.SemaphoreType.DMA((RING,)),
    "xir": pltpu.SemaphoreType.DMA((RING,)),
}


class Names:
    pass


def kernel(plen, prow, clen_in, q_in, skv, pkv, dq, nkv, cache, w_in, out_p, out_d, *scratch):
    s = Names()
    for name, ref in zip(SCRATCH, scratch):
        setattr(s, name, ref)

    me = lax.axis_index("ctx")
    y, z = lax.div(me, RING), lax.rem(me, RING)
    head = lax.axis_index("head")
    x, core = lax.div(head, 2), lax.rem(head, 2)
    other = 1 - lax.axis_index("grp")

    def turned(j):
        return lax.rem(y + lax.div(j * (j + 1), 2), RING)

    def near(p):
        high = lax.rem(lax.div(z, 2) + lax.div(p, 2), 2)
        return 2 * high + lax.rem(z + p, 2)

    up, down, far = lax.rem(y + 1, RING), lax.rem(y + 3, RING), lax.rem(y + 2, RING)

    def at_y(yy):
        return {"ctx": yy * RING + z}

    def at_z(zz):
        return {"ctx": y * RING + zz}

    def across(zz):
        return {"ctx": y * RING + zz, "grp": other}

    def at_x(xx):
        return {"head": xx * 2 + core}

    sibling = {"head": x * 2 + 1 - core}

    def send(src, dst, ssem, rsem, device):
        return pltpu.make_async_remote_copy(
            src_ref=src, dst_ref=dst, send_sem=ssem, recv_sem=rsem, device_id=device, device_id_type=MESH
        )

    def arrived(dst, rsem):
        send(dst, dst, s.loc.at[0], rsem, sibling).wait_recv()

    pairs = [
        (pkv.at[0], s.kl.at[pl.ds(0, PRE)]),
        (skv.at[0], s.kl.at[pl.ds(PRE, SPAN)]),
        (pkv.at[1], s.vb.at[y, pl.ds(0, PRE)]),
        (skv.at[1], s.vb.at[y, pl.ds(PRE, SPAN)]),
    ]
    pairs += [(q_in.at[:, pl.ds(h * HD, HD)], s.qb.at[z, pl.ds(h * SPAN, SPAN)]) for h in range(GQ)]
    pairs += [(dq, s.dq), (nkv, s.nkv), (clen_in, s.clen), (cache.at[0], s.ck), (cache.at[1], s.cv), (w_in, s.wb)]
    loads = [pltpu.make_async_copy(src, dst, s.loc.at[at]) for at, (src, dst) in enumerate(pairs)]
    for load in loads:
        load.start()

    barrier = pltpu.get_barrier_semaphore()
    greeted = [at_y(lax.rem(y + d, RING)) for d in (1, 2, 3)] + [at_z(lax.rem(z + d, RING)) for d in (1, 2, 3)]
    greeted += [across(zz) for zz in range(RING)] + [sibling] + [at_x(lax.rem(x + d, RING)) for d in (1, 2, 3)]
    for device in greeted:
        pl.semaphore_signal(barrier, inc=1, device_id=device, device_id_type=MESH)

    def clear(p, carry):
        s.acc[p] = jnp.zeros((GQ * SPAN, HD), F32)
        s.tot[p] = jnp.zeros((GQ * SPAN, HD), F32)
        s.top[p] = jnp.full((GQ * SPAN, HD), MASKED, F32)
        slot = iota((HD, KEYS), 1)
        unused = ((p * RING + z) * PRE + slot >= plen[0]) & (slot < PRE) & (iota((HD, KEYS), 0) == 0)
        s.kb[p, HD : 2 * HD, :] = jnp.where(unused, MASKED, 0.0).astype(BF16)
        return carry

    lax.fori_loop(0, RING, clear, 0)


    for load in loads[2:12]:
        load.wait()
    pl.semaphore_wait(barrier, len(greeted))

    def keys_of(yy):
        return s.kb.at[yy, pl.ds(0, HD)]

    kv_own = [
        send(s.vb.at[y], s.vb.at[y], s.kvs.at[0], s.vr.at[y], at_y(up)),
        send(s.vb.at[y], s.vb.at[y], s.kvs.at[1], s.vr.at[y], at_y(down)),
        send(keys_of(y), keys_of(y), s.kvs.at[2], s.kr.at[y], at_y(up)),
        send(keys_of(y), keys_of(y), s.kvs.at[3], s.kr.at[y], at_y(down)),
    ]
    kv_on = [
        send(keys_of(down), keys_of(down), s.kvs.at[4], s.kr.at[down], at_y(up)),
        send(s.vb.at[up], s.vb.at[up], s.kvs.at[5], s.vr.at[up], at_y(down)),
    ]

    def q_copy(source, step, sem):
        return send(s.qb.at[source], s.qb.at[source], s.qs.at[sem], s.qr.at[source], at_z(z + step))

    q_first = [(z < 3, z, 1, 0), (z > 0, z, -1, 1)]
    q_second = [((z > 0) & (z < 3), z - 1, 1, 2), ((z > 0) & (z < 3), z + 1, -1, 3)]
    q_third = [(z == 2, z - 2, 1, 4), (z == 1, z + 2, -1, 5)]

    def q_start(group):
        for when, source, step, sem in group:

            @pl.when(when)
            def _(source=source, step=step, sem=sem):
                q_copy(source, step, sem).start()

    def q_wait(distance):
        @pl.when(z >= distance)
        def _():
            arrived(s.qb.at[z - distance], s.qr.at[z - distance])

        @pl.when(z + distance < RING)
        def _():
            arrived(s.qb.at[z + distance], s.qr.at[z + distance])

    def b_copy(d):
        return send(s.sb.at[y], s.sb.at[y], s.bs.at[d], s.br.at[y], at_y(lax.rem(y + d, RING)))

    for copy in kv_own[:2]:
        copy.start()
    q_start(q_first)
    for load in loads[:2]:
        load.wait()
    s.kb[y, 0:HD, :] = s.kl[...].T
    for copy in kv_own[2:]:
        copy.start()

    for load in loads[12:15]:
        load.wait()
    for r in range(ROWS):
        row = s.dq[r].astype(F32)
        for h in range(GQ):
            s.qf[pl.ds(r * QROWS + h, STEPS, stride=GQ), :] = row[:, h * HD : (h + 1) * HD]
    s.kn[...] = jnp.zeros((HD, HD), F32)
    s.vn[...] = jnp.zeros((HD, HD), F32)
    for r in range(ROWS):
        s.kn[pl.ds(r * STEPS, STEPS), :] = s.nkv[0, r].astype(F32)
        s.vn[pl.ds(r * STEPS, STEPS), :] = s.nkv[1, r].astype(F32)

    def picked(ref):
        def add(r, total):
            mine = jnp.where(me * ROWS + r == prow[0], 1.0, 0.0)
            return total + mine * ref[pl.ds(pl.multiple_of(r * QROWS, QROWS), QROWS), :]

        return lax.fori_loop(0, ROWS, add, jnp.zeros((QROWS, HD), F32))

    s.sb[y] = picked(s.qf).astype(BF16)

    for d in (1, 2, 3):
        b_copy(d).start()

    lanes = (ROWS * QROWS, HD)
    at_row, at_key = iota(lanes, 0), iota(lanes, 1)
    same = lax.shift_right_logical(at_row, 5) == lax.shift_right_logical(at_key, 2)
    early = jnp.bitwise_and(at_key, 3) <= jnp.bitwise_and(lax.shift_right_logical(at_row, 3), 3)
    new = jnp.where(same & early, dot_nt(s.qf[...].astype(BF16), s.kn[...].astype(BF16)) * SCALE, MASKED)
    new_top = jnp.max(new, axis=1, keepdims=True)
    new_weights = jnp.exp2(new - new_top)
    s.mf[...] = jnp.broadcast_to(new_top, lanes)
    s.lf[...] = jnp.broadcast_to(jnp.sum(new_weights, axis=1, keepdims=True), lanes)
    s.of[...] = dot_nn(new_weights.astype(BF16), s.vn[...].astype(BF16))

    for load in loads[15:]:
        load.wait()

    def cached(r):
        rows = pl.ds(pl.multiple_of(r * QROWS, QROWS), QROWS)
        scores = dot_nt(s.qf[rows, :].astype(BF16), s.ck[r]) * SCALE
        scores = jnp.where(iota((QROWS, SLOTS), 1) < s.clen[0, r], scores, MASKED)
        before = s.mf[rows, :]
        after = jnp.maximum(before, jnp.max(scores, axis=1, keepdims=True))
        weights = jnp.exp2(scores - after[:, :1])
        keep = jnp.exp2(before - after)
        total = s.lf[rows, :] * keep + jnp.sum(weights, axis=1, keepdims=True)
        mixed = s.of[rows, :] * keep + dot_nn(weights.astype(BF16), s.cv[r])
        s.of[rows, :] = mixed / total
        s.lf[rows, :] = after + log2(total)

    def first_queries():
        q_wait(1)
        q_start(q_second)

    def some_rows(i, carry):
        @pl.when(i == 2)
        def _():
            first_queries()

        for u in range(4):
            cached(i * 4 + u)
        return carry

    lax.fori_loop(0, ROWS // 4, some_rows, 0)
    for h in range(GQ):
        s.ab[y, z, h] = s.of[pl.ds(h, ROWS * STEPS, stride=GQ), :].astype(BF16)

    def a_copy(d):
        return send(s.ab.at[y, z], s.ab.at[y, z], s.as_.at[d], s.ar.at[z], at_z(lax.rem(z + d, RING)))

    for d in (1, 2, 3):
        a_copy(d).start()
    s.sl[z] = jnp.broadcast_to(to_row(picked(s.lf)), (8, HD))

    def x_copy(d):
        zz = lax.rem(z + d, RING)
        return send(s.sx, s.xb.at[z], s.xs.at[d], s.xr.at[z], across(zz))

    def pass_query():
        for d in (1, 2, 3):
            yy = lax.rem(y + d, RING)
            arrived(s.sb.at[yy], s.br.at[yy])
        total = s.sb[0].astype(F32)
        for yy in (1, 2, 3):
            total = total + s.sb[yy].astype(F32)
        s.sx[...] = total.astype(BF16)
        for d in range(RING):
            x_copy(d).start()

    def h_copies(d):
        zz = lax.rem(z + d, RING)
        copies = [
            send(s.hos, s.ho.at[z], s.hs.at[d], s.hr.at[z], across(zz)),
            send(s.hls, s.hl.at[z], s.hls_s.at[d], s.hlr.at[z], across(zz)),
        ]
        if d:
            copies.append(send(s.sl.at[z], s.sl.at[z], s.sls.at[d], s.slr.at[z], at_z(zz)))
        return copies

    def answer():
        for zz in range(RING):
            arrived(s.xb.at[zz], s.xr.at[zz])
        query = s.xb[0].astype(F32)
        for zz in (1, 2, 3):
            query = query + s.xb[zz].astype(F32)
        span = pl.ds(PRE, SPAN)
        scores = dot_nn(query.astype(BF16), s.kb[y, 0:HD, span]) * SCALE
        top = jnp.max(scores, axis=1, keepdims=True)
        weights = jnp.exp2(scores - top)
        total = jnp.sum(weights, axis=1, keepdims=True)
        s.hos[...] = (dot_nn(weights.astype(BF16), s.vb[y, span, :]) / total).astype(BF16)
        level = jnp.broadcast_to(top + log2(total), (QROWS, HD))
        s.hls[...] = jnp.broadcast_to(to_row(level), (8, HD))
        for d in range(RING):
            for copy in h_copies(d):
                copy.start()

    def h2_copies(d):
        yy = lax.rem(y + d, RING)
        return [
            send(s.ho2.at[y], s.ho2.at[y], s.h2s.at[d], s.h2r.at[y], at_y(yy)),
            send(s.hl2.at[y], s.hl2.at[y], s.hl2s.at[d], s.hl2r.at[y], at_y(yy)),
        ]

    def combine_z():
        for zz in range(RING):
            arrived(s.ho.at[zz], s.hr.at[zz])
            arrived(s.hl.at[zz], s.hlr.at[zz])
        for d in (1, 2, 3):
            zz = lax.rem(z + d, RING)
            arrived(s.sl.at[zz], s.slr.at[zz])
        out, level = merge([(s.ho[zz].astype(F32), to_column(s.hl[zz, 0:1, :], QROWS)) for zz in range(RING)])
        s.ho2[y] = out.astype(BF16)
        s.hl2[y, 0:8, :] = jnp.broadcast_to(to_row(jnp.broadcast_to(level, (QROWS, HD))), (8, HD))
        s.hl2[y, 8:16, :] = s.sl[0] + s.sl[1] + s.sl[2] + s.sl[3]
        for d in (1, 2, 3):
            for copy in h2_copies(d):
                copy.start()

    def combine_y():
        for d in (1, 2, 3):
            yy = lax.rem(y + d, RING)
            arrived(s.ho2.at[yy], s.h2r.at[yy])
            arrived(s.hl2.at[yy], s.hl2r.at[yy])
        out, level = merge([(s.ho2[yy].astype(F32), to_column(s.hl2[yy, 0:1, :], QROWS)) for yy in range(RING)])
        rows = s.hl2[0, 8:9, :] + s.hl2[1, 8:9, :] + s.hl2[2, 8:9, :] + s.hl2[3, 8:9, :]
        before = to_column(rows, QROWS)
        top = jnp.maximum(before, level)
        w_own, w_span = jnp.exp2(before - top), jnp.exp2(level - top)
        total = w_own + w_span
        keep = jnp.broadcast_to(w_own / total, (QROWS, HD))
        added = out * (w_span / total)
        for at in range(2):
            s.wt[pl.ds(at * QROWS, QROWS), :] = keep
            s.ot[pl.ds(at * QROWS, QROWS), :] = added

    def half(yy, i):
        return s.ab.at[yy, pl.ds(2 * i, 2)]

    def ay_copy(yy, i, sem, to):
        return send(half(yy, i), half(yy, i), s.ays.at[sem], s.ayr.at[yy, i], at_y(to))

    ay_own = [ay_copy(y, 0, 0, up), ay_copy(y, 1, 1, down), ay_copy(y, 1, 2, up), ay_copy(y, 0, 3, down)]
    ay_on = [ay_copy(down, 0, 4, up), ay_copy(up, 1, 5, down)]

    def spread_rows():
        for d in (1, 2, 3):
            zz = lax.rem(z + d, RING)
            arrived(s.ab.at[y, zz], s.ar.at[zz])
        for copy in ay_own:
            copy.start()

    def pass_rows():
        arrived(half(down, 0), s.ayr.at[down, 0])
        ay_on[0].start()
        arrived(half(up, 1), s.ayr.at[up, 1])
        ay_on[1].start()

    def rest_of_rows():
        arrived(half(down, 1), s.ayr.at[down, 1])
        arrived(half(up, 0), s.ayr.at[up, 0])

    def far_rows():
        for i in range(2):
            arrived(half(far, i), s.ayr.at[far, i])

    def si_copy(j):
        return send(s.so.at[j], s.si.at[j], s.sis.at[j], s.sir.at[j], sibling)

    def project(j):
        yc = turned(j)
        count = RING * ROWS * STEPS
        row = yc * (RING * ROWS) + lax.shift_right_logical(iota((count, HD), 0), 2)
        hit = row == prow[0]
        for h in range(GQ):
            block = jnp.concatenate([s.ab[yc, zz, h] for zz in range(RING)], axis=0).astype(F32)
            keep = s.wt[pl.ds(h, 2 * STEPS, stride=GQ), :]
            added = s.ot[pl.ds(h, 2 * STEPS, stride=GQ), :]
            keep = jnp.concatenate([keep] * (count // (2 * STEPS)), axis=0)
            added = jnp.concatenate([added] * (count // (2 * STEPS)), axis=0)
            block = jnp.where(hit, block * keep + added, block)
            s.am[:, h * HD : (h + 1) * HD] = block.astype(BF16)
        s.pr[...] = dot_nn(s.am[...], s.wb[...])
        s.pm[j] = s.pr[pl.ds(pl.multiple_of(core * 128, 128), 128), :]
        s.so[j] = s.pr[pl.ds(pl.multiple_of((1 - core) * 128, 128), 128), :].astype(BF16)
        si_copy(j).start()

    def xi_copy(j):
        return send(s.xo.at[j], s.xi.at[x], s.xis.at[j], s.xir.at[x], at_x(turned(j)))

    def join(j):
        arrived(s.si.at[j], s.sir.at[j])
        total = s.pm[j] + s.si[j].astype(F32)

        @pl.when(turned(j) == x)
        def _():
            s.own[...] = total

        @pl.when(turned(j) != x)
        def _():
            s.xo[j] = total.astype(BF16)
            xi_copy(j).start()

    count = BLOCK // SPAN
    first_lane = jnp.where(iota((BLOCK, HD), 1) == 0, 1.0, 0.0).astype(BF16)
    ones = jnp.ones((KEYS, HD), BF16)

    def scores_of(at, b, held):
        p, yc = lookup(PIECES, at), turned(lookup(CHUNKS, at))
        zq = near(p)
        queries = jnp.concatenate([s.qb[zq, b * BLOCK : (b + 1) * BLOCK, :], first_lane], axis=1)

        def quarter(j):
            scores = dot_nn(queries, s.kb[yc, :, 2 * j * HD : 2 * (j + 1) * HD])
            for k in (2 * j, 2 * j + 1):
                part = scores[:, (k - 2 * j) * HD : (k - 2 * j + 1) * HD] * SCALE
                if k == PRE // HD:
                    late = (y * RING + zq) * SPAN - (yc * RING + z) * SPAN
                    shape = (SPAN, SPAN)
                    ahead = jnp.where(iota(shape, 1) - iota(shape, 0) <= late, 0.0, MASKED)
                    part = part + jnp.concatenate([ahead] * count, axis=0)
                held[:, k * HD : (k + 1) * HD] = part

        return quarter

    def weigh(at, b, held, keeps, packed):
        p = lookup(PIECES, at)

        def quarter(j):
            for i in range(j * SPAN, (j + 1) * SPAN, 32):
                mine = slice(i, i + 32)
                rows = slice(b * BLOCK + i, b * BLOCK + i + 32)
                tiles = [held[mine, k * HD : (k + 1) * HD] for k in range(KEYS // HD)]
                highest = tiles[0]
                for part in tiles[1:]:
                    highest = jnp.maximum(highest, part)
                before = s.top[p, rows, :]
                after = jnp.maximum(before, jnp.max(highest, axis=1, keepdims=True))
                s.top[p, rows, :] = after
                keeps[mine, :] = jnp.exp2(before - after)
                for k, part in enumerate(tiles):
                    packed[mine, k * HD : (k + 1) * HD] = jnp.exp2(part - after).astype(BF16)

        return quarter

    def mix(at, b, keeps, packed):
        p, yc = lookup(PIECES, at), turned(lookup(CHUNKS, at))

        def half_block(j):
            size = BLOCK // 2
            mine = slice(j * size, (j + 1) * size)
            rows = slice(b * BLOCK + j * size, b * BLOCK + (j + 1) * size)
            mixed = dot_nn(packed[mine, :], jnp.concatenate([s.vb[yc], ones], axis=1))
            keep = keeps[mine, :]
            s.tot[p, rows, :] = s.tot[p, rows, :] * keep + mixed[:, HD:]
            s.acc[p, rows, :] = s.acc[p, rows, :] * keep + mixed[:, :HD]

        return half_block

    def together(scores, weights, products):
        for j in range(4):
            scores(j)
            weights(j)
            if j % 2 == 0:
                products(j // 2)

    def o_copies(p):
        return [
            send(s.os.at[p], s.orb.at[p], s.ops.at[p], s.opr.at[p], at_z(near(p))),
            send(s.ls.at[p], s.lrb.at[p], s.lps.at[p], s.lpr.at[p], at_z(near(p))),
        ]

    def each_head(one):
        def some(i, carry):
            for u in range(4):
                one(i * 4 + u)
            return carry

        lax.fori_loop(0, GQ // 4, some, 0)

    def ship(p):
        def one(h):
            rows = pl.ds(pl.multiple_of(h * SPAN, SPAN), SPAN)
            total = s.tot[p, rows, :]
            s.os[p, h] = (s.acc[p, rows, :] / total).astype(BF16)
            s.ls[p, pl.ds(h, 1), :] = to_row(s.top[p, rows, :] + log2(total))

        each_head(one)
        for copy in o_copies(p):
            copy.start()

    def settle():
        def one(h):
            rows = pl.ds(pl.multiple_of(h * SPAN, SPAN), SPAN)
            levels = [to_column(s.lrb[p, pl.ds(h, 1), :], SPAN) for p in (1, 2, 3)]
            top = s.top[0, rows, :]
            for level in levels:
                top = jnp.maximum(top, level)
            weight = jnp.exp2(s.top[0, rows, :] - top)
            total = s.tot[0, rows, :] * weight
            mixed = s.acc[0, rows, :] * weight
            for p, level in zip((1, 2, 3), levels):
                weight = jnp.exp2(level - top)
                total = total + weight
                mixed = mixed + s.orb[p, h].astype(F32) * weight
            out_p[:, pl.ds(pl.multiple_of(h * HD, HD), HD)] = (mixed / total).astype(BF16)

        each_head(one)

    def keys_near():
        arrived(keys_of(down), s.kr.at[down])
        kv_on[0].start()
        arrived(s.vb.at[up], s.vr.at[up])
        kv_on[1].start()
        arrived(s.vb.at[down], s.vr.at[down])
        arrived(keys_of(up), s.kr.at[up])

    def keys_far():
        arrived(keys_of(far), s.kr.at[far])
        arrived(s.vb.at[far], s.vr.at[far])

    def second_queries():
        q_wait(2)
        q_start(q_third)

    actions = {
        0: [pass_query],
        2: [keys_near],
        3: [answer],
        4: [second_queries],
        6: [combine_z],
        7: [keys_far, spread_rows],
        8: [lambda: q_wait(3)],
        9: [combine_y],
        11: [pass_rows],
        14: [rest_of_rows],
        16: [far_rows],
    }

    def prepare(i):
        for at, todo in actions.items():

            @pl.when(i == at)
            def _(todo=todo):
                for action in todo:
                    action()

        @pl.when(i >= 14)
        def _():
            join(i - 14)

        @pl.when((i == 12) | (i >= 14))
        def _():
            project(jnp.maximum(i - 13, 0))

    even = (s.ts0, s.kp0, s.pk0)
    odd = (s.ts1, s.kp1, s.pk1)

    def step(i, carry):
        last = jnp.maximum(i - 1, 0)
        together(scores_of(i, 1, odd[0]), weigh(i, 0, *even), mix(last, 1, *odd[1:]))
        p, k = lookup(PIECES, last), lookup(CHUNKS, last)

        @pl.when((k == 3) & (p > 0))
        def _():
            ship(p)

        prepare(i + 1)
        together(scores_of(jnp.minimum(i + 1, 15), 0, even[0]), weigh(i, 1, *odd), mix(i, 0, *even[1:]))
        return carry

    s.kp1[...] = jnp.ones((BLOCK, HD), F32)
    s.pk1[...] = jnp.zeros((BLOCK, KEYS), BF16)
    for action in actions.pop(0):
        action()
    first = scores_of(0, 0, s.ts0)
    for j in range(4):
        first(j)
    lax.fori_loop(0, 16, step, 0)
    rest = mix(15, 1, *odd[1:])
    for j in range(2):
        rest(j)
    join(RING - 1)

    for p in (1, 2, 3):
        arrived(s.orb.at[p], s.opr.at[p])
        arrived(s.lrb.at[p], s.lpr.at[p])
    settle()

    total = s.own[...]
    for d in (1, 2, 3):
        xx = lax.rem(x + d, RING)
        arrived(s.xi.at[xx], s.xir.at[xx])
        total = total + s.xi[xx].astype(F32)
    for r in range(32):
        out_d[r] = total[r * STEPS : (r + 1) * STEPS, :].astype(BF16)

    for copy in kv_own + kv_on + ay_own + ay_on:
        copy.wait_send()
    for when, source, step_z, sem in q_first + q_second + q_third:

        @pl.when(when)
        def _(source=source, step_z=step_z, sem=sem):
            q_copy(source, step_z, sem).wait_send()

    for d in range(RING):
        x_copy(d).wait_send()
        for copy in h_copies(d):
            copy.wait_send()
        if d:
            b_copy(d).wait_send()
            a_copy(d).wait_send()
            for copy in h2_copies(d):
                copy.wait_send()
            for copy in o_copies(d):
                copy.wait_send()
    for j in range(RING):
        si_copy(j).wait_send()

        @pl.when(turned(j) != x)
        def _(j=j):
            xi_copy(j).wait_send()


def shards(span_q, span_kv, prefix_kv, prefix_len, dec_q, dec_new_kv, dec_cache, cache_len, prompt_row, out_weight):
    vmem = pl.BlockSpec(memory_space=pltpu.VMEM)
    smem = pl.BlockSpec(memory_space=pltpu.SMEM)
    hbm = pl.BlockSpec(memory_space=pltpu.HBM)
    prefill, decode = pl.pallas_call(
        kernel,
        out_shape=(
            jax.ShapeDtypeStruct((SPAN, GQ * HD), BF16),
            jax.ShapeDtypeStruct((32, STEPS, COLS), BF16),
        ),
        in_specs=[smem] * 2 + [hbm] * 8,
        out_specs=(vmem, vmem),
        scratch_shapes=list(SCRATCH.values()),
        compiler_params=pltpu.CompilerParams(
            collective_id=0, has_side_effects=True, vmem_limit_bytes=VMEM_BYTES
        ),
        cost_estimate=pl.CostEstimate(flops=11_000_000_000, bytes_accessed=8_000_000, transcendentals=17_000_000),
    )(
        prefix_len,
        prompt_row,
        *[
            pltpu.with_memory_space_constraint(operand, pltpu.HBM)
            for operand in (
                cache_len,
                span_q[0],
                span_kv[0],
                prefix_kv[0],
                dec_q[0],
                dec_new_kv[0],
                dec_cache[0],
                out_weight,
            )
        ],
    )
    return prefill[None], decode[None]


def solution(mesh):
    placed = (
        P("grp", "ctx", "head"),
        P("grp", None, "ctx", "head"),
        P("grp", None, "ctx", "head"),
        P("grp"),
        P("grp", "ctx", None, "head"),
        P("grp", None, "ctx", None, "head"),
        P("grp", None, "ctx", None, "head"),
        P("grp", "ctx"),
        P("grp"),
        P("head", "ctx"),
    )
    return jax.shard_map(
        shards,
        mesh=mesh,
        in_specs=placed,
        out_specs=(P("grp", "ctx", "head"), P("grp", "head", None, "ctx")),
        check_vma=False,
    )
```

```python
import math

import jax
import jax.numpy as jnp
from jax import lax
from jax.experimental import pallas as pl
from jax.experimental.pallas import tpu as pltpu
from jax.sharding import PartitionSpec as P

HD = 128
GQ = 8
RING = 4
PRE = 896
SPAN = 128
KEYS = PRE + SPAN
ROWS = 16
STEPS = 4
SLOTS = 512
QROWS = STEPS * GQ
COLS = 512
MASKED = -1e30
LOG2E = math.log2(math.e)
SCALE = LOG2E / math.sqrt(HD)
MESH = pl.DeviceIdType.MESH
F32 = jnp.float32
BF16 = jnp.bfloat16
BLOCK = 512
VMEM_BYTES = 40 * 1024 * 1024

PIECES = (0, 1, 1, 1, 2, 2, 2, 2, 3, 3, 3, 3, 1, 0, 0, 0)
CHUNKS = (0, 0, 1, 2, 0, 1, 2, 3, 0, 1, 2, 3, 3, 1, 2, 3)


def dot_nt(a, b):
    return lax.dot_general(a, b, (((1,), (1,)), ((), ())), preferred_element_type=F32)


def dot_nn(a, b):
    return lax.dot_general(a, b, (((1,), (0,)), ((), ())), preferred_element_type=F32)


def log2(v):
    return jnp.log(v) * LOG2E


def iota(shape, axis):
    return lax.broadcasted_iota(jnp.int32, shape, axis)


def lookup(table, index):
    value = jnp.int32(table[0])
    for at, entry in enumerate(table[1:], 1):
        value = jnp.where(index == at, jnp.int32(entry), value)
    return value


def to_row(column):
    shape = column.shape
    return jnp.sum(jnp.where(iota(shape, 0) == iota(shape, 1), column, 0.0), axis=0, keepdims=True)


def to_column(row, count):
    shape = (count, HD)
    spread = jnp.broadcast_to(row, shape)
    return jnp.sum(jnp.where(iota(shape, 0) == iota(shape, 1), spread, 0.0), axis=1, keepdims=True)


def merge(parts):
    top = parts[0][1]
    for _, level in parts[1:]:
        top = jnp.maximum(top, level)
    weights = [jnp.exp2(level - top) for _, level in parts]
    total = weights[0]
    for w in weights[1:]:
        total = total + w
    mixed = parts[0][0] * weights[0]
    for (out, _), w in zip(parts[1:], weights[1:]):
        mixed = mixed + out * w
    return mixed / total, top + log2(total)


SCRATCH = {
    "kl": pltpu.VMEM((KEYS, HD), BF16),
    "kb": pltpu.VMEM((RING, 2 * HD, KEYS), BF16),
    "vb": pltpu.VMEM((RING, KEYS, HD), BF16),
    "qb": pltpu.VMEM((RING, GQ * SPAN, HD), BF16),
    "ts0": pltpu.VMEM((BLOCK, KEYS), F32),
    "ts1": pltpu.VMEM((BLOCK, KEYS), F32),
    "mx0": pltpu.VMEM((BLOCK, HD), F32),
    "mx1": pltpu.VMEM((BLOCK, HD), F32),
    "dq": pltpu.VMEM((ROWS, STEPS, GQ * HD), BF16),
    "nkv": pltpu.VMEM((2, ROWS, STEPS, HD), BF16),
    "acc": pltpu.VMEM((RING, GQ * SPAN, HD), F32),
    "top": pltpu.VMEM((RING, GQ * SPAN, HD), F32),
    "tot": pltpu.VMEM((RING, GQ * SPAN, HD), F32),
    "os": pltpu.VMEM((RING, GQ, SPAN, HD), BF16),
    "ls": pltpu.VMEM((RING, GQ, SPAN), F32),
    "orb": pltpu.VMEM((RING, GQ, SPAN, HD), BF16),
    "lrb": pltpu.VMEM((RING, GQ, SPAN), F32),
    "ck": pltpu.VMEM((ROWS, SLOTS, HD), BF16),
    "cv": pltpu.VMEM((ROWS, SLOTS, HD), BF16),
    "wb": pltpu.VMEM((GQ * HD, COLS), BF16),
    "qf": pltpu.VMEM((ROWS * QROWS, HD), F32),
    "kn": pltpu.VMEM((HD, HD), F32),
    "vn": pltpu.VMEM((HD, HD), F32),
    "of": pltpu.VMEM((ROWS * QROWS, HD), F32),
    "mf": pltpu.VMEM((ROWS * QROWS, HD), F32),
    "lf": pltpu.VMEM((ROWS * QROWS, HD), F32),
    "sb": pltpu.VMEM((RING, QROWS, HD), BF16),
    "sx": pltpu.VMEM((QROWS, HD), BF16),
    "xb": pltpu.VMEM((RING, QROWS, HD), BF16),
    "hos": pltpu.VMEM((QROWS, HD), BF16),
    "hls": pltpu.VMEM((8, HD), F32),
    "ho": pltpu.VMEM((RING, QROWS, HD), BF16),
    "hl": pltpu.VMEM((RING, 8, HD), F32),
    "sl": pltpu.VMEM((RING, 8, HD), F32),
    "ho2": pltpu.VMEM((RING, QROWS, HD), BF16),
    "hl2": pltpu.VMEM((RING, 16, HD), F32),
    "wt": pltpu.VMEM((2 * QROWS, HD), F32),
    "ot": pltpu.VMEM((2 * QROWS, HD), F32),
    "ab": pltpu.VMEM((RING, RING, GQ, ROWS * STEPS, HD), BF16),
    "am": pltpu.VMEM((RING * ROWS * STEPS, GQ * HD), BF16),
    "pr": pltpu.VMEM((RING * ROWS * STEPS, COLS), F32),
    "pm": pltpu.VMEM((RING, 128, COLS), F32),
    "so": pltpu.VMEM((RING, 128, COLS), BF16),
    "si": pltpu.VMEM((RING, 128, COLS), BF16),
    "xo": pltpu.VMEM((RING, 128, COLS), BF16),
    "xi": pltpu.VMEM((RING, 128, COLS), BF16),
    "own": pltpu.VMEM((128, COLS), F32),
    "clen": pltpu.SMEM((1, ROWS), jnp.int32),
    "loc": pltpu.SemaphoreType.DMA((18,)),
    "kvs": pltpu.SemaphoreType.DMA((6,)),
    "kr": pltpu.SemaphoreType.DMA((RING,)),
    "vr": pltpu.SemaphoreType.DMA((RING,)),
    "qs": pltpu.SemaphoreType.DMA((6,)),
    "qr": pltpu.SemaphoreType.DMA((RING,)),
    "bs": pltpu.SemaphoreType.DMA((RING,)),
    "br": pltpu.SemaphoreType.DMA((RING,)),
    "xs": pltpu.SemaphoreType.DMA((RING,)),
    "xr": pltpu.SemaphoreType.DMA((RING,)),
    "hs": pltpu.SemaphoreType.DMA((RING,)),
    "hr": pltpu.SemaphoreType.DMA((RING,)),
    "hls_s": pltpu.SemaphoreType.DMA((RING,)),
    "hlr": pltpu.SemaphoreType.DMA((RING,)),
    "sls": pltpu.SemaphoreType.DMA((RING,)),
    "slr": pltpu.SemaphoreType.DMA((RING,)),
    "h2s": pltpu.SemaphoreType.DMA((RING,)),
    "h2r": pltpu.SemaphoreType.DMA((RING,)),
    "hl2s": pltpu.SemaphoreType.DMA((RING,)),
    "hl2r": pltpu.SemaphoreType.DMA((RING,)),
    "as_": pltpu.SemaphoreType.DMA((RING,)),
    "ar": pltpu.SemaphoreType.DMA((RING,)),
    "ays": pltpu.SemaphoreType.DMA((3 * RING,)),
    "ayr": pltpu.SemaphoreType.DMA((RING, RING)),
    "ops": pltpu.SemaphoreType.DMA((RING,)),
    "opr": pltpu.SemaphoreType.DMA((RING,)),
    "lps": pltpu.SemaphoreType.DMA((RING,)),
    "lpr": pltpu.SemaphoreType.DMA((RING,)),
    "sis": pltpu.SemaphoreType.DMA((RING,)),
    "sir": pltpu.SemaphoreType.DMA((RING,)),
    "xis": pltpu.SemaphoreType.DMA((RING,)),
    "xir": pltpu.SemaphoreType.DMA((RING,)),
}


class Names:
    pass


def kernel(plen, prow, clen_in, q_in, skv, pkv, dq, nkv, cache, w_in, out_p, out_d, *scratch):
    s = Names()
    for name, ref in zip(SCRATCH, scratch):
        setattr(s, name, ref)

    me = lax.axis_index("ctx")
    y, z = lax.div(me, RING), lax.rem(me, RING)
    head = lax.axis_index("head")
    x, core = lax.div(head, 2), lax.rem(head, 2)
    other = 1 - lax.axis_index("grp")

    def turned(j):
        return lax.rem(y + lax.div(j * (j + 1), 2), RING)

    def near(p):
        high = lax.rem(lax.div(z, 2) + lax.div(p, 2), 2)
        return 2 * high + lax.rem(z + p, 2)

    up, down, far = lax.rem(y + 1, RING), lax.rem(y + 3, RING), lax.rem(y + 2, RING)

    def at_y(yy):
        return {"ctx": yy * RING + z}

    def at_z(zz):
        return {"ctx": y * RING + zz}

    def across(zz):
        return {"ctx": y * RING + zz, "grp": other}

    def at_x(xx):
        return {"head": xx * 2 + core}

    sibling = {"head": x * 2 + 1 - core}

    def send(src, dst, ssem, rsem, device):
        return pltpu.make_async_remote_copy(
            src_ref=src, dst_ref=dst, send_sem=ssem, recv_sem=rsem, device_id=device, device_id_type=MESH
        )

    def arrived(dst, rsem):
        send(dst, dst, s.loc.at[0], rsem, sibling).wait_recv()

    pairs = [
        (pkv.at[0], s.kl.at[pl.ds(0, PRE)]),
        (skv.at[0], s.kl.at[pl.ds(PRE, SPAN)]),
        (pkv.at[1], s.vb.at[y, pl.ds(0, PRE)]),
        (skv.at[1], s.vb.at[y, pl.ds(PRE, SPAN)]),
    ]
    pairs += [(q_in.at[:, pl.ds(h * HD, HD)], s.qb.at[z, pl.ds(h * SPAN, SPAN)]) for h in range(GQ)]
    pairs += [(dq, s.dq), (nkv, s.nkv), (clen_in, s.clen), (cache.at[0], s.ck), (cache.at[1], s.cv), (w_in, s.wb)]
    loads = [pltpu.make_async_copy(src, dst, s.loc.at[at]) for at, (src, dst) in enumerate(pairs)]
    for load in loads:
        load.start()

    barrier = pltpu.get_barrier_semaphore()
    greeted = [at_y(lax.rem(y + d, RING)) for d in (1, 2, 3)] + [at_z(lax.rem(z + d, RING)) for d in (1, 2, 3)]
    greeted += [across(zz) for zz in range(RING)] + [sibling] + [at_x(lax.rem(x + d, RING)) for d in (1, 2, 3)]
    for device in greeted:
        pl.semaphore_signal(barrier, inc=1, device_id=device, device_id_type=MESH)

    def clear(p, carry):
        s.acc[p] = jnp.zeros((GQ * SPAN, HD), F32)
        s.tot[p] = jnp.zeros((GQ * SPAN, HD), F32)
        s.top[p] = jnp.full((GQ * SPAN, HD), MASKED, F32)
        slot = iota((HD, KEYS), 1)
        unused = ((p * RING + z) * PRE + slot >= plen[0]) & (slot < PRE) & (iota((HD, KEYS), 0) == 0)
        s.kb[p, HD : 2 * HD, :] = jnp.where(unused, MASKED, 0.0).astype(BF16)
        return carry

    lax.fori_loop(0, RING, clear, 0)


    for load in loads[2:12]:
        load.wait()
    pl.semaphore_wait(barrier, len(greeted))

    def keys_of(yy):
        return s.kb.at[yy, pl.ds(0, HD)]

    kv_own = [
        send(s.vb.at[y], s.vb.at[y], s.kvs.at[0], s.vr.at[y], at_y(up)),
        send(s.vb.at[y], s.vb.at[y], s.kvs.at[1], s.vr.at[y], at_y(down)),
        send(keys_of(y), keys_of(y), s.kvs.at[2], s.kr.at[y], at_y(up)),
        send(keys_of(y), keys_of(y), s.kvs.at[3], s.kr.at[y], at_y(down)),
    ]
    kv_on = [
        send(keys_of(down), keys_of(down), s.kvs.at[4], s.kr.at[down], at_y(up)),
        send(s.vb.at[up], s.vb.at[up], s.kvs.at[5], s.vr.at[up], at_y(down)),
    ]

    def q_copy(source, step, sem):
        return send(s.qb.at[source], s.qb.at[source], s.qs.at[sem], s.qr.at[source], at_z(z + step))

    q_first = [(z < 3, z, 1, 0), (z > 0, z, -1, 1)]
    q_second = [((z > 0) & (z < 3), z - 1, 1, 2), ((z > 0) & (z < 3), z + 1, -1, 3)]
    q_third = [(z == 2, z - 2, 1, 4), (z == 1, z + 2, -1, 5)]

    def q_start(group):
        for when, source, step, sem in group:

            @pl.when(when)
            def _(source=source, step=step, sem=sem):
                q_copy(source, step, sem).start()

    def q_wait(distance):
        @pl.when(z >= distance)
        def _():
            arrived(s.qb.at[z - distance], s.qr.at[z - distance])

        @pl.when(z + distance < RING)
        def _():
            arrived(s.qb.at[z + distance], s.qr.at[z + distance])

    def b_copy(d):
        return send(s.sb.at[y], s.sb.at[y], s.bs.at[d], s.br.at[y], at_y(lax.rem(y + d, RING)))

    for copy in kv_own[:2]:
        copy.start()
    q_start(q_first)
    for load in loads[:2]:
        load.wait()
    s.kb[y, 0:HD, :] = s.kl[...].T
    for copy in kv_own[2:]:
        copy.start()

    for load in loads[12:15]:
        load.wait()
    for r in range(ROWS):
        row = s.dq[r].astype(F32)
        for h in range(GQ):
            s.qf[pl.ds(r * QROWS + h, STEPS, stride=GQ), :] = row[:, h * HD : (h + 1) * HD]
    s.kn[...] = jnp.zeros((HD, HD), F32)
    s.vn[...] = jnp.zeros((HD, HD), F32)
    for r in range(ROWS):
        s.kn[pl.ds(r * STEPS, STEPS), :] = s.nkv[0, r].astype(F32)
        s.vn[pl.ds(r * STEPS, STEPS), :] = s.nkv[1, r].astype(F32)

    def picked(ref):
        def add(r, total):
            mine = jnp.where(me * ROWS + r == prow[0], 1.0, 0.0)
            return total + mine * ref[pl.ds(pl.multiple_of(r * QROWS, QROWS), QROWS), :]

        return lax.fori_loop(0, ROWS, add, jnp.zeros((QROWS, HD), F32))

    s.sb[y] = picked(s.qf).astype(BF16)

    for d in (1, 2, 3):
        b_copy(d).start()

    lanes = (ROWS * QROWS, HD)
    at_row, at_key = iota(lanes, 0), iota(lanes, 1)
    same = lax.shift_right_logical(at_row, 5) == lax.shift_right_logical(at_key, 2)
    early = jnp.bitwise_and(at_key, 3) <= jnp.bitwise_and(lax.shift_right_logical(at_row, 3), 3)
    new = jnp.where(same & early, dot_nt(s.qf[...].astype(BF16), s.kn[...].astype(BF16)) * SCALE, MASKED)
    new_top = jnp.max(new, axis=1, keepdims=True)
    new_weights = jnp.exp2(new - new_top)
    s.mf[...] = jnp.broadcast_to(new_top, lanes)
    s.lf[...] = jnp.broadcast_to(jnp.sum(new_weights, axis=1, keepdims=True), lanes)
    s.of[...] = dot_nn(new_weights.astype(BF16), s.vn[...].astype(BF16))

    for load in loads[15:]:
        load.wait()

    def cached(r):
        rows = pl.ds(pl.multiple_of(r * QROWS, QROWS), QROWS)
        scores = dot_nt(s.qf[rows, :].astype(BF16), s.ck[r]) * SCALE
        scores = jnp.where(iota((QROWS, SLOTS), 1) < s.clen[0, r], scores, MASKED)
        before = s.mf[rows, :]
        after = jnp.maximum(before, jnp.max(scores, axis=1, keepdims=True))
        weights = jnp.exp2(scores - after[:, :1])
        keep = jnp.exp2(before - after)
        total = s.lf[rows, :] * keep + jnp.sum(weights, axis=1, keepdims=True)
        mixed = s.of[rows, :] * keep + dot_nn(weights.astype(BF16), s.cv[r])
        s.of[rows, :] = mixed / total
        s.lf[rows, :] = after + log2(total)

    def first_queries():
        q_wait(1)
        q_start(q_second)

    def some_rows(i, carry):
        @pl.when(i == 2)
        def _():
            first_queries()

        for u in range(4):
            cached(i * 4 + u)
        return carry

    lax.fori_loop(0, ROWS // 4, some_rows, 0)
    for h in range(GQ):
        s.ab[y, z, h] = s.of[pl.ds(h, ROWS * STEPS, stride=GQ), :].astype(BF16)

    def a_copy(p):
        return send(s.ab.at[y, z], s.ab.at[y, z], s.as_.at[p], s.ar.at[z], at_z(near(p)))

    def ay_copy(yy, p, sem, to):
        block = s.ab.at[yy, near(p)]
        return send(block, block, s.ays.at[sem], s.ayr.at[yy, near(p)], at_y(to))

    def ay_own(p):
        return [ay_copy(y, p, 3 * p, up), ay_copy(y, p, 3 * p + 1, down)]

    def ay_on(p):
        return ay_copy(down, p, 3 * p + 2, up) if p < 2 else ay_copy(up, p, 3 * p + 2, down)

    def rows_in(yy, p):
        arrived(s.ab.at[yy, near(p)], s.ayr.at[yy, near(p)])

    def spread_rows(p):
        if p:
            arrived(s.ab.at[y, near(p)], s.ar.at[near(p)])
        for copy in ay_own(p):
            copy.start()

    def pass_rows(p):
        rows_in(down if p < 2 else up, p)
        ay_on(p).start()

    def rest_of_rows():
        for p in range(RING):
            rows_in(up if p < 2 else down, p)

    def far_rows():
        for p in range(RING):
            rows_in(far, p)

    for p in (1, 2, 3):
        a_copy(p).start()
    spread_rows(0)
    s.sl[z] = jnp.broadcast_to(to_row(picked(s.lf)), (8, HD))

    def x_copy(d):
        zz = lax.rem(z + d, RING)
        return send(s.sx, s.xb.at[z], s.xs.at[d], s.xr.at[z], across(zz))

    def pass_query():
        for d in (1, 2, 3):
            yy = lax.rem(y + d, RING)
            arrived(s.sb.at[yy], s.br.at[yy])
        total = s.sb[0].astype(F32)
        for yy in (1, 2, 3):
            total = total + s.sb[yy].astype(F32)
        s.sx[...] = total.astype(BF16)
        for d in range(RING):
            x_copy(d).start()

    def h_copies(d):
        zz = lax.rem(z + d, RING)
        copies = [
            send(s.hos, s.ho.at[z], s.hs.at[d], s.hr.at[z], across(zz)),
            send(s.hls, s.hl.at[z], s.hls_s.at[d], s.hlr.at[z], across(zz)),
        ]
        if d:
            copies.append(send(s.sl.at[z], s.sl.at[z], s.sls.at[d], s.slr.at[z], at_z(zz)))
        return copies

    def answer():
        for zz in range(RING):
            arrived(s.xb.at[zz], s.xr.at[zz])
        query = s.xb[0].astype(F32)
        for zz in (1, 2, 3):
            query = query + s.xb[zz].astype(F32)
        span = pl.ds(PRE, SPAN)
        scores = dot_nn(query.astype(BF16), s.kb[y, 0:HD, span]) * SCALE
        top = jnp.max(scores, axis=1, keepdims=True)
        weights = jnp.exp2(scores - top)
        total = jnp.sum(weights, axis=1, keepdims=True)
        s.hos[...] = (dot_nn(weights.astype(BF16), s.vb[y, span, :]) / total).astype(BF16)
        level = jnp.broadcast_to(top + log2(total), (QROWS, HD))
        s.hls[...] = jnp.broadcast_to(to_row(level), (8, HD))
        for d in range(RING):
            for copy in h_copies(d):
                copy.start()

    def h2_copies(d):
        yy = lax.rem(y + d, RING)
        return [
            send(s.ho2.at[y], s.ho2.at[y], s.h2s.at[d], s.h2r.at[y], at_y(yy)),
            send(s.hl2.at[y], s.hl2.at[y], s.hl2s.at[d], s.hl2r.at[y], at_y(yy)),
        ]

    def combine_z():
        for zz in range(RING):
            arrived(s.ho.at[zz], s.hr.at[zz])
            arrived(s.hl.at[zz], s.hlr.at[zz])
        for d in (1, 2, 3):
            zz = lax.rem(z + d, RING)
            arrived(s.sl.at[zz], s.slr.at[zz])
        out, level = merge([(s.ho[zz].astype(F32), to_column(s.hl[zz, 0:1, :], QROWS)) for zz in range(RING)])
        s.ho2[y] = out.astype(BF16)
        s.hl2[y, 0:8, :] = jnp.broadcast_to(to_row(jnp.broadcast_to(level, (QROWS, HD))), (8, HD))
        s.hl2[y, 8:16, :] = s.sl[0] + s.sl[1] + s.sl[2] + s.sl[3]
        for d in (1, 2, 3):
            for copy in h2_copies(d):
                copy.start()

    def combine_y():
        for d in (1, 2, 3):
            yy = lax.rem(y + d, RING)
            arrived(s.ho2.at[yy], s.h2r.at[yy])
            arrived(s.hl2.at[yy], s.hl2r.at[yy])
        out, level = merge([(s.ho2[yy].astype(F32), to_column(s.hl2[yy, 0:1, :], QROWS)) for yy in range(RING)])
        rows = s.hl2[0, 8:9, :] + s.hl2[1, 8:9, :] + s.hl2[2, 8:9, :] + s.hl2[3, 8:9, :]
        before = to_column(rows, QROWS)
        top = jnp.maximum(before, level)
        w_own, w_span = jnp.exp2(before - top), jnp.exp2(level - top)
        total = w_own + w_span
        keep = jnp.broadcast_to(w_own / total, (QROWS, HD))
        added = out * (w_span / total)
        for at in range(2):
            s.wt[pl.ds(at * QROWS, QROWS), :] = keep
            s.ot[pl.ds(at * QROWS, QROWS), :] = added

    def si_copy(j):
        return send(s.so.at[j], s.si.at[j], s.sis.at[j], s.sir.at[j], sibling)

    def project(j):
        yc = turned(j)
        count = RING * ROWS * STEPS
        row = yc * (RING * ROWS) + lax.shift_right_logical(iota((count, HD), 0), 2)
        hit = row == prow[0]
        for h in range(GQ):
            block = jnp.concatenate([s.ab[yc, zz, h] for zz in range(RING)], axis=0).astype(F32)
            keep = s.wt[pl.ds(h, 2 * STEPS, stride=GQ), :]
            added = s.ot[pl.ds(h, 2 * STEPS, stride=GQ), :]
            keep = jnp.concatenate([keep] * (count // (2 * STEPS)), axis=0)
            added = jnp.concatenate([added] * (count // (2 * STEPS)), axis=0)
            block = jnp.where(hit, block * keep + added, block)
            s.am[:, h * HD : (h + 1) * HD] = block.astype(BF16)
        s.pr[...] = dot_nn(s.am[...], s.wb[...])
        s.pm[j] = s.pr[pl.ds(pl.multiple_of(core * 128, 128), 128), :]
        s.so[j] = s.pr[pl.ds(pl.multiple_of((1 - core) * 128, 128), 128), :].astype(BF16)
        si_copy(j).start()

    def xi_copy(j):
        return send(s.xo.at[j], s.xi.at[x], s.xis.at[j], s.xir.at[x], at_x(turned(j)))

    def join(j):
        arrived(s.si.at[j], s.sir.at[j])
        total = s.pm[j] + s.si[j].astype(F32)

        @pl.when(turned(j) == x)
        def _():
            s.own[...] = total

        @pl.when(turned(j) != x)
        def _():
            s.xo[j] = total.astype(BF16)
            xi_copy(j).start()

    count = BLOCK // SPAN
    first_lane = jnp.where(iota((BLOCK, HD), 1) == 0, 1.0, 0.0).astype(BF16)
    ones = jnp.ones((KEYS, HD), BF16)

    def scores_of(at, b, held, peak):
        p, yc = lookup(PIECES, at), turned(lookup(CHUNKS, at))
        zq = near(p)
        late = (y * RING + zq) * SPAN - (yc * RING + z) * SPAN
        shape = (SPAN, SPAN)
        ahead = jnp.where(iota(shape, 1) - iota(shape, 0) <= late, 0.0, MASKED)
        ahead = jnp.concatenate([ahead] * count, axis=0)
        queries = jnp.concatenate([s.qb[zq, b * BLOCK : (b + 1) * BLOCK, :], first_lane], axis=1)
        scores = dot_nn(queries, s.kb[yc])
        highest = None
        for k in range(KEYS // HD):
            cols = slice(k * HD, (k + 1) * HD)
            part = scores[:, cols] * SCALE
            if k == PRE // HD:
                part = part + ahead
            held[:, cols] = part
            highest = part if highest is None else jnp.maximum(highest, part)
        peak[...] = jnp.broadcast_to(jnp.max(highest, axis=1, keepdims=True), (BLOCK, HD))

    def weigh(at, b, held, peak):
        p, yc = lookup(PIECES, at), turned(lookup(CHUNKS, at))
        rows = slice(b * BLOCK, (b + 1) * BLOCK)
        before = s.top[p, rows, :]
        after = jnp.maximum(before, peak[...])
        keep = jnp.exp2(before - after)
        packed = []
        for k in range(KEYS // HD):
            packed.append(jnp.exp2(held[:, k * HD : (k + 1) * HD] - after).astype(BF16))
        mixed = dot_nn(jnp.concatenate(packed, axis=1), jnp.concatenate([s.vb[yc], ones], axis=1))
        s.top[p, rows, :] = after
        s.tot[p, rows, :] = s.tot[p, rows, :] * keep + mixed[:, HD:]
        s.acc[p, rows, :] = s.acc[p, rows, :] * keep + mixed[:, :HD]

    def o_copies(p):
        return [
            send(s.os.at[p], s.orb.at[p], s.ops.at[p], s.opr.at[p], at_z(near(p))),
            send(s.ls.at[p], s.lrb.at[p], s.lps.at[p], s.lpr.at[p], at_z(near(p))),
        ]

    def each_head(one):
        def some(i, carry):
            for u in range(4):
                one(i * 4 + u)
            return carry

        lax.fori_loop(0, GQ // 4, some, 0)

    def ship(p):
        def one(h):
            rows = pl.ds(pl.multiple_of(h * SPAN, SPAN), SPAN)
            total = s.tot[p, rows, :]
            s.os[p, h] = (s.acc[p, rows, :] / total).astype(BF16)
            s.ls[p, pl.ds(h, 1), :] = to_row(s.top[p, rows, :] + log2(total))

        each_head(one)
        for copy in o_copies(p):
            copy.start()

    def settle():
        def one(h):
            rows = pl.ds(pl.multiple_of(h * SPAN, SPAN), SPAN)
            levels = [to_column(s.lrb[p, pl.ds(h, 1), :], SPAN) for p in (1, 2, 3)]
            top = s.top[0, rows, :]
            for level in levels:
                top = jnp.maximum(top, level)
            weight = jnp.exp2(s.top[0, rows, :] - top)
            total = s.tot[0, rows, :] * weight
            mixed = s.acc[0, rows, :] * weight
            for p, level in zip((1, 2, 3), levels):
                weight = jnp.exp2(level - top)
                total = total + weight
                mixed = mixed + s.orb[p, h].astype(F32) * weight
            out_p[:, pl.ds(pl.multiple_of(h * HD, HD), HD)] = (mixed / total).astype(BF16)

        each_head(one)

    def keys_near():
        arrived(keys_of(down), s.kr.at[down])
        kv_on[0].start()
        arrived(s.vb.at[up], s.vr.at[up])
        kv_on[1].start()
        arrived(s.vb.at[down], s.vr.at[down])
        arrived(keys_of(up), s.kr.at[up])

    def keys_far():
        arrived(keys_of(far), s.kr.at[far])
        arrived(s.vb.at[far], s.vr.at[far])

    def second_queries():
        q_wait(2)
        q_start(q_third)

    actions = {
        0: [pass_query],
        2: [keys_near],
        3: [answer],
        4: [second_queries, lambda: spread_rows(1)],
        5: [lambda: pass_rows(0)],
        6: [combine_z, lambda: spread_rows(2)],
        7: [keys_far, lambda: pass_rows(1)],
        8: [lambda: q_wait(3), lambda: spread_rows(3)],
        9: [combine_y, lambda: pass_rows(2)],
        10: [lambda: pass_rows(3)],
        12: [rest_of_rows],
        14: [far_rows],
    }

    def prepare(i):
        for at, todo in actions.items():

            @pl.when(i == at)
            def _(todo=todo):
                for action in todo:
                    action()

        @pl.when((i == 11) | ((i >= 13) & (i < 16)))
        def _():
            join(jnp.maximum(i - 12, 0))

        @pl.when((i == 10) | ((i >= 12) & (i < 15)))
        def _():
            project(jnp.maximum(i - 11, 0))

    def step(i, carry):
        scores_of(i, 1, s.ts1, s.mx1)
        weigh(i, 0, s.ts0, s.mx0)
        prepare(i + 1)
        scores_of(jnp.minimum(i + 1, 15), 0, s.ts0, s.mx0)
        weigh(i, 1, s.ts1, s.mx1)
        p, k = lookup(PIECES, i), lookup(CHUNKS, i)

        @pl.when((k == 3) & (p > 0))
        def _():
            ship(p)

        return carry

    for action in actions.pop(0):
        action()
    scores_of(0, 0, s.ts0, s.mx0)
    lax.fori_loop(0, 16, step, 0)
    for p in (1, 2, 3):
        arrived(s.orb.at[p], s.opr.at[p])
        arrived(s.lrb.at[p], s.lpr.at[p])
    settle()

    total = s.own[...]
    for d in (1, 2, 3):
        xx = lax.rem(x + d, RING)
        arrived(s.xi.at[xx], s.xir.at[xx])
        total = total + s.xi[xx].astype(F32)
    for r in range(32):
        out_d[r] = total[r * STEPS : (r + 1) * STEPS, :].astype(BF16)

    for copy in kv_own + kv_on + [c for p in range(RING) for c in ay_own(p) + [ay_on(p)]]:
        copy.wait_send()
    for when, source, step_z, sem in q_first + q_second + q_third:

        @pl.when(when)
        def _(source=source, step_z=step_z, sem=sem):
            q_copy(source, step_z, sem).wait_send()

    for d in range(RING):
        x_copy(d).wait_send()
        for copy in h_copies(d):
            copy.wait_send()
        if d:
            b_copy(d).wait_send()
            a_copy(d).wait_send()
            for copy in h2_copies(d):
                copy.wait_send()
            for copy in o_copies(d):
                copy.wait_send()
    for j in range(RING):
        si_copy(j).wait_send()

        @pl.when(turned(j) != x)
        def _(j=j):
            xi_copy(j).wait_send()


def shards(span_q, span_kv, prefix_kv, prefix_len, dec_q, dec_new_kv, dec_cache, cache_len, prompt_row, out_weight):
    vmem = pl.BlockSpec(memory_space=pltpu.VMEM)
    smem = pl.BlockSpec(memory_space=pltpu.SMEM)
    hbm = pl.BlockSpec(memory_space=pltpu.HBM)
    prefill, decode = pl.pallas_call(
        kernel,
        out_shape=(
            jax.ShapeDtypeStruct((SPAN, GQ * HD), BF16),
            jax.ShapeDtypeStruct((32, STEPS, COLS), BF16),
        ),
        in_specs=[smem] * 2 + [hbm] * 8,
        out_specs=(vmem, vmem),
        scratch_shapes=list(SCRATCH.values()),
        compiler_params=pltpu.CompilerParams(
            collective_id=0, has_side_effects=True, vmem_limit_bytes=VMEM_BYTES
        ),
        cost_estimate=pl.CostEstimate(flops=11_000_000_000, bytes_accessed=8_000_000, transcendentals=17_000_000),
    )(
        prefix_len,
        prompt_row,
        *[
            pltpu.with_memory_space_constraint(operand, pltpu.HBM)
            for operand in (
                cache_len,
                span_q[0],
                span_kv[0],
                prefix_kv[0],
                dec_q[0],
                dec_new_kv[0],
                dec_cache[0],
                out_weight,
            )
        ],
    )
    return prefill[None], decode[None]


def solution(mesh):
    placed = (
        P("grp", "ctx", "head"),
        P("grp", None, "ctx", "head"),
        P("grp", None, "ctx", "head"),
        P("grp"),
        P("grp", "ctx", None, "head"),
        P("grp", None, "ctx", None, "head"),
        P("grp", None, "ctx", None, "head"),
        P("grp", "ctx"),
        P("grp"),
        P("head", "ctx"),
    )
    return jax.shard_map(
        shards,
        mesh=mesh,
        in_specs=placed,
        out_specs=(P("grp", "ctx", "head"), P("grp", "head", None, "ctx")),
        check_vma=False,
    )
```

```python
import math

import jax
import jax.numpy as jnp
from jax import lax
from jax.experimental import pallas as pl
from jax.experimental.pallas import tpu as pltpu
from jax.sharding import PartitionSpec as P

HD = 128
GQ = 8
RING = 4
PRE = 896
SPAN = 128
KEYS = PRE + SPAN
ROWS = 16
STEPS = 4
SLOTS = 512
QROWS = STEPS * GQ
COLS = 512
MASKED = -1e30
LOG2E = math.log2(math.e)
SCALE = LOG2E / math.sqrt(HD)
MESH = pl.DeviceIdType.MESH
F32 = jnp.float32
BF16 = jnp.bfloat16
BLOCK = 512
VMEM_BYTES = 40 * 1024 * 1024

PIECES = (0, 2, 2, 2, 2, 3, 3, 3, 3, 1, 1, 1, 1, 0, 0, 0)
CHUNKS = (0, 0, 1, 2, 3, 0, 1, 2, 3, 0, 1, 2, 3, 1, 2, 3)


def dot_nt(a, b):
    return lax.dot_general(a, b, (((1,), (1,)), ((), ())), preferred_element_type=F32)


def dot_nn(a, b):
    return lax.dot_general(a, b, (((1,), (0,)), ((), ())), preferred_element_type=F32)


def log2(v):
    return jnp.log(v) * LOG2E


def iota(shape, axis):
    return lax.broadcasted_iota(jnp.int32, shape, axis)


def lookup(table, index):
    value = jnp.int32(table[0])
    for at, entry in enumerate(table[1:], 1):
        value = jnp.where(index == at, jnp.int32(entry), value)
    return value


def to_row(column):
    shape = column.shape
    return jnp.sum(jnp.where(iota(shape, 0) == iota(shape, 1), column, 0.0), axis=0, keepdims=True)


def to_column(row, count):
    shape = (count, HD)
    spread = jnp.broadcast_to(row, shape)
    return jnp.sum(jnp.where(iota(shape, 0) == iota(shape, 1), spread, 0.0), axis=1, keepdims=True)


def merge(parts):
    top = parts[0][1]
    for _, level in parts[1:]:
        top = jnp.maximum(top, level)
    weights = [jnp.exp2(level - top) for _, level in parts]
    total = weights[0]
    for w in weights[1:]:
        total = total + w
    mixed = parts[0][0] * weights[0]
    for (out, _), w in zip(parts[1:], weights[1:]):
        mixed = mixed + out * w
    return mixed / total, top + log2(total)


SCRATCH = {
    "kl": pltpu.VMEM((KEYS, HD), BF16),
    "kb": pltpu.VMEM((RING, 2 * HD, KEYS), BF16),
    "vb": pltpu.VMEM((RING, KEYS, HD), BF16),
    "qb": pltpu.VMEM((RING, GQ * SPAN, HD), BF16),
    "ts0": pltpu.VMEM((BLOCK, KEYS), F32),
    "ts1": pltpu.VMEM((BLOCK, KEYS), F32),
    "mx0": pltpu.VMEM((BLOCK, HD), F32),
    "mx1": pltpu.VMEM((BLOCK, HD), F32),
    "dq": pltpu.VMEM((ROWS, STEPS, GQ * HD), BF16),
    "nkv": pltpu.VMEM((2, ROWS, STEPS, HD), BF16),
    "acc": pltpu.VMEM((RING, GQ * SPAN, HD), F32),
    "top": pltpu.VMEM((RING, GQ * SPAN, HD), F32),
    "tot": pltpu.VMEM((RING, GQ * SPAN, HD), F32),
    "os": pltpu.VMEM((RING, GQ, SPAN, HD), BF16),
    "ls": pltpu.VMEM((RING, GQ, SPAN), F32),
    "orb": pltpu.VMEM((RING, GQ, SPAN, HD), BF16),
    "lrb": pltpu.VMEM((RING, GQ, SPAN), F32),
    "ck": pltpu.VMEM((ROWS, SLOTS, HD), BF16),
    "cv": pltpu.VMEM((ROWS, SLOTS, HD), BF16),
    "wb": pltpu.VMEM((GQ * HD, COLS), BF16),
    "qf": pltpu.VMEM((ROWS * QROWS, HD), F32),
    "kn": pltpu.VMEM((HD, HD), F32),
    "vn": pltpu.VMEM((HD, HD), F32),
    "of": pltpu.VMEM((ROWS * QROWS, HD), F32),
    "mf": pltpu.VMEM((ROWS * QROWS, HD), F32),
    "lf": pltpu.VMEM((ROWS * QROWS, HD), F32),
    "sb": pltpu.VMEM((RING, QROWS, HD), BF16),
    "sx": pltpu.VMEM((QROWS, HD), BF16),
    "xb": pltpu.VMEM((RING, QROWS, HD), BF16),
    "hos": pltpu.VMEM((QROWS, HD), BF16),
    "hls": pltpu.VMEM((8, HD), F32),
    "ho": pltpu.VMEM((RING, QROWS, HD), BF16),
    "hl": pltpu.VMEM((RING, 8, HD), F32),
    "sl": pltpu.VMEM((RING, 8, HD), F32),
    "ho2": pltpu.VMEM((RING, QROWS, HD), BF16),
    "hl2": pltpu.VMEM((RING, 16, HD), F32),
    "wt": pltpu.VMEM((2 * QROWS, HD), F32),
    "ot": pltpu.VMEM((2 * QROWS, HD), F32),
    "ab": pltpu.VMEM((RING, RING, GQ, ROWS * STEPS, HD), BF16),
    "am": pltpu.VMEM((RING * ROWS * STEPS, GQ * HD), BF16),
    "pr": pltpu.VMEM((RING * ROWS * STEPS, COLS), F32),
    "pm": pltpu.VMEM((RING, 128, COLS), F32),
    "so": pltpu.VMEM((RING, 128, COLS), BF16),
    "si": pltpu.VMEM((RING, 128, COLS), BF16),
    "xo": pltpu.VMEM((RING, 128, COLS), BF16),
    "xi": pltpu.VMEM((RING, 128, COLS), BF16),
    "own": pltpu.VMEM((128, COLS), F32),
    "clen": pltpu.SMEM((1, ROWS), jnp.int32),
    "loc": pltpu.SemaphoreType.DMA((18,)),
    "kvs": pltpu.SemaphoreType.DMA((6,)),
    "kr": pltpu.SemaphoreType.DMA((RING,)),
    "vr": pltpu.SemaphoreType.DMA((RING,)),
    "qs": pltpu.SemaphoreType.DMA((6,)),
    "qr": pltpu.SemaphoreType.DMA((RING,)),
    "bs": pltpu.SemaphoreType.DMA((RING,)),
    "br": pltpu.SemaphoreType.DMA((RING,)),
    "xs": pltpu.SemaphoreType.DMA((RING,)),
    "xr": pltpu.SemaphoreType.DMA((RING,)),
    "hs": pltpu.SemaphoreType.DMA((RING,)),
    "hr": pltpu.SemaphoreType.DMA((RING,)),
    "hls_s": pltpu.SemaphoreType.DMA((RING,)),
    "hlr": pltpu.SemaphoreType.DMA((RING,)),
    "sls": pltpu.SemaphoreType.DMA((RING,)),
    "slr": pltpu.SemaphoreType.DMA((RING,)),
    "h2s": pltpu.SemaphoreType.DMA((RING,)),
    "h2r": pltpu.SemaphoreType.DMA((RING,)),
    "hl2s": pltpu.SemaphoreType.DMA((RING,)),
    "hl2r": pltpu.SemaphoreType.DMA((RING,)),
    "as_": pltpu.SemaphoreType.DMA((RING,)),
    "ar": pltpu.SemaphoreType.DMA((RING,)),
    "ays": pltpu.SemaphoreType.DMA((3 * RING,)),
    "ayr": pltpu.SemaphoreType.DMA((RING, RING)),
    "ops": pltpu.SemaphoreType.DMA((RING,)),
    "opr": pltpu.SemaphoreType.DMA((RING,)),
    "lps": pltpu.SemaphoreType.DMA((RING,)),
    "lpr": pltpu.SemaphoreType.DMA((RING,)),
    "sis": pltpu.SemaphoreType.DMA((RING,)),
    "sir": pltpu.SemaphoreType.DMA((RING,)),
    "xis": pltpu.SemaphoreType.DMA((RING,)),
    "xir": pltpu.SemaphoreType.DMA((RING,)),
}


class Names:
    pass


def kernel(plen, prow, clen_in, q_in, skv, pkv, dq, nkv, cache, w_in, out_p, out_d, *scratch):
    s = Names()
    for name, ref in zip(SCRATCH, scratch):
        setattr(s, name, ref)

    me = lax.axis_index("ctx")
    y, z = lax.div(me, RING), lax.rem(me, RING)
    head = lax.axis_index("head")
    x, core = lax.div(head, 2), lax.rem(head, 2)
    other = 1 - lax.axis_index("grp")

    def turned(j):
        return lax.rem(y + lax.div(j * (j + 1), 2), RING)

    def near(p):
        high = lax.rem(lax.div(z, 2) + lax.div(p, 2), 2)
        return 2 * high + lax.rem(z + p, 2)

    up, down, far = lax.rem(y + 1, RING), lax.rem(y + 3, RING), lax.rem(y + 2, RING)

    def at_y(yy):
        return {"ctx": yy * RING + z}

    def at_z(zz):
        return {"ctx": y * RING + zz}

    def across(zz):
        return {"ctx": y * RING + zz, "grp": other}

    def at_x(xx):
        return {"head": xx * 2 + core}

    sibling = {"head": x * 2 + 1 - core}

    def send(src, dst, ssem, rsem, device):
        return pltpu.make_async_remote_copy(
            src_ref=src, dst_ref=dst, send_sem=ssem, recv_sem=rsem, device_id=device, device_id_type=MESH
        )

    def arrived(dst, rsem):
        send(dst, dst, s.loc.at[0], rsem, sibling).wait_recv()

    pairs = [
        (pkv.at[0], s.kl.at[pl.ds(0, PRE)]),
        (skv.at[0], s.kl.at[pl.ds(PRE, SPAN)]),
        (pkv.at[1], s.vb.at[y, pl.ds(0, PRE)]),
        (skv.at[1], s.vb.at[y, pl.ds(PRE, SPAN)]),
    ]
    pairs += [(q_in.at[:, pl.ds(h * HD, HD)], s.qb.at[z, pl.ds(h * SPAN, SPAN)]) for h in range(GQ)]
    pairs += [(dq, s.dq), (nkv, s.nkv), (clen_in, s.clen), (cache.at[0], s.ck), (cache.at[1], s.cv), (w_in, s.wb)]
    loads = [pltpu.make_async_copy(src, dst, s.loc.at[at]) for at, (src, dst) in enumerate(pairs)]
    for load in loads:
        load.start()

    barrier = pltpu.get_barrier_semaphore()
    greeted = [at_y(lax.rem(y + d, RING)) for d in (1, 2, 3)] + [at_z(lax.rem(z + d, RING)) for d in (1, 2, 3)]
    greeted += [across(zz) for zz in range(RING)] + [sibling] + [at_x(lax.rem(x + d, RING)) for d in (1, 2, 3)]
    for device in greeted:
        pl.semaphore_signal(barrier, inc=1, device_id=device, device_id_type=MESH)

    def clear(p, carry):
        s.acc[p] = jnp.zeros((GQ * SPAN, HD), F32)
        s.tot[p] = jnp.zeros((GQ * SPAN, HD), F32)
        s.top[p] = jnp.full((GQ * SPAN, HD), MASKED, F32)
        slot = iota((HD, KEYS), 1)
        unused = ((p * RING + z) * PRE + slot >= plen[0]) & (slot < PRE) & (iota((HD, KEYS), 0) == 0)
        s.kb[p, HD : 2 * HD, :] = jnp.where(unused, MASKED, 0.0).astype(BF16)
        return carry

    lax.fori_loop(0, RING, clear, 0)


    for load in loads[2:12]:
        load.wait()
    pl.semaphore_wait(barrier, len(greeted))

    def keys_of(yy):
        return s.kb.at[yy, pl.ds(0, HD)]

    kv_own = [
        send(s.vb.at[y], s.vb.at[y], s.kvs.at[0], s.vr.at[y], at_y(up)),
        send(s.vb.at[y], s.vb.at[y], s.kvs.at[1], s.vr.at[y], at_y(down)),
        send(keys_of(y), keys_of(y), s.kvs.at[2], s.kr.at[y], at_y(up)),
        send(keys_of(y), keys_of(y), s.kvs.at[3], s.kr.at[y], at_y(down)),
    ]
    kv_on = [
        send(keys_of(down), keys_of(down), s.kvs.at[4], s.kr.at[down], at_y(up)),
        send(s.vb.at[up], s.vb.at[up], s.kvs.at[5], s.vr.at[up], at_y(down)),
    ]

    def q_copy(source, step, sem):
        return send(s.qb.at[source], s.qb.at[source], s.qs.at[sem], s.qr.at[source], at_z(z + step))

    q_first = [(z < 3, z, 1, 0), (z > 0, z, -1, 1)]
    q_second = [((z > 0) & (z < 3), z - 1, 1, 2), ((z > 0) & (z < 3), z + 1, -1, 3)]
    q_third = [(z == 2, z - 2, 1, 4), (z == 1, z + 2, -1, 5)]

    def q_start(group):
        for when, source, step, sem in group:

            @pl.when(when)
            def _(source=source, step=step, sem=sem):
                q_copy(source, step, sem).start()

    def q_wait(distance):
        @pl.when(z >= distance)
        def _():
            arrived(s.qb.at[z - distance], s.qr.at[z - distance])

        @pl.when(z + distance < RING)
        def _():
            arrived(s.qb.at[z + distance], s.qr.at[z + distance])

    def b_copy(d):
        return send(s.sb.at[y], s.sb.at[y], s.bs.at[d], s.br.at[y], at_y(lax.rem(y + d, RING)))

    for copy in kv_own[:2]:
        copy.start()
    q_start(q_first)
    for load in loads[:2]:
        load.wait()
    s.kb[y, 0:HD, :] = s.kl[...].T
    for copy in kv_own[2:]:
        copy.start()

    for load in loads[12:15]:
        load.wait()
    for r in range(ROWS):
        row = s.dq[r].astype(F32)
        for h in range(GQ):
            s.qf[pl.ds(r * QROWS + h, STEPS, stride=GQ), :] = row[:, h * HD : (h + 1) * HD]
    s.kn[...] = jnp.zeros((HD, HD), F32)
    s.vn[...] = jnp.zeros((HD, HD), F32)
    for r in range(ROWS):
        s.kn[pl.ds(r * STEPS, STEPS), :] = s.nkv[0, r].astype(F32)
        s.vn[pl.ds(r * STEPS, STEPS), :] = s.nkv[1, r].astype(F32)

    def picked(ref):
        total = jnp.zeros((QROWS, HD), F32)
        for r in range(ROWS):
            mine = jnp.where(me * ROWS + r == prow[0], 1.0, 0.0)
            total = total + mine * ref[r * QROWS : (r + 1) * QROWS, :]
        return total

    s.sb[y] = picked(s.qf).astype(BF16)

    for d in (1, 2, 3):
        b_copy(d).start()

    lanes = (ROWS * QROWS, HD)
    at_row, at_key = iota(lanes, 0), iota(lanes, 1)
    same = lax.shift_right_logical(at_row, 5) == lax.shift_right_logical(at_key, 2)
    early = jnp.bitwise_and(at_key, 3) <= jnp.bitwise_and(lax.shift_right_logical(at_row, 3), 3)
    new = jnp.where(same & early, dot_nt(s.qf[...].astype(BF16), s.kn[...].astype(BF16)) * SCALE, MASKED)
    new_top = jnp.max(new, axis=1, keepdims=True)
    new_weights = jnp.exp2(new - new_top)
    s.mf[...] = jnp.broadcast_to(new_top, lanes)
    s.lf[...] = jnp.broadcast_to(jnp.sum(new_weights, axis=1, keepdims=True), lanes)
    s.of[...] = dot_nn(new_weights.astype(BF16), s.vn[...].astype(BF16))

    for load in loads[15:]:
        load.wait()

    def cached(r):
        rows = pl.ds(pl.multiple_of(r * QROWS, QROWS), QROWS)
        scores = dot_nt(s.qf[rows, :].astype(BF16), s.ck[r]) * SCALE
        scores = jnp.where(iota((QROWS, SLOTS), 1) < s.clen[0, r], scores, MASKED)
        before = s.mf[rows, :]
        after = jnp.maximum(before, jnp.max(scores, axis=1, keepdims=True))
        weights = jnp.exp2(scores - after[:, :1])
        keep = jnp.exp2(before - after)
        total = s.lf[rows, :] * keep + jnp.sum(weights, axis=1, keepdims=True)
        mixed = s.of[rows, :] * keep + dot_nn(weights.astype(BF16), s.cv[r])
        s.of[rows, :] = mixed / total
        s.lf[rows, :] = after + log2(total)

    def first_queries():
        q_wait(1)
        q_start(q_second)

    def some_rows(i, carry):
        @pl.when(i == 1)
        def _():
            first_queries()

        for u in range(8):
            cached(i * 8 + u)
        return carry

    lax.fori_loop(0, ROWS // 8, some_rows, 0)
    for h in range(GQ):
        s.ab[y, z, h] = s.of[pl.ds(h, ROWS * STEPS, stride=GQ), :].astype(BF16)

    def a_copy(p):
        return send(s.ab.at[y, z], s.ab.at[y, z], s.as_.at[p], s.ar.at[z], at_z(near(p)))

    def ay_copy(yy, p, sem, to):
        block = s.ab.at[yy, near(p)]
        return send(block, block, s.ays.at[sem], s.ayr.at[yy, near(p)], at_y(to))

    def ay_own(p):
        return [ay_copy(y, p, 3 * p, up), ay_copy(y, p, 3 * p + 1, down)]

    def ay_on(p):
        return ay_copy(down, p, 3 * p + 2, up) if p < 2 else ay_copy(up, p, 3 * p + 2, down)

    def rows_in(yy, p):
        arrived(s.ab.at[yy, near(p)], s.ayr.at[yy, near(p)])

    def spread_rows(p):
        if p:
            arrived(s.ab.at[y, near(p)], s.ar.at[near(p)])
        for copy in ay_own(p):
            copy.start()

    def pass_rows(p):
        rows_in(down if p < 2 else up, p)
        ay_on(p).start()

    def rest_of_rows():
        for p in range(RING):
            rows_in(up if p < 2 else down, p)

    def far_rows():
        for p in range(RING):
            rows_in(far, p)

    for p in (1, 2, 3):
        a_copy(p).start()
    spread_rows(0)
    s.sl[z] = jnp.broadcast_to(to_row(picked(s.lf)), (8, HD))

    def x_copy(d):
        zz = lax.rem(z + d, RING)
        return send(s.sx, s.xb.at[z], s.xs.at[d], s.xr.at[z], across(zz))

    def pass_query():
        for d in (1, 2, 3):
            yy = lax.rem(y + d, RING)
            arrived(s.sb.at[yy], s.br.at[yy])
        total = s.sb[0].astype(F32)
        for yy in (1, 2, 3):
            total = total + s.sb[yy].astype(F32)
        s.sx[...] = total.astype(BF16)
        for d in range(RING):
            x_copy(d).start()

    def h_copies(d):
        zz = lax.rem(z + d, RING)
        copies = [
            send(s.hos, s.ho.at[z], s.hs.at[d], s.hr.at[z], across(zz)),
            send(s.hls, s.hl.at[z], s.hls_s.at[d], s.hlr.at[z], across(zz)),
        ]
        if d:
            copies.append(send(s.sl.at[z], s.sl.at[z], s.sls.at[d], s.slr.at[z], at_z(zz)))
        return copies

    def answer():
        for zz in range(RING):
            arrived(s.xb.at[zz], s.xr.at[zz])
        query = s.xb[0].astype(F32)
        for zz in (1, 2, 3):
            query = query + s.xb[zz].astype(F32)
        span = pl.ds(PRE, SPAN)
        scores = dot_nn(query.astype(BF16), s.kb[y, 0:HD, span]) * SCALE
        top = jnp.max(scores, axis=1, keepdims=True)
        weights = jnp.exp2(scores - top)
        total = jnp.sum(weights, axis=1, keepdims=True)
        s.hos[...] = (dot_nn(weights.astype(BF16), s.vb[y, span, :]) / total).astype(BF16)
        level = jnp.broadcast_to(top + log2(total), (QROWS, HD))
        s.hls[...] = jnp.broadcast_to(to_row(level), (8, HD))
        for d in range(RING):
            for copy in h_copies(d):
                copy.start()

    def h2_copies(d):
        yy = lax.rem(y + d, RING)
        return [
            send(s.ho2.at[y], s.ho2.at[y], s.h2s.at[d], s.h2r.at[y], at_y(yy)),
            send(s.hl2.at[y], s.hl2.at[y], s.hl2s.at[d], s.hl2r.at[y], at_y(yy)),
        ]

    def combine_z():
        for zz in range(RING):
            arrived(s.ho.at[zz], s.hr.at[zz])
            arrived(s.hl.at[zz], s.hlr.at[zz])
        for d in (1, 2, 3):
            zz = lax.rem(z + d, RING)
            arrived(s.sl.at[zz], s.slr.at[zz])
        out, level = merge([(s.ho[zz].astype(F32), to_column(s.hl[zz, 0:1, :], QROWS)) for zz in range(RING)])
        s.ho2[y] = out.astype(BF16)
        s.hl2[y, 0:8, :] = jnp.broadcast_to(to_row(jnp.broadcast_to(level, (QROWS, HD))), (8, HD))
        s.hl2[y, 8:16, :] = s.sl[0] + s.sl[1] + s.sl[2] + s.sl[3]
        for d in (1, 2, 3):
            for copy in h2_copies(d):
                copy.start()

    def combine_y():
        for d in (1, 2, 3):
            yy = lax.rem(y + d, RING)
            arrived(s.ho2.at[yy], s.h2r.at[yy])
            arrived(s.hl2.at[yy], s.hl2r.at[yy])
        out, level = merge([(s.ho2[yy].astype(F32), to_column(s.hl2[yy, 0:1, :], QROWS)) for yy in range(RING)])
        rows = s.hl2[0, 8:9, :] + s.hl2[1, 8:9, :] + s.hl2[2, 8:9, :] + s.hl2[3, 8:9, :]
        before = to_column(rows, QROWS)
        top = jnp.maximum(before, level)
        w_own, w_span = jnp.exp2(before - top), jnp.exp2(level - top)
        total = w_own + w_span
        keep = jnp.broadcast_to(w_own / total, (QROWS, HD))
        added = out * (w_span / total)
        for at in range(2):
            s.wt[pl.ds(at * QROWS, QROWS), :] = keep
            s.ot[pl.ds(at * QROWS, QROWS), :] = added

    def si_copy(j):
        return send(s.so.at[j], s.si.at[j], s.sis.at[j], s.sir.at[j], sibling)

    def project(j):
        yc = turned(j)
        count = RING * ROWS * STEPS
        row = yc * (RING * ROWS) + lax.shift_right_logical(iota((count, HD), 0), 2)
        hit = row == prow[0]
        for h in range(GQ):
            block = jnp.concatenate([s.ab[yc, zz, h] for zz in range(RING)], axis=0).astype(F32)
            keep = s.wt[pl.ds(h, 2 * STEPS, stride=GQ), :]
            added = s.ot[pl.ds(h, 2 * STEPS, stride=GQ), :]
            keep = jnp.concatenate([keep] * (count // (2 * STEPS)), axis=0)
            added = jnp.concatenate([added] * (count // (2 * STEPS)), axis=0)
            block = jnp.where(hit, block * keep + added, block)
            s.am[:, h * HD : (h + 1) * HD] = block.astype(BF16)
        s.pr[...] = dot_nn(s.am[...], s.wb[...])
        s.pm[j] = s.pr[pl.ds(pl.multiple_of(core * 128, 128), 128), :]
        s.so[j] = s.pr[pl.ds(pl.multiple_of((1 - core) * 128, 128), 128), :].astype(BF16)
        si_copy(j).start()

    def xi_copy(j):
        return send(s.xo.at[j], s.xi.at[x], s.xis.at[j], s.xir.at[x], at_x(turned(j)))

    def join(j):
        arrived(s.si.at[j], s.sir.at[j])
        total = s.pm[j] + s.si[j].astype(F32)

        @pl.when(turned(j) == x)
        def _():
            s.own[...] = total

        @pl.when(turned(j) != x)
        def _():
            s.xo[j] = total.astype(BF16)
            xi_copy(j).start()

    count = BLOCK // SPAN
    first_lane = jnp.where(iota((BLOCK, HD), 1) == 0, 1.0, 0.0).astype(BF16)
    ones = jnp.ones((KEYS, HD), BF16)

    def scores_of(at, b, held, peak):
        p, yc = lookup(PIECES, at), turned(lookup(CHUNKS, at))
        zq = near(p)
        late = (y * RING + zq) * SPAN - (yc * RING + z) * SPAN
        shape = (SPAN, SPAN)
        ahead = jnp.where(iota(shape, 1) - iota(shape, 0) <= late, 0.0, MASKED)
        ahead = jnp.concatenate([ahead] * count, axis=0)
        queries = jnp.concatenate([s.qb[zq, b * BLOCK : (b + 1) * BLOCK, :], first_lane], axis=1)
        scores = dot_nn(queries, s.kb[yc])
        highest = None
        for k in range(KEYS // HD):
            cols = slice(k * HD, (k + 1) * HD)
            part = scores[:, cols] * SCALE
            if k == PRE // HD:
                part = part + ahead
            held[:, cols] = part
            highest = part if highest is None else jnp.maximum(highest, part)
        peak[...] = jnp.broadcast_to(jnp.max(highest, axis=1, keepdims=True), (BLOCK, HD))

    def weigh(at, b, held, peak):
        p, yc = lookup(PIECES, at), turned(lookup(CHUNKS, at))
        rows = slice(b * BLOCK, (b + 1) * BLOCK)
        before = s.top[p, rows, :]
        after = jnp.maximum(before, peak[...])
        keep = jnp.exp2(before - after)
        packed = []
        for k in range(KEYS // HD):
            packed.append(jnp.exp2(held[:, k * HD : (k + 1) * HD] - after).astype(BF16))
        mixed = dot_nn(jnp.concatenate(packed, axis=1), jnp.concatenate([s.vb[yc], ones], axis=1))
        s.top[p, rows, :] = after
        s.tot[p, rows, :] = s.tot[p, rows, :] * keep + mixed[:, HD:]
        s.acc[p, rows, :] = s.acc[p, rows, :] * keep + mixed[:, :HD]

    def o_copies(p):
        return [
            send(s.os.at[p], s.orb.at[p], s.ops.at[p], s.opr.at[p], at_z(near(p))),
            send(s.ls.at[p], s.lrb.at[p], s.lps.at[p], s.lpr.at[p], at_z(near(p))),
        ]

    def each_head(one):
        def some(i, carry):
            for u in range(4):
                one(i * 4 + u)
            return carry

        lax.fori_loop(0, GQ // 4, some, 0)

    def ship(p):
        def one(h):
            rows = pl.ds(pl.multiple_of(h * SPAN, SPAN), SPAN)
            total = s.tot[p, rows, :]
            s.os[p, h] = (s.acc[p, rows, :] / total).astype(BF16)
            s.ls[p, pl.ds(h, 1), :] = to_row(s.top[p, rows, :] + log2(total))

        each_head(one)
        for copy in o_copies(p):
            copy.start()

    def settle():
        def one(h):
            rows = pl.ds(pl.multiple_of(h * SPAN, SPAN), SPAN)
            levels = [to_column(s.lrb[p, pl.ds(h, 1), :], SPAN) for p in (1, 2, 3)]
            top = s.top[0, rows, :]
            for level in levels:
                top = jnp.maximum(top, level)
            weight = jnp.exp2(s.top[0, rows, :] - top)
            total = s.tot[0, rows, :] * weight
            mixed = s.acc[0, rows, :] * weight
            for p, level in zip((1, 2, 3), levels):
                weight = jnp.exp2(level - top)
                total = total + weight
                mixed = mixed + s.orb[p, h].astype(F32) * weight
            out_p[:, pl.ds(pl.multiple_of(h * HD, HD), HD)] = (mixed / total).astype(BF16)

        each_head(one)

    def keys_near():
        arrived(keys_of(down), s.kr.at[down])
        kv_on[0].start()
        arrived(s.vb.at[up], s.vr.at[up])
        kv_on[1].start()
        arrived(s.vb.at[down], s.vr.at[down])
        arrived(keys_of(up), s.kr.at[up])

    def keys_far():
        arrived(keys_of(far), s.kr.at[far])
        arrived(s.vb.at[far], s.vr.at[far])

    def second_queries():
        q_wait(2)
        q_start(q_third)

    actions = {
        0: [pass_query],
        1: [second_queries, keys_near],
        2: [answer],
        3: [lambda: spread_rows(1)],
        4: [keys_far, lambda: pass_rows(0)],
        5: [lambda: q_wait(3), lambda: spread_rows(2)],
        6: [combine_z, lambda: pass_rows(1)],
        7: [lambda: spread_rows(3)],
        8: [combine_y, lambda: pass_rows(2)],
        9: [lambda: pass_rows(3)],
        11: [rest_of_rows],
        13: [far_rows],
    }

    def prepare(i):
        for at, todo in actions.items():

            @pl.when(i == at)
            def _(todo=todo):
                for action in todo:
                    action()

        @pl.when((i == 10) | ((i >= 12) & (i < 15)))
        def _():
            join(jnp.maximum(i - 11, 0))

        @pl.when((i == 9) | ((i >= 11) & (i < 14)))
        def _():
            project(jnp.maximum(i - 10, 0))

    def step(i, carry):
        scores_of(i, 1, s.ts1, s.mx1)
        weigh(i, 0, s.ts0, s.mx0)
        prepare(i + 1)
        scores_of(jnp.minimum(i + 1, 15), 0, s.ts0, s.mx0)
        weigh(i, 1, s.ts1, s.mx1)
        p, k = lookup(PIECES, i), lookup(CHUNKS, i)

        @pl.when((k == 3) & (p > 0))
        def _():
            ship(p)

        return carry

    for action in actions.pop(0):
        action()
    scores_of(0, 0, s.ts0, s.mx0)
    lax.fori_loop(0, 16, step, 0)
    for p in (1, 2, 3):
        arrived(s.orb.at[p], s.opr.at[p])
        arrived(s.lrb.at[p], s.lpr.at[p])
    settle()

    total = s.own[...]
    for d in (1, 2, 3):
        xx = lax.rem(x + d, RING)
        arrived(s.xi.at[xx], s.xir.at[xx])
        total = total + s.xi[xx].astype(F32)
    for r in range(32):
        out_d[r] = total[r * STEPS : (r + 1) * STEPS, :].astype(BF16)

    for copy in kv_own + kv_on + [c for p in range(RING) for c in ay_own(p) + [ay_on(p)]]:
        copy.wait_send()
    for when, source, step_z, sem in q_first + q_second + q_third:

        @pl.when(when)
        def _(source=source, step_z=step_z, sem=sem):
            q_copy(source, step_z, sem).wait_send()

    for d in range(RING):
        x_copy(d).wait_send()
        for copy in h_copies(d):
            copy.wait_send()
        if d:
            b_copy(d).wait_send()
            a_copy(d).wait_send()
            for copy in h2_copies(d):
                copy.wait_send()
            for copy in o_copies(d):
                copy.wait_send()
    for j in range(RING):
        si_copy(j).wait_send()

        @pl.when(turned(j) != x)
        def _(j=j):
            xi_copy(j).wait_send()


def shards(span_q, span_kv, prefix_kv, prefix_len, dec_q, dec_new_kv, dec_cache, cache_len, prompt_row, out_weight):
    vmem = pl.BlockSpec(memory_space=pltpu.VMEM)
    smem = pl.BlockSpec(memory_space=pltpu.SMEM)
    hbm = pl.BlockSpec(memory_space=pltpu.HBM)
    prefill, decode = pl.pallas_call(
        kernel,
        out_shape=(
            jax.ShapeDtypeStruct((SPAN, GQ * HD), BF16),
            jax.ShapeDtypeStruct((32, STEPS, COLS), BF16),
        ),
        in_specs=[smem] * 2 + [hbm] * 8,
        out_specs=(vmem, vmem),
        scratch_shapes=list(SCRATCH.values()),
        compiler_params=pltpu.CompilerParams(
            collective_id=0, has_side_effects=True, vmem_limit_bytes=VMEM_BYTES
        ),
        cost_estimate=pl.CostEstimate(flops=11_000_000_000, bytes_accessed=8_000_000, transcendentals=17_000_000),
    )(
        prefix_len,
        prompt_row,
        *[
            pltpu.with_memory_space_constraint(operand, pltpu.HBM)
            for operand in (
                cache_len,
                span_q[0],
                span_kv[0],
                prefix_kv[0],
                dec_q[0],
                dec_new_kv[0],
                dec_cache[0],
                out_weight,
            )
        ],
    )
    return prefill[None], decode[None]


def solution(mesh):
    placed = (
        P("grp", "ctx", "head"),
        P("grp", None, "ctx", "head"),
        P("grp", None, "ctx", "head"),
        P("grp"),
        P("grp", "ctx", None, "head"),
        P("grp", None, "ctx", None, "head"),
        P("grp", None, "ctx", None, "head"),
        P("grp", "ctx"),
        P("grp"),
        P("head", "ctx"),
    )
    return jax.shard_map(
        shards,
        mesh=mesh,
        in_specs=placed,
        out_specs=(P("grp", "ctx", "head"), P("grp", "head", None, "ctx")),
        check_vma=False,
    )
```

```python
import math

import jax
import jax.numpy as jnp
from jax import lax
from jax.experimental import pallas as pl
from jax.experimental.pallas import tpu as pltpu
from jax.sharding import PartitionSpec as P

HD = 128
GQ = 8
RING = 4
PRE = 896
SPAN = 128
KEYS = PRE + SPAN
ROWS = 16
STEPS = 4
SLOTS = 512
QROWS = STEPS * GQ
COLS = 512
MASKED = -1e30
LOG2E = math.log2(math.e)
SCALE = LOG2E / math.sqrt(HD)
MESH = pl.DeviceIdType.MESH
F32 = jnp.float32
BF16 = jnp.bfloat16
BLOCK = 512
VMEM_BYTES = 40 * 1024 * 1024

PIECES = (0, 2, 2, 2, 2, 3, 3, 3, 3, 1, 1, 1, 1, 0, 0, 0)
CHUNKS = (0, 0, 1, 2, 3, 0, 1, 2, 3, 0, 1, 2, 3, 1, 2, 3)


def dot_nt(a, b):
    return lax.dot_general(a, b, (((1,), (1,)), ((), ())), preferred_element_type=F32)


def dot_nn(a, b):
    return lax.dot_general(a, b, (((1,), (0,)), ((), ())), preferred_element_type=F32)


def log2(v):
    return jnp.log(v) * LOG2E


def iota(shape, axis):
    return lax.broadcasted_iota(jnp.int32, shape, axis)


def lookup(table, index):
    value = jnp.int32(table[0])
    for at, entry in enumerate(table[1:], 1):
        value = jnp.where(index == at, jnp.int32(entry), value)
    return value


def to_row(column):
    shape = column.shape
    return jnp.sum(jnp.where(iota(shape, 0) == iota(shape, 1), column, 0.0), axis=0, keepdims=True)


def to_column(row, count):
    shape = (count, HD)
    spread = jnp.broadcast_to(row, shape)
    return jnp.sum(jnp.where(iota(shape, 0) == iota(shape, 1), spread, 0.0), axis=1, keepdims=True)


def merge(parts):
    top = parts[0][1]
    for _, level in parts[1:]:
        top = jnp.maximum(top, level)
    weights = [jnp.exp2(level - top) for _, level in parts]
    total = weights[0]
    for w in weights[1:]:
        total = total + w
    mixed = parts[0][0] * weights[0]
    for (out, _), w in zip(parts[1:], weights[1:]):
        mixed = mixed + out * w
    return mixed / total, top + log2(total)


SCRATCH = {
    "kl": pltpu.VMEM((KEYS, HD), BF16),
    "kb": pltpu.VMEM((RING, 2 * HD, KEYS), BF16),
    "vb": pltpu.VMEM((RING, KEYS, HD), BF16),
    "qb": pltpu.VMEM((RING, GQ * SPAN, HD), BF16),
    "ts0": pltpu.VMEM((BLOCK, KEYS), F32),
    "ts1": pltpu.VMEM((BLOCK, KEYS), F32),
    "kp0": pltpu.VMEM((BLOCK, HD), F32),
    "kp1": pltpu.VMEM((BLOCK, HD), F32),
    "pk0": pltpu.VMEM((BLOCK, KEYS), BF16),
    "pk1": pltpu.VMEM((BLOCK, KEYS), BF16),
    "dq": pltpu.VMEM((ROWS, STEPS, GQ * HD), BF16),
    "nkv": pltpu.VMEM((2, ROWS, STEPS, HD), BF16),
    "acc": pltpu.VMEM((RING, GQ * SPAN, HD), F32),
    "top": pltpu.VMEM((RING, GQ * SPAN, HD), F32),
    "tot": pltpu.VMEM((RING, GQ * SPAN, HD), F32),
    "os": pltpu.VMEM((RING, GQ, SPAN, HD), BF16),
    "ls": pltpu.VMEM((RING, GQ, SPAN), F32),
    "orb": pltpu.VMEM((RING, GQ, SPAN, HD), BF16),
    "lrb": pltpu.VMEM((RING, GQ, SPAN), F32),
    "ck": pltpu.VMEM((ROWS, SLOTS, HD), BF16),
    "cv": pltpu.VMEM((ROWS, SLOTS, HD), BF16),
    "wb": pltpu.VMEM((GQ * HD, COLS), BF16),
    "qf": pltpu.VMEM((ROWS * QROWS, HD), F32),
    "kn": pltpu.VMEM((HD, HD), F32),
    "vn": pltpu.VMEM((HD, HD), F32),
    "of": pltpu.VMEM((ROWS * QROWS, HD), F32),
    "mf": pltpu.VMEM((ROWS * QROWS, HD), F32),
    "lf": pltpu.VMEM((ROWS * QROWS, HD), F32),
    "sb": pltpu.VMEM((RING, QROWS, HD), BF16),
    "sx": pltpu.VMEM((QROWS, HD), BF16),
    "xb": pltpu.VMEM((RING, QROWS, HD), BF16),
    "hos": pltpu.VMEM((QROWS, HD), BF16),
    "hls": pltpu.VMEM((8, HD), F32),
    "ho": pltpu.VMEM((RING, QROWS, HD), BF16),
    "hl": pltpu.VMEM((RING, 8, HD), F32),
    "sl": pltpu.VMEM((RING, 8, HD), F32),
    "ho2": pltpu.VMEM((RING, QROWS, HD), BF16),
    "hl2": pltpu.VMEM((RING, 16, HD), F32),
    "wt": pltpu.VMEM((2 * QROWS, HD), F32),
    "ot": pltpu.VMEM((2 * QROWS, HD), F32),
    "ab": pltpu.VMEM((RING, RING, GQ, ROWS * STEPS, HD), BF16),
    "am": pltpu.VMEM((RING * ROWS * STEPS, GQ * HD), BF16),
    "pr": pltpu.VMEM((RING * ROWS * STEPS, COLS), F32),
    "pm": pltpu.VMEM((RING, 128, COLS), F32),
    "so": pltpu.VMEM((RING, 128, COLS), BF16),
    "si": pltpu.VMEM((RING, 128, COLS), BF16),
    "xo": pltpu.VMEM((RING, 128, COLS), BF16),
    "xi": pltpu.VMEM((RING, 128, COLS), BF16),
    "own": pltpu.VMEM((128, COLS), F32),
    "clen": pltpu.SMEM((1, ROWS), jnp.int32),
    "loc": pltpu.SemaphoreType.DMA((18,)),
    "kvs": pltpu.SemaphoreType.DMA((6,)),
    "kr": pltpu.SemaphoreType.DMA((RING,)),
    "vr": pltpu.SemaphoreType.DMA((RING,)),
    "qs": pltpu.SemaphoreType.DMA((6,)),
    "qr": pltpu.SemaphoreType.DMA((RING,)),
    "bs": pltpu.SemaphoreType.DMA((RING,)),
    "br": pltpu.SemaphoreType.DMA((RING,)),
    "xs": pltpu.SemaphoreType.DMA((RING,)),
    "xr": pltpu.SemaphoreType.DMA((RING,)),
    "hs": pltpu.SemaphoreType.DMA((RING,)),
    "hr": pltpu.SemaphoreType.DMA((RING,)),
    "hls_s": pltpu.SemaphoreType.DMA((RING,)),
    "hlr": pltpu.SemaphoreType.DMA((RING,)),
    "sls": pltpu.SemaphoreType.DMA((RING,)),
    "slr": pltpu.SemaphoreType.DMA((RING,)),
    "h2s": pltpu.SemaphoreType.DMA((RING,)),
    "h2r": pltpu.SemaphoreType.DMA((RING,)),
    "hl2s": pltpu.SemaphoreType.DMA((RING,)),
    "hl2r": pltpu.SemaphoreType.DMA((RING,)),
    "as_": pltpu.SemaphoreType.DMA((RING,)),
    "ar": pltpu.SemaphoreType.DMA((RING,)),
    "ays": pltpu.SemaphoreType.DMA((3 * RING,)),
    "ayr": pltpu.SemaphoreType.DMA((RING, RING)),
    "ops": pltpu.SemaphoreType.DMA((RING,)),
    "opr": pltpu.SemaphoreType.DMA((RING,)),
    "lps": pltpu.SemaphoreType.DMA((RING,)),
    "lpr": pltpu.SemaphoreType.DMA((RING,)),
    "sis": pltpu.SemaphoreType.DMA((RING,)),
    "sir": pltpu.SemaphoreType.DMA((RING,)),
    "xis": pltpu.SemaphoreType.DMA((RING,)),
    "xir": pltpu.SemaphoreType.DMA((RING,)),
}


class Names:
    pass


def kernel(plen, prow, clen_in, q_in, skv, pkv, dq, nkv, cache, w_in, out_p, out_d, *scratch):
    s = Names()
    for name, ref in zip(SCRATCH, scratch):
        setattr(s, name, ref)

    me = lax.axis_index("ctx")
    y, z = lax.div(me, RING), lax.rem(me, RING)
    head = lax.axis_index("head")
    x, core = lax.div(head, 2), lax.rem(head, 2)
    other = 1 - lax.axis_index("grp")

    def turned(j):
        return lax.rem(y + lax.div(j * (j + 1), 2), RING)

    def near(p):
        high = lax.rem(lax.div(z, 2) + lax.div(p, 2), 2)
        return 2 * high + lax.rem(z + p, 2)

    up, down, far = lax.rem(y + 1, RING), lax.rem(y + 3, RING), lax.rem(y + 2, RING)

    def at_y(yy):
        return {"ctx": yy * RING + z}

    def at_z(zz):
        return {"ctx": y * RING + zz}

    def across(zz):
        return {"ctx": y * RING + zz, "grp": other}

    def at_x(xx):
        return {"head": xx * 2 + core}

    sibling = {"head": x * 2 + 1 - core}

    def send(src, dst, ssem, rsem, device):
        return pltpu.make_async_remote_copy(
            src_ref=src, dst_ref=dst, send_sem=ssem, recv_sem=rsem, device_id=device, device_id_type=MESH
        )

    def arrived(dst, rsem):
        send(dst, dst, s.loc.at[0], rsem, sibling).wait_recv()

    pairs = [
        (pkv.at[0], s.kl.at[pl.ds(0, PRE)]),
        (skv.at[0], s.kl.at[pl.ds(PRE, SPAN)]),
        (pkv.at[1], s.vb.at[y, pl.ds(0, PRE)]),
        (skv.at[1], s.vb.at[y, pl.ds(PRE, SPAN)]),
    ]
    pairs += [(q_in.at[:, pl.ds(h * HD, HD)], s.qb.at[z, pl.ds(h * SPAN, SPAN)]) for h in range(GQ)]
    pairs += [(dq, s.dq), (nkv, s.nkv), (clen_in, s.clen), (cache.at[0], s.ck), (cache.at[1], s.cv), (w_in, s.wb)]
    loads = [pltpu.make_async_copy(src, dst, s.loc.at[at]) for at, (src, dst) in enumerate(pairs)]
    for load in loads:
        load.start()

    barrier = pltpu.get_barrier_semaphore()
    greeted = [at_y(lax.rem(y + d, RING)) for d in (1, 2, 3)] + [at_z(lax.rem(z + d, RING)) for d in (1, 2, 3)]
    greeted += [across(zz) for zz in range(RING)] + [sibling] + [at_x(lax.rem(x + d, RING)) for d in (1, 2, 3)]
    for device in greeted:
        pl.semaphore_signal(barrier, inc=1, device_id=device, device_id_type=MESH)

    def clear(p, carry):
        s.acc[p] = jnp.zeros((GQ * SPAN, HD), F32)
        s.tot[p] = jnp.zeros((GQ * SPAN, HD), F32)
        s.top[p] = jnp.full((GQ * SPAN, HD), MASKED, F32)
        slot = iota((HD, KEYS), 1)
        unused = ((p * RING + z) * PRE + slot >= plen[0]) & (slot < PRE) & (iota((HD, KEYS), 0) == 0)
        s.kb[p, HD : 2 * HD, :] = jnp.where(unused, MASKED, 0.0).astype(BF16)
        return carry

    lax.fori_loop(0, RING, clear, 0)


    for load in loads[2:12]:
        load.wait()
    pl.semaphore_wait(barrier, len(greeted))

    def keys_of(yy):
        return s.kb.at[yy, pl.ds(0, HD)]

    kv_own = [
        send(s.vb.at[y], s.vb.at[y], s.kvs.at[0], s.vr.at[y], at_y(up)),
        send(s.vb.at[y], s.vb.at[y], s.kvs.at[1], s.vr.at[y], at_y(down)),
        send(keys_of(y), keys_of(y), s.kvs.at[2], s.kr.at[y], at_y(up)),
        send(keys_of(y), keys_of(y), s.kvs.at[3], s.kr.at[y], at_y(down)),
    ]
    kv_on = [
        send(keys_of(down), keys_of(down), s.kvs.at[4], s.kr.at[down], at_y(up)),
        send(s.vb.at[up], s.vb.at[up], s.kvs.at[5], s.vr.at[up], at_y(down)),
    ]

    def q_copy(source, step, sem):
        return send(s.qb.at[source], s.qb.at[source], s.qs.at[sem], s.qr.at[source], at_z(z + step))

    q_first = [(z < 3, z, 1, 0), (z > 0, z, -1, 1)]
    q_second = [((z > 0) & (z < 3), z - 1, 1, 2), ((z > 0) & (z < 3), z + 1, -1, 3)]
    q_third = [(z == 2, z - 2, 1, 4), (z == 1, z + 2, -1, 5)]

    def q_start(group):
        for when, source, step, sem in group:

            @pl.when(when)
            def _(source=source, step=step, sem=sem):
                q_copy(source, step, sem).start()

    def q_wait(distance):
        @pl.when(z >= distance)
        def _():
            arrived(s.qb.at[z - distance], s.qr.at[z - distance])

        @pl.when(z + distance < RING)
        def _():
            arrived(s.qb.at[z + distance], s.qr.at[z + distance])

    def b_copy(d):
        return send(s.sb.at[y], s.sb.at[y], s.bs.at[d], s.br.at[y], at_y(lax.rem(y + d, RING)))

    for copy in kv_own[:2]:
        copy.start()
    q_start(q_first)
    for load in loads[:2]:
        load.wait()
    s.kb[y, 0:HD, :] = s.kl[...].T
    for copy in kv_own[2:]:
        copy.start()

    for load in loads[12:15]:
        load.wait()
    for r in range(ROWS):
        row = s.dq[r].astype(F32)
        for h in range(GQ):
            s.qf[pl.ds(r * QROWS + h, STEPS, stride=GQ), :] = row[:, h * HD : (h + 1) * HD]
    s.kn[...] = jnp.zeros((HD, HD), F32)
    s.vn[...] = jnp.zeros((HD, HD), F32)
    for r in range(ROWS):
        s.kn[pl.ds(r * STEPS, STEPS), :] = s.nkv[0, r].astype(F32)
        s.vn[pl.ds(r * STEPS, STEPS), :] = s.nkv[1, r].astype(F32)

    def picked(ref):
        total = jnp.zeros((QROWS, HD), F32)
        for r in range(ROWS):
            mine = jnp.where(me * ROWS + r == prow[0], 1.0, 0.0)
            total = total + mine * ref[r * QROWS : (r + 1) * QROWS, :]
        return total

    s.sb[y] = picked(s.qf).astype(BF16)

    for d in (1, 2, 3):
        b_copy(d).start()

    lanes = (ROWS * QROWS, HD)
    at_row, at_key = iota(lanes, 0), iota(lanes, 1)
    same = lax.shift_right_logical(at_row, 5) == lax.shift_right_logical(at_key, 2)
    early = jnp.bitwise_and(at_key, 3) <= jnp.bitwise_and(lax.shift_right_logical(at_row, 3), 3)
    new = jnp.where(same & early, dot_nt(s.qf[...].astype(BF16), s.kn[...].astype(BF16)) * SCALE, MASKED)
    new_top = jnp.max(new, axis=1, keepdims=True)
    new_weights = jnp.exp2(new - new_top)
    s.mf[...] = jnp.broadcast_to(new_top, lanes)
    s.lf[...] = jnp.broadcast_to(jnp.sum(new_weights, axis=1, keepdims=True), lanes)
    s.of[...] = dot_nn(new_weights.astype(BF16), s.vn[...].astype(BF16))

    for load in loads[15:]:
        load.wait()

    def cached(r):
        rows = pl.ds(pl.multiple_of(r * QROWS, QROWS), QROWS)
        scores = dot_nt(s.qf[rows, :].astype(BF16), s.ck[r]) * SCALE
        scores = jnp.where(iota((QROWS, SLOTS), 1) < s.clen[0, r], scores, MASKED)
        before = s.mf[rows, :]
        after = jnp.maximum(before, jnp.max(scores, axis=1, keepdims=True))
        weights = jnp.exp2(scores - after[:, :1])
        keep = jnp.exp2(before - after)
        total = s.lf[rows, :] * keep + jnp.sum(weights, axis=1, keepdims=True)
        mixed = s.of[rows, :] * keep + dot_nn(weights.astype(BF16), s.cv[r])
        s.of[rows, :] = mixed / total
        s.lf[rows, :] = after + log2(total)

    def first_queries():
        q_wait(1)
        q_start(q_second)

    def some_rows(i, carry):
        @pl.when(i == 1)
        def _():
            first_queries()

        for u in range(8):
            cached(i * 8 + u)
        return carry

    lax.fori_loop(0, ROWS // 8, some_rows, 0)
    for h in range(GQ):
        s.ab[y, z, h] = s.of[pl.ds(h, ROWS * STEPS, stride=GQ), :].astype(BF16)

    def a_copy(p):
        return send(s.ab.at[y, z], s.ab.at[y, z], s.as_.at[p], s.ar.at[z], at_z(near(p)))

    def ay_copy(yy, p, sem, to):
        block = s.ab.at[yy, near(p)]
        return send(block, block, s.ays.at[sem], s.ayr.at[yy, near(p)], at_y(to))

    def ay_own(p):
        return [ay_copy(y, p, 3 * p, up), ay_copy(y, p, 3 * p + 1, down)]

    def ay_on(p):
        return ay_copy(down, p, 3 * p + 2, up) if p < 2 else ay_copy(up, p, 3 * p + 2, down)

    def rows_in(yy, p):
        arrived(s.ab.at[yy, near(p)], s.ayr.at[yy, near(p)])

    def spread_rows(p):
        if p:
            arrived(s.ab.at[y, near(p)], s.ar.at[near(p)])
        for copy in ay_own(p):
            copy.start()

    def pass_rows(p):
        rows_in(down if p < 2 else up, p)
        ay_on(p).start()

    def rest_of_rows():
        for p in range(RING):
            rows_in(up if p < 2 else down, p)

    def far_rows():
        for p in range(RING):
            rows_in(far, p)

    for p in (1, 2, 3):
        a_copy(p).start()
    spread_rows(0)
    s.sl[z] = jnp.broadcast_to(to_row(picked(s.lf)), (8, HD))

    def x_copy(d):
        zz = lax.rem(z + d, RING)
        return send(s.sx, s.xb.at[z], s.xs.at[d], s.xr.at[z], across(zz))

    def pass_query():
        for d in (1, 2, 3):
            yy = lax.rem(y + d, RING)
            arrived(s.sb.at[yy], s.br.at[yy])
        total = s.sb[0].astype(F32)
        for yy in (1, 2, 3):
            total = total + s.sb[yy].astype(F32)
        s.sx[...] = total.astype(BF16)
        for d in range(RING):
            x_copy(d).start()

    def h_copies(d):
        zz = lax.rem(z + d, RING)
        copies = [
            send(s.hos, s.ho.at[z], s.hs.at[d], s.hr.at[z], across(zz)),
            send(s.hls, s.hl.at[z], s.hls_s.at[d], s.hlr.at[z], across(zz)),
        ]
        if d:
            copies.append(send(s.sl.at[z], s.sl.at[z], s.sls.at[d], s.slr.at[z], at_z(zz)))
        return copies

    def answer():
        for zz in range(RING):
            arrived(s.xb.at[zz], s.xr.at[zz])
        query = s.xb[0].astype(F32)
        for zz in (1, 2, 3):
            query = query + s.xb[zz].astype(F32)
        span = pl.ds(PRE, SPAN)
        scores = dot_nn(query.astype(BF16), s.kb[y, 0:HD, span]) * SCALE
        top = jnp.max(scores, axis=1, keepdims=True)
        weights = jnp.exp2(scores - top)
        total = jnp.sum(weights, axis=1, keepdims=True)
        s.hos[...] = (dot_nn(weights.astype(BF16), s.vb[y, span, :]) / total).astype(BF16)
        level = jnp.broadcast_to(top + log2(total), (QROWS, HD))
        s.hls[...] = jnp.broadcast_to(to_row(level), (8, HD))
        for d in range(RING):
            for copy in h_copies(d):
                copy.start()

    def h2_copies(d):
        yy = lax.rem(y + d, RING)
        return [
            send(s.ho2.at[y], s.ho2.at[y], s.h2s.at[d], s.h2r.at[y], at_y(yy)),
            send(s.hl2.at[y], s.hl2.at[y], s.hl2s.at[d], s.hl2r.at[y], at_y(yy)),
        ]

    def combine_z():
        for zz in range(RING):
            arrived(s.ho.at[zz], s.hr.at[zz])
            arrived(s.hl.at[zz], s.hlr.at[zz])
        for d in (1, 2, 3):
            zz = lax.rem(z + d, RING)
            arrived(s.sl.at[zz], s.slr.at[zz])
        out, level = merge([(s.ho[zz].astype(F32), to_column(s.hl[zz, 0:1, :], QROWS)) for zz in range(RING)])
        s.ho2[y] = out.astype(BF16)
        s.hl2[y, 0:8, :] = jnp.broadcast_to(to_row(jnp.broadcast_to(level, (QROWS, HD))), (8, HD))
        s.hl2[y, 8:16, :] = s.sl[0] + s.sl[1] + s.sl[2] + s.sl[3]
        for d in (1, 2, 3):
            for copy in h2_copies(d):
                copy.start()

    def combine_y():
        for d in (1, 2, 3):
            yy = lax.rem(y + d, RING)
            arrived(s.ho2.at[yy], s.h2r.at[yy])
            arrived(s.hl2.at[yy], s.hl2r.at[yy])
        out, level = merge([(s.ho2[yy].astype(F32), to_column(s.hl2[yy, 0:1, :], QROWS)) for yy in range(RING)])
        rows = s.hl2[0, 8:9, :] + s.hl2[1, 8:9, :] + s.hl2[2, 8:9, :] + s.hl2[3, 8:9, :]
        before = to_column(rows, QROWS)
        top = jnp.maximum(before, level)
        w_own, w_span = jnp.exp2(before - top), jnp.exp2(level - top)
        total = w_own + w_span
        keep = jnp.broadcast_to(w_own / total, (QROWS, HD))
        added = out * (w_span / total)
        for at in range(2):
            s.wt[pl.ds(at * QROWS, QROWS), :] = keep
            s.ot[pl.ds(at * QROWS, QROWS), :] = added

    def si_copy(j):
        return send(s.so.at[j], s.si.at[j], s.sis.at[j], s.sir.at[j], sibling)

    def project(j):
        yc = turned(j)
        count = RING * ROWS * STEPS
        row = yc * (RING * ROWS) + lax.shift_right_logical(iota((count, HD), 0), 2)
        hit = row == prow[0]
        for h in range(GQ):
            block = jnp.concatenate([s.ab[yc, zz, h] for zz in range(RING)], axis=0).astype(F32)
            keep = s.wt[pl.ds(h, 2 * STEPS, stride=GQ), :]
            added = s.ot[pl.ds(h, 2 * STEPS, stride=GQ), :]
            keep = jnp.concatenate([keep] * (count // (2 * STEPS)), axis=0)
            added = jnp.concatenate([added] * (count // (2 * STEPS)), axis=0)
            block = jnp.where(hit, block * keep + added, block)
            s.am[:, h * HD : (h + 1) * HD] = block.astype(BF16)
        s.pr[...] = dot_nn(s.am[...], s.wb[...])
        s.pm[j] = s.pr[pl.ds(pl.multiple_of(core * 128, 128), 128), :]
        s.so[j] = s.pr[pl.ds(pl.multiple_of((1 - core) * 128, 128), 128), :].astype(BF16)
        si_copy(j).start()

    def xi_copy(j):
        return send(s.xo.at[j], s.xi.at[x], s.xis.at[j], s.xir.at[x], at_x(turned(j)))

    def join(j):
        arrived(s.si.at[j], s.sir.at[j])
        total = s.pm[j] + s.si[j].astype(F32)

        @pl.when(turned(j) == x)
        def _():
            s.own[...] = total

        @pl.when(turned(j) != x)
        def _():
            s.xo[j] = total.astype(BF16)
            xi_copy(j).start()

    count = BLOCK // SPAN
    first_lane = jnp.where(iota((BLOCK, HD), 1) == 0, 1.0, 0.0).astype(BF16)
    ones = jnp.ones((KEYS, HD), BF16)

    def scores_of(at, b, held):
        p, yc = lookup(PIECES, at), turned(lookup(CHUNKS, at))
        zq = near(p)
        queries = jnp.concatenate([s.qb[zq, b * BLOCK : (b + 1) * BLOCK, :], first_lane], axis=1)

        def quarter(j):
            scores = dot_nn(queries, s.kb[yc, :, 2 * j * HD : 2 * (j + 1) * HD])
            for k in (2 * j, 2 * j + 1):
                part = scores[:, (k - 2 * j) * HD : (k - 2 * j + 1) * HD] * SCALE
                if k == PRE // HD:
                    late = (y * RING + zq) * SPAN - (yc * RING + z) * SPAN
                    shape = (SPAN, SPAN)
                    ahead = jnp.where(iota(shape, 1) - iota(shape, 0) <= late, 0.0, MASKED)
                    part = part + jnp.concatenate([ahead] * count, axis=0)
                held[:, k * HD : (k + 1) * HD] = part

        return quarter

    def weigh(at, b, held, keeps, packed):
        p = lookup(PIECES, at)

        def quarter(j):
            for i in range(j * SPAN, (j + 1) * SPAN, 32):
                mine = slice(i, i + 32)
                rows = slice(b * BLOCK + i, b * BLOCK + i + 32)
                tiles = [held[mine, k * HD : (k + 1) * HD] for k in range(KEYS // HD)]
                highest = tiles[0]
                for part in tiles[1:]:
                    highest = jnp.maximum(highest, part)
                before = s.top[p, rows, :]
                after = jnp.maximum(before, jnp.max(highest, axis=1, keepdims=True))
                s.top[p, rows, :] = after
                keeps[mine, :] = jnp.exp2(before - after)
                for k, part in enumerate(tiles):
                    packed[mine, k * HD : (k + 1) * HD] = jnp.exp2(part - after).astype(BF16)

        return quarter

    def mix(at, b, keeps, packed):
        p, yc = lookup(PIECES, at), turned(lookup(CHUNKS, at))

        def half_block(j):
            size = BLOCK // 2
            mine = slice(j * size, (j + 1) * size)
            rows = slice(b * BLOCK + j * size, b * BLOCK + (j + 1) * size)
            mixed = dot_nn(packed[mine, :], jnp.concatenate([s.vb[yc], ones], axis=1))
            keep = keeps[mine, :]
            s.tot[p, rows, :] = s.tot[p, rows, :] * keep + mixed[:, HD:]
            s.acc[p, rows, :] = s.acc[p, rows, :] * keep + mixed[:, :HD]

        return half_block

    def together(scores, weights, products):
        for j in range(4):
            scores(j)
            weights(j)
            if j % 2 == 0:
                products(j // 2)

    def o_copies(p):
        return [
            send(s.os.at[p], s.orb.at[p], s.ops.at[p], s.opr.at[p], at_z(near(p))),
            send(s.ls.at[p], s.lrb.at[p], s.lps.at[p], s.lpr.at[p], at_z(near(p))),
        ]

    def each_head(one):
        def some(i, carry):
            for u in range(4):
                one(i * 4 + u)
            return carry

        lax.fori_loop(0, GQ // 4, some, 0)

    def ship(p):
        def one(h):
            rows = pl.ds(pl.multiple_of(h * SPAN, SPAN), SPAN)
            total = s.tot[p, rows, :]
            s.os[p, h] = (s.acc[p, rows, :] / total).astype(BF16)
            s.ls[p, pl.ds(h, 1), :] = to_row(s.top[p, rows, :] + log2(total))

        each_head(one)
        for copy in o_copies(p):
            copy.start()

    def settle():
        def one(h):
            rows = pl.ds(pl.multiple_of(h * SPAN, SPAN), SPAN)
            levels = [to_column(s.lrb[p, pl.ds(h, 1), :], SPAN) for p in (1, 2, 3)]
            top = s.top[0, rows, :]
            for level in levels:
                top = jnp.maximum(top, level)
            weight = jnp.exp2(s.top[0, rows, :] - top)
            total = s.tot[0, rows, :] * weight
            mixed = s.acc[0, rows, :] * weight
            for p, level in zip((1, 2, 3), levels):
                weight = jnp.exp2(level - top)
                total = total + weight
                mixed = mixed + s.orb[p, h].astype(F32) * weight
            out_p[:, pl.ds(pl.multiple_of(h * HD, HD), HD)] = (mixed / total).astype(BF16)

        each_head(one)

    def keys_near():
        arrived(keys_of(down), s.kr.at[down])
        kv_on[0].start()
        arrived(s.vb.at[up], s.vr.at[up])
        kv_on[1].start()
        arrived(s.vb.at[down], s.vr.at[down])
        arrived(keys_of(up), s.kr.at[up])

    def keys_far():
        arrived(keys_of(far), s.kr.at[far])
        arrived(s.vb.at[far], s.vr.at[far])

    def second_queries():
        q_wait(2)
        q_start(q_third)

    actions = {
        0: [pass_query],
        1: [second_queries, keys_near],
        2: [answer],
        3: [lambda: spread_rows(1)],
        4: [keys_far, lambda: pass_rows(0)],
        5: [lambda: q_wait(3), lambda: spread_rows(2)],
        6: [combine_z, lambda: pass_rows(1)],
        7: [lambda: spread_rows(3)],
        8: [combine_y, lambda: pass_rows(2)],
        9: [lambda: pass_rows(3)],
        11: [rest_of_rows],
        13: [far_rows],
    }

    def prepare(i):
        for at, todo in actions.items():

            @pl.when(i == at)
            def _(todo=todo):
                for action in todo:
                    action()

        @pl.when((i == 10) | ((i >= 12) & (i < 15)))
        def _():
            join(jnp.maximum(i - 11, 0))

        @pl.when((i == 9) | ((i >= 11) & (i < 14)))
        def _():
            project(jnp.maximum(i - 10, 0))

    even = (s.ts0, s.kp0, s.pk0)
    odd = (s.ts1, s.kp1, s.pk1)

    def step(i, carry):
        last = jnp.maximum(i - 1, 0)
        together(scores_of(i, 1, odd[0]), weigh(i, 0, *even), mix(last, 1, *odd[1:]))
        p, k = lookup(PIECES, last), lookup(CHUNKS, last)

        @pl.when((k == 3) & (p > 0))
        def _():
            ship(p)

        prepare(i + 1)
        together(scores_of(jnp.minimum(i + 1, 15), 0, even[0]), weigh(i, 1, *odd), mix(i, 0, *even[1:]))
        return carry

    s.kp1[...] = jnp.ones((BLOCK, HD), F32)
    s.pk1[...] = jnp.zeros((BLOCK, KEYS), BF16)
    for action in actions.pop(0):
        action()
    first = scores_of(0, 0, s.ts0)
    for j in range(4):
        first(j)
    lax.fori_loop(0, 16, step, 0)
    rest = mix(15, 1, *odd[1:])
    for j in range(2):
        rest(j)

    for p in (1, 2, 3):
        arrived(s.orb.at[p], s.opr.at[p])
        arrived(s.lrb.at[p], s.lpr.at[p])
    settle()

    total = s.own[...]
    for d in (1, 2, 3):
        xx = lax.rem(x + d, RING)
        arrived(s.xi.at[xx], s.xir.at[xx])
        total = total + s.xi[xx].astype(F32)
    for r in range(32):
        out_d[r] = total[r * STEPS : (r + 1) * STEPS, :].astype(BF16)

    for copy in kv_own + kv_on + [c for p in range(RING) for c in ay_own(p) + [ay_on(p)]]:
        copy.wait_send()
    for when, source, step_z, sem in q_first + q_second + q_third:

        @pl.when(when)
        def _(source=source, step_z=step_z, sem=sem):
            q_copy(source, step_z, sem).wait_send()

    for d in range(RING):
        x_copy(d).wait_send()
        for copy in h_copies(d):
            copy.wait_send()
        if d:
            b_copy(d).wait_send()
            a_copy(d).wait_send()
            for copy in h2_copies(d):
                copy.wait_send()
            for copy in o_copies(d):
                copy.wait_send()
    for j in range(RING):
        si_copy(j).wait_send()

        @pl.when(turned(j) != x)
        def _(j=j):
            xi_copy(j).wait_send()


def shards(span_q, span_kv, prefix_kv, prefix_len, dec_q, dec_new_kv, dec_cache, cache_len, prompt_row, out_weight):
    vmem = pl.BlockSpec(memory_space=pltpu.VMEM)
    smem = pl.BlockSpec(memory_space=pltpu.SMEM)
    hbm = pl.BlockSpec(memory_space=pltpu.HBM)
    prefill, decode = pl.pallas_call(
        kernel,
        out_shape=(
            jax.ShapeDtypeStruct((SPAN, GQ * HD), BF16),
            jax.ShapeDtypeStruct((32, STEPS, COLS), BF16),
        ),
        in_specs=[smem] * 2 + [hbm] * 8,
        out_specs=(vmem, vmem),
        scratch_shapes=list(SCRATCH.values()),
        compiler_params=pltpu.CompilerParams(
            collective_id=0, has_side_effects=True, vmem_limit_bytes=VMEM_BYTES
        ),
        cost_estimate=pl.CostEstimate(flops=11_000_000_000, bytes_accessed=8_000_000, transcendentals=17_000_000),
    )(
        prefix_len,
        prompt_row,
        *[
            pltpu.with_memory_space_constraint(operand, pltpu.HBM)
            for operand in (
                cache_len,
                span_q[0],
                span_kv[0],
                prefix_kv[0],
                dec_q[0],
                dec_new_kv[0],
                dec_cache[0],
                out_weight,
            )
        ],
    )
    return prefill[None], decode[None]


def solution(mesh):
    placed = (
        P("grp", "ctx", "head"),
        P("grp", None, "ctx", "head"),
        P("grp", None, "ctx", "head"),
        P("grp"),
        P("grp", "ctx", None, "head"),
        P("grp", None, "ctx", None, "head"),
        P("grp", None, "ctx", None, "head"),
        P("grp", "ctx"),
        P("grp"),
        P("head", "ctx"),
    )
    return jax.shard_map(
        shards,
        mesh=mesh,
        in_specs=placed,
        out_specs=(P("grp", "ctx", "head"), P("grp", "head", None, "ctx")),
        check_vma=False,
    )
```

```python
import math

import jax
import jax.numpy as jnp
from jax import lax
from jax.experimental import pallas as pl
from jax.experimental.pallas import tpu as pltpu
from jax.sharding import PartitionSpec as P

HD = 128
GQ = 8
RING = 4
PRE = 896
SPAN = 128
KEYS = PRE + SPAN
ROWS = 16
STEPS = 4
SLOTS = 512
QROWS = STEPS * GQ
COLS = 512
MASKED = -1e30
LOG2E = math.log2(math.e)
SCALE = LOG2E / math.sqrt(HD)
MESH = pl.DeviceIdType.MESH
F32 = jnp.float32
BF16 = jnp.bfloat16
BLOCK = GQ * SPAN
VMEM_BYTES = 52 * 1024 * 1024

PIECES = (0, 2, 2, 2, 2, 3, 3, 3, 3, 1, 1, 1, 1, 0, 0, 0)
CHUNKS = (0, 0, 1, 2, 3, 0, 1, 2, 3, 0, 1, 2, 3, 1, 2, 3)


def dot_nt(a, b):
    return lax.dot_general(a, b, (((1,), (1,)), ((), ())), preferred_element_type=F32)


def dot_nn(a, b):
    return lax.dot_general(a, b, (((1,), (0,)), ((), ())), preferred_element_type=F32)


def log2(v):
    return jnp.log(v) * LOG2E


def iota(shape, axis):
    return lax.broadcasted_iota(jnp.int32, shape, axis)


def lookup(table, index):
    value = jnp.int32(table[0])
    for at, entry in enumerate(table[1:], 1):
        value = jnp.where(index == at, jnp.int32(entry), value)
    return value


def to_row(column):
    shape = column.shape
    return jnp.sum(jnp.where(iota(shape, 0) == iota(shape, 1), column, 0.0), axis=0, keepdims=True)


def to_column(row, count):
    shape = (count, HD)
    spread = jnp.broadcast_to(row, shape)
    return jnp.sum(jnp.where(iota(shape, 0) == iota(shape, 1), spread, 0.0), axis=1, keepdims=True)


def merge(parts):
    top = parts[0][1]
    for _, level in parts[1:]:
        top = jnp.maximum(top, level)
    weights = [jnp.exp2(level - top) for _, level in parts]
    total = weights[0]
    for w in weights[1:]:
        total = total + w
    mixed = parts[0][0] * weights[0]
    for (out, _), w in zip(parts[1:], weights[1:]):
        mixed = mixed + out * w
    return mixed / total, top + log2(total)


SCRATCH = {
    "kl": pltpu.VMEM((KEYS, HD), BF16),
    "kb": pltpu.VMEM((RING, 2 * HD, KEYS), BF16),
    "vb": pltpu.VMEM((RING, KEYS, HD), BF16),
    "qb": pltpu.VMEM((RING, GQ * SPAN, HD), BF16),
    "ts0": pltpu.VMEM((BLOCK, KEYS), F32),
    "ts1": pltpu.VMEM((BLOCK, KEYS), F32),
    "kp": pltpu.VMEM((BLOCK, HD), F32),
    "pk": pltpu.VMEM((BLOCK, KEYS), BF16),
    "ahead": pltpu.VMEM((SPAN, SPAN), F32),
    "dq": pltpu.VMEM((ROWS, STEPS, GQ * HD), BF16),
    "nkv": pltpu.VMEM((2, ROWS, STEPS, HD), BF16),
    "acc": pltpu.VMEM((RING, GQ * SPAN, HD), F32),
    "top": pltpu.VMEM((RING, GQ * SPAN, HD), F32),
    "tot": pltpu.VMEM((RING, GQ * SPAN, HD), F32),
    "os": pltpu.VMEM((RING, GQ, SPAN, HD), BF16),
    "ls": pltpu.VMEM((RING, GQ, SPAN), F32),
    "orb": pltpu.VMEM((RING, GQ, SPAN, HD), BF16),
    "lrb": pltpu.VMEM((RING, GQ, SPAN), F32),
    "ck": pltpu.VMEM((ROWS, SLOTS, HD), BF16),
    "cv": pltpu.VMEM((ROWS, SLOTS, HD), BF16),
    "wb": pltpu.VMEM((GQ * HD, COLS), BF16),
    "qf": pltpu.VMEM((ROWS * QROWS, HD), F32),
    "kn": pltpu.VMEM((HD, HD), F32),
    "vn": pltpu.VMEM((HD, HD), F32),
    "of": pltpu.VMEM((ROWS * QROWS, HD), F32),
    "mf": pltpu.VMEM((ROWS * QROWS, HD), F32),
    "lf": pltpu.VMEM((ROWS * QROWS, HD), F32),
    "sb": pltpu.VMEM((RING, QROWS, HD), BF16),
    "sx": pltpu.VMEM((QROWS, HD), BF16),
    "xb": pltpu.VMEM((RING, QROWS, HD), BF16),
    "hos": pltpu.VMEM((QROWS, HD), BF16),
    "hls": pltpu.VMEM((8, HD), F32),
    "ho": pltpu.VMEM((RING, QROWS, HD), BF16),
    "hl": pltpu.VMEM((RING, 8, HD), F32),
    "sl": pltpu.VMEM((RING, 8, HD), F32),
    "ho2": pltpu.VMEM((RING, QROWS, HD), BF16),
    "hl2": pltpu.VMEM((RING, 16, HD), F32),
    "wt": pltpu.VMEM((2 * QROWS, HD), F32),
    "ot": pltpu.VMEM((2 * QROWS, HD), F32),
    "ab": pltpu.VMEM((RING, RING, GQ, ROWS * STEPS, HD), BF16),
    "am": pltpu.VMEM((RING * ROWS * STEPS, GQ * HD), BF16),
    "pr": pltpu.VMEM((RING * ROWS * STEPS, COLS), F32),
    "pm": pltpu.VMEM((RING, 128, COLS), F32),
    "so": pltpu.VMEM((RING, 128, COLS), BF16),
    "si": pltpu.VMEM((RING, 128, COLS), BF16),
    "xo": pltpu.VMEM((RING, 128, COLS), BF16),
    "xi": pltpu.VMEM((RING, 128, COLS), BF16),
    "own": pltpu.VMEM((128, COLS), F32),
    "clen": pltpu.SMEM((1, ROWS), jnp.int32),
    "loc": pltpu.SemaphoreType.DMA((18,)),
    "kvs": pltpu.SemaphoreType.DMA((6,)),
    "kr": pltpu.SemaphoreType.DMA((RING,)),
    "vr": pltpu.SemaphoreType.DMA((RING,)),
    "qs": pltpu.SemaphoreType.DMA((6,)),
    "qr": pltpu.SemaphoreType.DMA((RING,)),
    "bs": pltpu.SemaphoreType.DMA((RING,)),
    "br": pltpu.SemaphoreType.DMA((RING,)),
    "xs": pltpu.SemaphoreType.DMA((RING,)),
    "xr": pltpu.SemaphoreType.DMA((RING,)),
    "hs": pltpu.SemaphoreType.DMA((RING,)),
    "hr": pltpu.SemaphoreType.DMA((RING,)),
    "hls_s": pltpu.SemaphoreType.DMA((RING,)),
    "hlr": pltpu.SemaphoreType.DMA((RING,)),
    "sls": pltpu.SemaphoreType.DMA((RING,)),
    "slr": pltpu.SemaphoreType.DMA((RING,)),
    "h2s": pltpu.SemaphoreType.DMA((RING,)),
    "h2r": pltpu.SemaphoreType.DMA((RING,)),
    "hl2s": pltpu.SemaphoreType.DMA((RING,)),
    "hl2r": pltpu.SemaphoreType.DMA((RING,)),
    "as_": pltpu.SemaphoreType.DMA((RING,)),
    "ar": pltpu.SemaphoreType.DMA((RING,)),
    "ays": pltpu.SemaphoreType.DMA((3 * RING,)),
    "ayr": pltpu.SemaphoreType.DMA((RING, RING)),
    "ops": pltpu.SemaphoreType.DMA((RING,)),
    "opr": pltpu.SemaphoreType.DMA((RING,)),
    "lps": pltpu.SemaphoreType.DMA((RING,)),
    "lpr": pltpu.SemaphoreType.DMA((RING,)),
    "sis": pltpu.SemaphoreType.DMA((RING,)),
    "sir": pltpu.SemaphoreType.DMA((RING,)),
    "xis": pltpu.SemaphoreType.DMA((RING,)),
    "xir": pltpu.SemaphoreType.DMA((RING,)),
}


class Names:
    pass


def kernel(plen, prow, clen_in, q_in, skv, pkv, dq, nkv, cache, w_in, out_p, out_d, *scratch):
    s = Names()
    for name, ref in zip(SCRATCH, scratch):
        setattr(s, name, ref)

    me = lax.axis_index("ctx")
    y, z = lax.div(me, RING), lax.rem(me, RING)
    head = lax.axis_index("head")
    x, core = lax.div(head, 2), lax.rem(head, 2)
    other = 1 - lax.axis_index("grp")

    def turned(j):
        return lax.rem(y + lax.div(j * (j + 1), 2), RING)

    def near(p):
        high = lax.rem(lax.div(z, 2) + lax.div(p, 2), 2)
        return 2 * high + lax.rem(z + p, 2)

    up, down, far = lax.rem(y + 1, RING), lax.rem(y + 3, RING), lax.rem(y + 2, RING)

    def at_y(yy):
        return {"ctx": yy * RING + z}

    def at_z(zz):
        return {"ctx": y * RING + zz}

    def across(zz):
        return {"ctx": y * RING + zz, "grp": other}

    def at_x(xx):
        return {"head": xx * 2 + core}

    sibling = {"head": x * 2 + 1 - core}

    def send(src, dst, ssem, rsem, device):
        return pltpu.make_async_remote_copy(
            src_ref=src, dst_ref=dst, send_sem=ssem, recv_sem=rsem, device_id=device, device_id_type=MESH
        )

    def arrived(dst, rsem):
        send(dst, dst, s.loc.at[0], rsem, sibling).wait_recv()

    pairs = [
        (pkv.at[0], s.kl.at[pl.ds(0, PRE)]),
        (skv.at[0], s.kl.at[pl.ds(PRE, SPAN)]),
        (pkv.at[1], s.vb.at[y, pl.ds(0, PRE)]),
        (skv.at[1], s.vb.at[y, pl.ds(PRE, SPAN)]),
    ]
    pairs += [(q_in.at[:, pl.ds(h * HD, HD)], s.qb.at[z, pl.ds(h * SPAN, SPAN)]) for h in range(GQ)]
    pairs += [(dq, s.dq), (nkv, s.nkv), (clen_in, s.clen), (cache.at[0], s.ck), (cache.at[1], s.cv), (w_in, s.wb)]
    loads = [pltpu.make_async_copy(src, dst, s.loc.at[at]) for at, (src, dst) in enumerate(pairs)]
    for load in loads:
        load.start()

    barrier = pltpu.get_barrier_semaphore()
    greeted = [at_y(lax.rem(y + d, RING)) for d in (1, 2, 3)] + [at_z(lax.rem(z + d, RING)) for d in (1, 2, 3)]
    greeted += [across(zz) for zz in range(RING)] + [sibling] + [at_x(lax.rem(x + d, RING)) for d in (1, 2, 3)]
    for device in greeted:
        pl.semaphore_signal(barrier, inc=1, device_id=device, device_id_type=MESH)

    def clear(p, carry):
        s.acc[p] = jnp.zeros((GQ * SPAN, HD), F32)
        s.tot[p] = jnp.zeros((GQ * SPAN, HD), F32)
        s.top[p] = jnp.full((GQ * SPAN, HD), MASKED, F32)
        slot = iota((HD, KEYS), 1)
        unused = ((p * RING + z) * PRE + slot >= plen[0]) & (slot < PRE) & (iota((HD, KEYS), 0) == 0)
        s.kb[p, HD : 2 * HD, :] = jnp.where(unused, MASKED, 0.0).astype(BF16)
        return carry

    lax.fori_loop(0, RING, clear, 0)


    for load in loads[2:12]:
        load.wait()
    pl.semaphore_wait(barrier, len(greeted))

    def keys_of(yy):
        return s.kb.at[yy, pl.ds(0, HD)]

    kv_own = [
        send(s.vb.at[y], s.vb.at[y], s.kvs.at[0], s.vr.at[y], at_y(up)),
        send(s.vb.at[y], s.vb.at[y], s.kvs.at[1], s.vr.at[y], at_y(down)),
        send(keys_of(y), keys_of(y), s.kvs.at[2], s.kr.at[y], at_y(up)),
        send(keys_of(y), keys_of(y), s.kvs.at[3], s.kr.at[y], at_y(down)),
    ]
    kv_on = [
        send(keys_of(down), keys_of(down), s.kvs.at[4], s.kr.at[down], at_y(up)),
        send(s.vb.at[up], s.vb.at[up], s.kvs.at[5], s.vr.at[up], at_y(down)),
    ]

    def q_copy(source, step, sem):
        return send(s.qb.at[source], s.qb.at[source], s.qs.at[sem], s.qr.at[source], at_z(z + step))

    q_first = [(z < 3, z, 1, 0), (z > 0, z, -1, 1)]
    q_second = [((z > 0) & (z < 3), z - 1, 1, 2), ((z > 0) & (z < 3), z + 1, -1, 3)]
    q_third = [(z == 2, z - 2, 1, 4), (z == 1, z + 2, -1, 5)]

    def q_start(group):
        for when, source, step, sem in group:

            @pl.when(when)
            def _(source=source, step=step, sem=sem):
                q_copy(source, step, sem).start()

    def q_wait(distance):
        @pl.when(z >= distance)
        def _():
            arrived(s.qb.at[z - distance], s.qr.at[z - distance])

        @pl.when(z + distance < RING)
        def _():
            arrived(s.qb.at[z + distance], s.qr.at[z + distance])

    def b_copy(d):
        return send(s.sb.at[y], s.sb.at[y], s.bs.at[d], s.br.at[y], at_y(lax.rem(y + d, RING)))

    for copy in kv_own[:2]:
        copy.start()
    q_start(q_first)
    for load in loads[:2]:
        load.wait()
    s.kb[y, 0:HD, :] = s.kl[...].T
    for copy in kv_own[2:]:
        copy.start()

    for load in loads[12:15]:
        load.wait()
    for r in range(ROWS):
        row = s.dq[r].astype(F32)
        for h in range(GQ):
            s.qf[pl.ds(r * QROWS + h, STEPS, stride=GQ), :] = row[:, h * HD : (h + 1) * HD]
    s.kn[...] = jnp.zeros((HD, HD), F32)
    s.vn[...] = jnp.zeros((HD, HD), F32)
    for r in range(ROWS):
        s.kn[pl.ds(r * STEPS, STEPS), :] = s.nkv[0, r].astype(F32)
        s.vn[pl.ds(r * STEPS, STEPS), :] = s.nkv[1, r].astype(F32)

    def picked(ref):
        total = jnp.zeros((QROWS, HD), F32)
        for r in range(ROWS):
            mine = jnp.where(me * ROWS + r == prow[0], 1.0, 0.0)
            total = total + mine * ref[r * QROWS : (r + 1) * QROWS, :]
        return total

    s.sb[y] = picked(s.qf).astype(BF16)

    for d in (1, 2, 3):
        b_copy(d).start()

    lanes = (ROWS * QROWS, HD)
    at_row, at_key = iota(lanes, 0), iota(lanes, 1)
    same = lax.shift_right_logical(at_row, 5) == lax.shift_right_logical(at_key, 2)
    early = jnp.bitwise_and(at_key, 3) <= jnp.bitwise_and(lax.shift_right_logical(at_row, 3), 3)
    new = jnp.where(same & early, dot_nt(s.qf[...].astype(BF16), s.kn[...].astype(BF16)) * SCALE, MASKED)
    new_top = jnp.max(new, axis=1, keepdims=True)
    new_weights = jnp.exp2(new - new_top)
    s.mf[...] = jnp.broadcast_to(new_top, lanes)
    s.lf[...] = jnp.broadcast_to(jnp.sum(new_weights, axis=1, keepdims=True), lanes)
    s.of[...] = dot_nn(new_weights.astype(BF16), s.vn[...].astype(BF16))

    for load in loads[15:]:
        load.wait()

    def cached(r):
        rows = pl.ds(pl.multiple_of(r * QROWS, QROWS), QROWS)
        scores = dot_nt(s.qf[rows, :].astype(BF16), s.ck[r]) * SCALE
        scores = jnp.where(iota((QROWS, SLOTS), 1) < s.clen[0, r], scores, MASKED)
        before = s.mf[rows, :]
        after = jnp.maximum(before, jnp.max(scores, axis=1, keepdims=True))
        weights = jnp.exp2(scores - after[:, :1])
        keep = jnp.exp2(before - after)
        total = s.lf[rows, :] * keep + jnp.sum(weights, axis=1, keepdims=True)
        mixed = s.of[rows, :] * keep + dot_nn(weights.astype(BF16), s.cv[r])
        s.of[rows, :] = mixed / total
        s.lf[rows, :] = after + log2(total)

    def first_queries():
        q_wait(1)
        q_start(q_second)

    def some_rows(i, carry):
        @pl.when(i == 1)
        def _():
            first_queries()

        for u in range(8):
            cached(i * 8 + u)
        return carry

    lax.fori_loop(0, ROWS // 8, some_rows, 0)
    for h in range(GQ):
        s.ab[y, z, h] = s.of[pl.ds(h, ROWS * STEPS, stride=GQ), :].astype(BF16)

    def a_copy(p):
        return send(s.ab.at[y, z], s.ab.at[y, z], s.as_.at[p], s.ar.at[z], at_z(near(p)))

    def ay_copy(yy, p, sem, to):
        block = s.ab.at[yy, near(p)]
        return send(block, block, s.ays.at[sem], s.ayr.at[yy, near(p)], at_y(to))

    def ay_own(p):
        return [ay_copy(y, p, 3 * p, up), ay_copy(y, p, 3 * p + 1, down)]

    def ay_on(p):
        return ay_copy(down, p, 3 * p + 2, up) if p < 2 else ay_copy(up, p, 3 * p + 2, down)

    def rows_in(yy, p):
        arrived(s.ab.at[yy, near(p)], s.ayr.at[yy, near(p)])

    def spread_rows(p):
        if p:
            arrived(s.ab.at[y, near(p)], s.ar.at[near(p)])
        for copy in ay_own(p):
            copy.start()

    def pass_rows(p):
        rows_in(down if p < 2 else up, p)
        ay_on(p).start()

    def rest_of_rows():
        for p in range(RING):
            rows_in(up if p < 2 else down, p)

    def far_rows():
        for p in range(RING):
            rows_in(far, p)

    for p in (1, 2, 3):
        a_copy(p).start()
    spread_rows(0)
    s.sl[z] = jnp.broadcast_to(to_row(picked(s.lf)), (8, HD))

    def x_copy(d):
        zz = lax.rem(z + d, RING)
        return send(s.sx, s.xb.at[z], s.xs.at[d], s.xr.at[z], across(zz))

    def pass_query():
        for d in (1, 2, 3):
            yy = lax.rem(y + d, RING)
            arrived(s.sb.at[yy], s.br.at[yy])
        total = s.sb[0].astype(F32)
        for yy in (1, 2, 3):
            total = total + s.sb[yy].astype(F32)
        s.sx[...] = total.astype(BF16)
        for d in range(RING):
            x_copy(d).start()

    def h_copies(d):
        zz = lax.rem(z + d, RING)
        copies = [
            send(s.hos, s.ho.at[z], s.hs.at[d], s.hr.at[z], across(zz)),
            send(s.hls, s.hl.at[z], s.hls_s.at[d], s.hlr.at[z], across(zz)),
        ]
        if d:
            copies.append(send(s.sl.at[z], s.sl.at[z], s.sls.at[d], s.slr.at[z], at_z(zz)))
        return copies

    def answer():
        for zz in range(RING):
            arrived(s.xb.at[zz], s.xr.at[zz])
        query = s.xb[0].astype(F32)
        for zz in (1, 2, 3):
            query = query + s.xb[zz].astype(F32)
        span = pl.ds(PRE, SPAN)
        scores = dot_nn(query.astype(BF16), s.kb[y, 0:HD, span]) * SCALE
        top = jnp.max(scores, axis=1, keepdims=True)
        weights = jnp.exp2(scores - top)
        total = jnp.sum(weights, axis=1, keepdims=True)
        s.hos[...] = (dot_nn(weights.astype(BF16), s.vb[y, span, :]) / total).astype(BF16)
        level = jnp.broadcast_to(top + log2(total), (QROWS, HD))
        s.hls[...] = jnp.broadcast_to(to_row(level), (8, HD))
        for d in range(RING):
            for copy in h_copies(d):
                copy.start()

    def h2_copies(d):
        yy = lax.rem(y + d, RING)
        return [
            send(s.ho2.at[y], s.ho2.at[y], s.h2s.at[d], s.h2r.at[y], at_y(yy)),
            send(s.hl2.at[y], s.hl2.at[y], s.hl2s.at[d], s.hl2r.at[y], at_y(yy)),
        ]

    def combine_z():
        for zz in range(RING):
            arrived(s.ho.at[zz], s.hr.at[zz])
            arrived(s.hl.at[zz], s.hlr.at[zz])
        for d in (1, 2, 3):
            zz = lax.rem(z + d, RING)
            arrived(s.sl.at[zz], s.slr.at[zz])
        out, level = merge([(s.ho[zz].astype(F32), to_column(s.hl[zz, 0:1, :], QROWS)) for zz in range(RING)])
        s.ho2[y] = out.astype(BF16)
        s.hl2[y, 0:8, :] = jnp.broadcast_to(to_row(jnp.broadcast_to(level, (QROWS, HD))), (8, HD))
        s.hl2[y, 8:16, :] = s.sl[0] + s.sl[1] + s.sl[2] + s.sl[3]
        for d in (1, 2, 3):
            for copy in h2_copies(d):
                copy.start()

    def combine_y():
        for d in (1, 2, 3):
            yy = lax.rem(y + d, RING)
            arrived(s.ho2.at[yy], s.h2r.at[yy])
            arrived(s.hl2.at[yy], s.hl2r.at[yy])
        out, level = merge([(s.ho2[yy].astype(F32), to_column(s.hl2[yy, 0:1, :], QROWS)) for yy in range(RING)])
        rows = s.hl2[0, 8:9, :] + s.hl2[1, 8:9, :] + s.hl2[2, 8:9, :] + s.hl2[3, 8:9, :]
        before = to_column(rows, QROWS)
        top = jnp.maximum(before, level)
        w_own, w_span = jnp.exp2(before - top), jnp.exp2(level - top)
        total = w_own + w_span
        keep = jnp.broadcast_to(w_own / total, (QROWS, HD))
        added = out * (w_span / total)
        for at in range(2):
            s.wt[pl.ds(at * QROWS, QROWS), :] = keep
            s.ot[pl.ds(at * QROWS, QROWS), :] = added

    def si_copy(j):
        return send(s.so.at[j], s.si.at[j], s.sis.at[j], s.sir.at[j], sibling)

    def project(j):
        yc = turned(j)
        count = RING * ROWS * STEPS
        row = yc * (RING * ROWS) + lax.shift_right_logical(iota((count, HD), 0), 2)
        hit = row == prow[0]
        for h in range(GQ):
            block = jnp.concatenate([s.ab[yc, zz, h] for zz in range(RING)], axis=0).astype(F32)
            keep = s.wt[pl.ds(h, 2 * STEPS, stride=GQ), :]
            added = s.ot[pl.ds(h, 2 * STEPS, stride=GQ), :]
            keep = jnp.concatenate([keep] * (count // (2 * STEPS)), axis=0)
            added = jnp.concatenate([added] * (count // (2 * STEPS)), axis=0)
            block = jnp.where(hit, block * keep + added, block)
            s.am[:, h * HD : (h + 1) * HD] = block.astype(BF16)
        s.pr[...] = dot_nn(s.am[...], s.wb[...])
        s.pm[j] = s.pr[pl.ds(pl.multiple_of(core * 128, 128), 128), :]
        s.so[j] = s.pr[pl.ds(pl.multiple_of((1 - core) * 128, 128), 128), :].astype(BF16)
        si_copy(j).start()

    def xi_copy(j):
        return send(s.xo.at[j], s.xi.at[x], s.xis.at[j], s.xir.at[x], at_x(turned(j)))

    def join(j):
        arrived(s.si.at[j], s.sir.at[j])
        total = s.pm[j] + s.si[j].astype(F32)

        @pl.when(turned(j) == x)
        def _():
            s.own[...] = total

        @pl.when(turned(j) != x)
        def _():
            s.xo[j] = total.astype(BF16)
            xi_copy(j).start()

    first_lane = jnp.where(iota((BLOCK, HD), 1) == 0, 1.0, 0.0).astype(BF16)
    ones = jnp.ones((KEYS, HD), BF16)

    def scores_of(at, held):
        p, yc = lookup(PIECES, at), turned(lookup(CHUNKS, at))
        queries = jnp.concatenate([s.qb[near(p)], first_lane], axis=1)

        def quarter(j):
            cols = slice(j * KEYS // 4, (j + 1) * KEYS // 4)
            held[:, cols] = dot_nn(queries, s.kb[yc, :, cols])

        return quarter

    def weigh(at, held):
        p, yc = lookup(PIECES, at), turned(lookup(CHUNKS, at))
        late = (y * RING + near(p)) * SPAN - (yc * RING + z) * SPAN
        shape = (SPAN, SPAN)
        s.ahead[...] = jnp.where(iota(shape, 1) - iota(shape, 0) <= late, 0.0, MASKED)

        def quarter(j):
            for i in range(j * BLOCK // 4, (j + 1) * BLOCK // 4, 32):
                rows = slice(i, i + 32)
                tiles = [held[rows, k * HD : (k + 1) * HD] for k in range(KEYS // HD)]
                tiles[-1] = tiles[-1] + s.ahead[i % SPAN : i % SPAN + 32, :]
                highest = tiles[0]
                for part in tiles[1:]:
                    highest = jnp.maximum(highest, part)
                before = s.top[p, rows, :]
                after = jnp.maximum(before, jnp.max(highest, axis=1, keepdims=True))
                s.top[p, rows, :] = after
                s.kp[rows, :] = jnp.exp2((before - after) * SCALE)
                for k, part in enumerate(tiles):
                    s.pk[rows, k * HD : (k + 1) * HD] = jnp.exp2((part - after) * SCALE).astype(BF16)

        return quarter

    def mix(at):
        p, yc = lookup(PIECES, at), turned(lookup(CHUNKS, at))
        mixed = dot_nn(s.pk[...], jnp.concatenate([s.vb[yc], ones], axis=1))
        s.tot[p] = s.tot[p] * s.kp[...] + mixed[:, HD:]
        s.acc[p] = s.acc[p] * s.kp[...] + mixed[:, :HD]

        @pl.when((lookup(CHUNKS, at) == 3) & (p > 0))
        def _():
            ship(p)

    def o_copies(p):
        return [
            send(s.os.at[p], s.orb.at[p], s.ops.at[p], s.opr.at[p], at_z(near(p))),
            send(s.ls.at[p], s.lrb.at[p], s.lps.at[p], s.lpr.at[p], at_z(near(p))),
        ]

    def each_head(one):
        def some(i, carry):
            for u in range(4):
                one(i * 4 + u)
            return carry

        lax.fori_loop(0, GQ // 4, some, 0)

    def ship(p):
        def one(h):
            rows = pl.ds(pl.multiple_of(h * SPAN, SPAN), SPAN)
            total = s.tot[p, rows, :]
            s.os[p, h] = (s.acc[p, rows, :] / total).astype(BF16)
            s.ls[p, pl.ds(h, 1), :] = to_row(s.top[p, rows, :] * SCALE + log2(total))

        each_head(one)
        for copy in o_copies(p):
            copy.start()

    def settle():
        def one(h):
            rows = pl.ds(pl.multiple_of(h * SPAN, SPAN), SPAN)
            levels = [to_column(s.lrb[p, pl.ds(h, 1), :], SPAN) for p in (1, 2, 3)]
            own = s.top[0, rows, :] * SCALE
            top = own
            for level in levels:
                top = jnp.maximum(top, level)
            weight = jnp.exp2(own - top)
            total = s.tot[0, rows, :] * weight
            mixed = s.acc[0, rows, :] * weight
            for p, level in zip((1, 2, 3), levels):
                weight = jnp.exp2(level - top)
                total = total + weight
                mixed = mixed + s.orb[p, h].astype(F32) * weight
            out_p[:, pl.ds(pl.multiple_of(h * HD, HD), HD)] = (mixed / total).astype(BF16)

        each_head(one)

    def keys_near():
        arrived(keys_of(down), s.kr.at[down])
        kv_on[0].start()
        arrived(s.vb.at[up], s.vr.at[up])
        kv_on[1].start()
        arrived(s.vb.at[down], s.vr.at[down])
        arrived(keys_of(up), s.kr.at[up])

    def keys_far():
        arrived(keys_of(far), s.kr.at[far])
        arrived(s.vb.at[far], s.vr.at[far])

    def second_queries():
        q_wait(2)
        q_start(q_third)

    actions = {
        0: [pass_query],
        1: [second_queries, keys_near],
        2: [answer],
        3: [lambda: spread_rows(1)],
        4: [keys_far, lambda: pass_rows(0)],
        5: [lambda: q_wait(3), lambda: spread_rows(2)],
        6: [combine_z, lambda: pass_rows(1)],
        7: [lambda: spread_rows(3)],
        8: [combine_y, lambda: pass_rows(2)],
        9: [lambda: pass_rows(3)],
        11: [rest_of_rows],
        13: [far_rows],
    }

    def prepare(i, parity):
        for at, todo in actions.items():
            if at % 2 != parity:
                continue

            @pl.when(i == at)
            def _(todo=todo):
                for action in todo:
                    action()

        @pl.when((i == 10) | ((i >= 12) & (i < 15)))
        def _():
            join(jnp.maximum(i - 11, 0))

        @pl.when((i == 9) | ((i >= 11) & (i < 14)))
        def _():
            project(jnp.maximum(i - 10, 0))

    def unit(i, parity, held, later):
        prepare(i + 1, 1 - parity)
        scores, weights = scores_of(jnp.minimum(i + 1, 15), later), weigh(i, held)
        for j in range(4):
            scores(j)
            weights(j)
        mix(i)

    def step(i, carry):
        unit(2 * i, 0, s.ts0, s.ts1)
        unit(2 * i + 1, 1, s.ts1, s.ts0)
        return carry

    for action in actions.pop(0):
        action()
    first = scores_of(0, s.ts0)
    for j in range(4):
        first(j)
    lax.fori_loop(0, 8, step, 0)

    for p in (1, 2, 3):
        arrived(s.orb.at[p], s.opr.at[p])
        arrived(s.lrb.at[p], s.lpr.at[p])
    settle()

    total = s.own[...]
    for d in (1, 2, 3):
        xx = lax.rem(x + d, RING)
        arrived(s.xi.at[xx], s.xir.at[xx])
        total = total + s.xi[xx].astype(F32)
    for r in range(32):
        out_d[r] = total[r * STEPS : (r + 1) * STEPS, :].astype(BF16)

    for copy in kv_own + kv_on + [c for p in range(RING) for c in ay_own(p) + [ay_on(p)]]:
        copy.wait_send()
    for when, source, step_z, sem in q_first + q_second + q_third:

        @pl.when(when)
        def _(source=source, step_z=step_z, sem=sem):
            q_copy(source, step_z, sem).wait_send()

    for d in range(RING):
        x_copy(d).wait_send()
        for copy in h_copies(d):
            copy.wait_send()
        if d:
            b_copy(d).wait_send()
            a_copy(d).wait_send()
            for copy in h2_copies(d):
                copy.wait_send()
            for copy in o_copies(d):
                copy.wait_send()
    for j in range(RING):
        si_copy(j).wait_send()

        @pl.when(turned(j) != x)
        def _(j=j):
            xi_copy(j).wait_send()


def shards(span_q, span_kv, prefix_kv, prefix_len, dec_q, dec_new_kv, dec_cache, cache_len, prompt_row, out_weight):
    vmem = pl.BlockSpec(memory_space=pltpu.VMEM)
    smem = pl.BlockSpec(memory_space=pltpu.SMEM)
    hbm = pl.BlockSpec(memory_space=pltpu.HBM)
    prefill, decode = pl.pallas_call(
        kernel,
        out_shape=(
            jax.ShapeDtypeStruct((SPAN, GQ * HD), BF16),
            jax.ShapeDtypeStruct((32, STEPS, COLS), BF16),
        ),
        in_specs=[smem] * 2 + [hbm] * 8,
        out_specs=(vmem, vmem),
        scratch_shapes=list(SCRATCH.values()),
        compiler_params=pltpu.CompilerParams(
            collective_id=0, has_side_effects=True, vmem_limit_bytes=VMEM_BYTES
        ),
        cost_estimate=pl.CostEstimate(flops=11_000_000_000, bytes_accessed=8_000_000, transcendentals=17_000_000),
    )(
        prefix_len,
        prompt_row,
        *[
            pltpu.with_memory_space_constraint(operand, pltpu.HBM)
            for operand in (
                cache_len,
                span_q[0],
                span_kv[0],
                prefix_kv[0],
                dec_q[0],
                dec_new_kv[0],
                dec_cache[0],
                out_weight,
            )
        ],
    )
    return prefill[None], decode[None]


def solution(mesh):
    placed = (
        P("grp", "ctx", "head"),
        P("grp", None, "ctx", "head"),
        P("grp", None, "ctx", "head"),
        P("grp"),
        P("grp", "ctx", None, "head"),
        P("grp", None, "ctx", None, "head"),
        P("grp", None, "ctx", None, "head"),
        P("grp", "ctx"),
        P("grp"),
        P("head", "ctx"),
    )
    return jax.shard_map(
        shards,
        mesh=mesh,
        in_specs=placed,
        out_specs=(P("grp", "ctx", "head"), P("grp", "head", None, "ctx")),
        check_vma=False,
    )
```

```python
import math

import jax
import jax.numpy as jnp
from jax import lax
from jax.experimental import pallas as pl
from jax.experimental.pallas import tpu as pltpu
from jax.sharding import PartitionSpec as P

HD = 128
GQ = 8
RING = 4
PRE = 896
SPAN = 128
KEYS = PRE + SPAN
ROWS = 16
STEPS = 4
SLOTS = 512
QROWS = STEPS * GQ
COLS = 512
MASKED = -1e30
LOG2E = math.log2(math.e)
SCALE = LOG2E / math.sqrt(HD)
MESH = pl.DeviceIdType.MESH
F32 = jnp.float32
BF16 = jnp.bfloat16
BLOCK = 512
VMEM_BYTES = 40 * 1024 * 1024

PIECES = (0, 1, 1, 1, 2, 2, 2, 2, 1, 3, 3, 3, 3, 0, 0, 0)
CHUNKS = (0, 0, 1, 2, 0, 1, 2, 3, 3, 0, 1, 2, 3, 1, 2, 3)


def dot_nt(a, b):
    return lax.dot_general(a, b, (((1,), (1,)), ((), ())), preferred_element_type=F32)


def dot_nn(a, b):
    return lax.dot_general(a, b, (((1,), (0,)), ((), ())), preferred_element_type=F32)


def log2(v):
    return jnp.log(v) * LOG2E


def iota(shape, axis):
    return lax.broadcasted_iota(jnp.int32, shape, axis)


def lookup(table, index):
    value = jnp.int32(table[0])
    for at, entry in enumerate(table[1:], 1):
        value = jnp.where(index == at, jnp.int32(entry), value)
    return value


def to_row(column):
    shape = column.shape
    return jnp.sum(jnp.where(iota(shape, 0) == iota(shape, 1), column, 0.0), axis=0, keepdims=True)


def to_column(row, count):
    shape = (count, HD)
    spread = jnp.broadcast_to(row, shape)
    return jnp.sum(jnp.where(iota(shape, 0) == iota(shape, 1), spread, 0.0), axis=1, keepdims=True)


def merge(parts):
    top = parts[0][1]
    for _, level in parts[1:]:
        top = jnp.maximum(top, level)
    weights = [jnp.exp2(level - top) for _, level in parts]
    total = weights[0]
    for w in weights[1:]:
        total = total + w
    mixed = parts[0][0] * weights[0]
    for (out, _), w in zip(parts[1:], weights[1:]):
        mixed = mixed + out * w
    return mixed / total, top + log2(total)


SCRATCH = {
    "kl": pltpu.VMEM((KEYS, HD), BF16),
    "kb": pltpu.VMEM((RING, 2 * HD, KEYS), BF16),
    "vb": pltpu.VMEM((RING, KEYS, HD), BF16),
    "qb": pltpu.VMEM((RING, GQ * SPAN, HD), BF16),
    "ts0": pltpu.VMEM((BLOCK, KEYS), F32),
    "ts1": pltpu.VMEM((BLOCK, KEYS), F32),
    "mx0": pltpu.VMEM((BLOCK, HD), F32),
    "mx1": pltpu.VMEM((BLOCK, HD), F32),
    "dq": pltpu.VMEM((ROWS, STEPS, GQ * HD), BF16),
    "nkv": pltpu.VMEM((2, ROWS, STEPS, HD), BF16),
    "acc": pltpu.VMEM((RING, GQ * SPAN, HD), F32),
    "top": pltpu.VMEM((RING, GQ * SPAN, HD), F32),
    "tot": pltpu.VMEM((RING, GQ * SPAN, HD), F32),
    "os": pltpu.VMEM((RING, GQ, SPAN, HD), BF16),
    "ls": pltpu.VMEM((RING, GQ, SPAN), F32),
    "orb": pltpu.VMEM((RING, GQ, SPAN, HD), BF16),
    "lrb": pltpu.VMEM((RING, GQ, SPAN), F32),
    "ck": pltpu.VMEM((ROWS, SLOTS, HD), BF16),
    "cv": pltpu.VMEM((ROWS, SLOTS, HD), BF16),
    "wb": pltpu.VMEM((GQ * HD, COLS), BF16),
    "qf": pltpu.VMEM((ROWS * QROWS, HD), F32),
    "kn": pltpu.VMEM((HD, HD), F32),
    "vn": pltpu.VMEM((HD, HD), F32),
    "of": pltpu.VMEM((ROWS * QROWS, HD), F32),
    "mf": pltpu.VMEM((ROWS * QROWS, HD), F32),
    "lf": pltpu.VMEM((ROWS * QROWS, HD), F32),
    "sb": pltpu.VMEM((RING, QROWS, HD), BF16),
    "sx": pltpu.VMEM((QROWS, HD), BF16),
    "xb": pltpu.VMEM((RING, QROWS, HD), BF16),
    "hos": pltpu.VMEM((QROWS, HD), BF16),
    "hls": pltpu.VMEM((8, HD), F32),
    "ho": pltpu.VMEM((RING, QROWS, HD), BF16),
    "hl": pltpu.VMEM((RING, 8, HD), F32),
    "sl": pltpu.VMEM((RING, 8, HD), F32),
    "ho2": pltpu.VMEM((RING, QROWS, HD), BF16),
    "hl2": pltpu.VMEM((RING, 16, HD), F32),
    "wt": pltpu.VMEM((2 * QROWS, HD), F32),
    "ot": pltpu.VMEM((2 * QROWS, HD), F32),
    "ab": pltpu.VMEM((RING, RING, GQ, ROWS * STEPS, HD), BF16),
    "am": pltpu.VMEM((RING * ROWS * STEPS, GQ * HD), BF16),
    "pr": pltpu.VMEM((RING * ROWS * STEPS, COLS), F32),
    "pm": pltpu.VMEM((RING, 128, COLS), F32),
    "so": pltpu.VMEM((RING, 128, COLS), BF16),
    "si": pltpu.VMEM((RING, 128, COLS), BF16),
    "xo": pltpu.VMEM((RING, 128, COLS), BF16),
    "xi": pltpu.VMEM((RING, 128, COLS), BF16),
    "own": pltpu.VMEM((128, COLS), F32),
    "clen": pltpu.SMEM((1, ROWS), jnp.int32),
    "loc": pltpu.SemaphoreType.DMA((18,)),
    "kvs": pltpu.SemaphoreType.DMA((6,)),
    "kr": pltpu.SemaphoreType.DMA((RING,)),
    "vr": pltpu.SemaphoreType.DMA((RING,)),
    "qs": pltpu.SemaphoreType.DMA((6,)),
    "qr": pltpu.SemaphoreType.DMA((RING,)),
    "bs": pltpu.SemaphoreType.DMA((RING,)),
    "br": pltpu.SemaphoreType.DMA((RING,)),
    "xs": pltpu.SemaphoreType.DMA((RING,)),
    "xr": pltpu.SemaphoreType.DMA((RING,)),
    "hs": pltpu.SemaphoreType.DMA((RING,)),
    "hr": pltpu.SemaphoreType.DMA((RING,)),
    "hls_s": pltpu.SemaphoreType.DMA((RING,)),
    "hlr": pltpu.SemaphoreType.DMA((RING,)),
    "sls": pltpu.SemaphoreType.DMA((RING,)),
    "slr": pltpu.SemaphoreType.DMA((RING,)),
    "h2s": pltpu.SemaphoreType.DMA((RING,)),
    "h2r": pltpu.SemaphoreType.DMA((RING,)),
    "hl2s": pltpu.SemaphoreType.DMA((RING,)),
    "hl2r": pltpu.SemaphoreType.DMA((RING,)),
    "as_": pltpu.SemaphoreType.DMA((6,)),
    "ar": pltpu.SemaphoreType.DMA((RING,)),
    "ays": pltpu.SemaphoreType.DMA((3 * RING,)),
    "ayr": pltpu.SemaphoreType.DMA((RING, RING)),
    "ops": pltpu.SemaphoreType.DMA((RING,)),
    "opr": pltpu.SemaphoreType.DMA((RING,)),
    "lps": pltpu.SemaphoreType.DMA((RING,)),
    "lpr": pltpu.SemaphoreType.DMA((RING,)),
    "sis": pltpu.SemaphoreType.DMA((RING,)),
    "sir": pltpu.SemaphoreType.DMA((RING,)),
    "xis": pltpu.SemaphoreType.DMA((RING,)),
    "xir": pltpu.SemaphoreType.DMA((RING,)),
}


class Names:
    pass


def kernel(plen, prow, clen_in, q_in, skv, pkv, dq, nkv, cache, w_in, out_p, out_d, *scratch):
    s = Names()
    for name, ref in zip(SCRATCH, scratch):
        setattr(s, name, ref)

    me = lax.axis_index("ctx")
    y, z = lax.div(me, RING), lax.rem(me, RING)
    head = lax.axis_index("head")
    x, core = lax.div(head, 2), lax.rem(head, 2)
    other = 1 - lax.axis_index("grp")

    def turned(j):
        return lax.rem(y + lax.div(j * (j + 1), 2), RING)

    def near(p):
        high = lax.rem(lax.div(z, 2) + lax.div(p, 2), 2)
        return 2 * high + lax.rem(z + p, 2)

    up, down, far = lax.rem(y + 1, RING), lax.rem(y + 3, RING), lax.rem(y + 2, RING)

    def at_y(yy):
        return {"ctx": yy * RING + z}

    def at_z(zz):
        return {"ctx": y * RING + zz}

    def across(zz):
        return {"ctx": y * RING + zz, "grp": other}

    def at_x(xx):
        return {"head": xx * 2 + core}

    sibling = {"head": x * 2 + 1 - core}

    def send(src, dst, ssem, rsem, device):
        return pltpu.make_async_remote_copy(
            src_ref=src, dst_ref=dst, send_sem=ssem, recv_sem=rsem, device_id=device, device_id_type=MESH
        )

    def arrived(dst, rsem):
        send(dst, dst, s.loc.at[0], rsem, sibling).wait_recv()

    pairs = [
        (pkv.at[0], s.kl.at[pl.ds(0, PRE)]),
        (skv.at[0], s.kl.at[pl.ds(PRE, SPAN)]),
        (pkv.at[1], s.vb.at[y, pl.ds(0, PRE)]),
        (skv.at[1], s.vb.at[y, pl.ds(PRE, SPAN)]),
    ]
    pairs += [(q_in.at[:, pl.ds(h * HD, HD)], s.qb.at[z, pl.ds(h * SPAN, SPAN)]) for h in range(GQ)]
    pairs += [(dq, s.dq), (nkv, s.nkv), (clen_in, s.clen), (cache.at[0], s.ck), (cache.at[1], s.cv), (w_in, s.wb)]
    loads = [pltpu.make_async_copy(src, dst, s.loc.at[at]) for at, (src, dst) in enumerate(pairs)]
    for load in loads:
        load.start()

    barrier = pltpu.get_barrier_semaphore()
    greeted = [at_y(lax.rem(y + d, RING)) for d in (1, 2, 3)] + [at_z(lax.rem(z + d, RING)) for d in (1, 2, 3)]
    greeted += [across(zz) for zz in range(RING)] + [sibling] + [at_x(lax.rem(x + d, RING)) for d in (1, 2, 3)]
    for device in greeted:
        pl.semaphore_signal(barrier, inc=1, device_id=device, device_id_type=MESH)

    def clear(p, carry):
        s.acc[p] = jnp.zeros((GQ * SPAN, HD), F32)
        s.tot[p] = jnp.zeros((GQ * SPAN, HD), F32)
        s.top[p] = jnp.full((GQ * SPAN, HD), MASKED, F32)
        slot = iota((HD, KEYS), 1)
        unused = ((p * RING + z) * PRE + slot >= plen[0]) & (slot < PRE) & (iota((HD, KEYS), 0) == 0)
        s.kb[p, HD : 2 * HD, :] = jnp.where(unused, MASKED, 0.0).astype(BF16)
        return carry

    lax.fori_loop(0, RING, clear, 0)


    for load in loads[2:12]:
        load.wait()
    pl.semaphore_wait(barrier, len(greeted))

    def keys_of(yy):
        return s.kb.at[yy, pl.ds(0, HD)]

    kv_own = [
        send(s.vb.at[y], s.vb.at[y], s.kvs.at[0], s.vr.at[y], at_y(up)),
        send(s.vb.at[y], s.vb.at[y], s.kvs.at[1], s.vr.at[y], at_y(down)),
        send(keys_of(y), keys_of(y), s.kvs.at[2], s.kr.at[y], at_y(up)),
        send(keys_of(y), keys_of(y), s.kvs.at[3], s.kr.at[y], at_y(down)),
    ]
    kv_on = [
        send(keys_of(down), keys_of(down), s.kvs.at[4], s.kr.at[down], at_y(up)),
        send(s.vb.at[up], s.vb.at[up], s.kvs.at[5], s.vr.at[up], at_y(down)),
    ]

    def q_copy(source, step, sem):
        return send(s.qb.at[source], s.qb.at[source], s.qs.at[sem], s.qr.at[source], at_z(z + step))

    def a_copy(source, step, sem):
        block = s.ab.at[y, source]
        return send(block, block, s.as_.at[sem], s.ar.at[source], at_z(z + step))

    q_first = [(z < 3, z, 1, 0), (z > 0, z, -1, 1)]
    q_second = [((z > 0) & (z < 3), z - 1, 1, 2), ((z > 0) & (z < 3), z + 1, -1, 3)]
    q_third = [(z == 2, z - 2, 1, 4), (z == 1, z + 2, -1, 5)]

    def z_start(copy, group):
        for when, source, step, sem in group:

            @pl.when(when)
            def _(source=source, step=step, sem=sem):
                copy(source, step, sem).start()

    def z_wait(block, sems, distance):
        @pl.when(z >= distance)
        def _():
            arrived(block(z - distance), sems.at[z - distance])

        @pl.when(z + distance < RING)
        def _():
            arrived(block(z + distance), sems.at[z + distance])

    def q_wait(distance):
        z_wait(lambda source: s.qb.at[source], s.qr, distance)

    def a_wait(distance):
        z_wait(lambda source: s.ab.at[y, source], s.ar, distance)

    def b_copy(d):
        return send(s.sb.at[y], s.sb.at[y], s.bs.at[d], s.br.at[y], at_y(lax.rem(y + d, RING)))

    for copy in kv_own[:2]:
        copy.start()
    z_start(q_copy, q_first)
    for load in loads[:2]:
        load.wait()
    s.kb[y, 0:HD, :] = s.kl[...].T
    for copy in kv_own[2:]:
        copy.start()

    for load in loads[12:15]:
        load.wait()
    for r in range(ROWS):
        row = s.dq[r].astype(F32)
        for h in range(GQ):
            s.qf[pl.ds(r * QROWS + h, STEPS, stride=GQ), :] = row[:, h * HD : (h + 1) * HD]
    s.kn[...] = jnp.zeros((HD, HD), F32)
    s.vn[...] = jnp.zeros((HD, HD), F32)
    for r in range(ROWS):
        s.kn[pl.ds(r * STEPS, STEPS), :] = s.nkv[0, r].astype(F32)
        s.vn[pl.ds(r * STEPS, STEPS), :] = s.nkv[1, r].astype(F32)

    def picked(ref):
        total = jnp.zeros((QROWS, HD), F32)
        for r in range(ROWS):
            mine = jnp.where(me * ROWS + r == prow[0], 1.0, 0.0)
            total = total + mine * ref[r * QROWS : (r + 1) * QROWS, :]
        return total

    s.sb[y] = picked(s.qf).astype(BF16)

    for d in (1, 2, 3):
        b_copy(d).start()

    lanes = (ROWS * QROWS, HD)
    at_row, at_key = iota(lanes, 0), iota(lanes, 1)
    same = lax.shift_right_logical(at_row, 5) == lax.shift_right_logical(at_key, 2)
    early = jnp.bitwise_and(at_key, 3) <= jnp.bitwise_and(lax.shift_right_logical(at_row, 3), 3)
    new = jnp.where(same & early, dot_nt(s.qf[...].astype(BF16), s.kn[...].astype(BF16)) * SCALE, MASKED)
    new_top = jnp.max(new, axis=1, keepdims=True)
    new_weights = jnp.exp2(new - new_top)
    s.mf[...] = jnp.broadcast_to(new_top, lanes)
    s.lf[...] = jnp.broadcast_to(jnp.sum(new_weights, axis=1, keepdims=True), lanes)
    s.of[...] = dot_nn(new_weights.astype(BF16), s.vn[...].astype(BF16))

    for load in loads[15:]:
        load.wait()

    def cached(r):
        rows = pl.ds(pl.multiple_of(r * QROWS, QROWS), QROWS)
        scores = dot_nt(s.qf[rows, :].astype(BF16), s.ck[r]) * SCALE
        scores = jnp.where(iota((QROWS, SLOTS), 1) < s.clen[0, r], scores, MASKED)
        before = s.mf[rows, :]
        after = jnp.maximum(before, jnp.max(scores, axis=1, keepdims=True))
        weights = jnp.exp2(scores - after[:, :1])
        keep = jnp.exp2(before - after)
        total = s.lf[rows, :] * keep + jnp.sum(weights, axis=1, keepdims=True)
        mixed = s.of[rows, :] * keep + dot_nn(weights.astype(BF16), s.cv[r])
        s.of[rows, :] = mixed / total
        s.lf[rows, :] = after + log2(total)

    def first_queries():
        q_wait(1)
        z_start(q_copy, q_second)

    def some_rows(i, carry):
        @pl.when(i == 1)
        def _():
            first_queries()
            arrived(s.vb.at[up], s.vr.at[up])
            kv_on[1].start()

        for u in range(8):
            cached(i * 8 + u)
        return carry

    lax.fori_loop(0, ROWS // 8, some_rows, 0)
    for h in range(GQ):
        s.ab[y, z, h] = s.of[pl.ds(h, ROWS * STEPS, stride=GQ), :].astype(BF16)

    def ay_copy(yy, p, sem, to):
        block = s.ab.at[yy, near(p)]
        return send(block, block, s.ays.at[sem], s.ayr.at[yy, near(p)], at_y(to))

    def ay_own(p):
        return [ay_copy(y, p, 3 * p, up), ay_copy(y, p, 3 * p + 1, down)]

    def ay_on(p):
        return ay_copy(down, p, 3 * p + 2, up) if p < 2 else ay_copy(up, p, 3 * p + 2, down)

    def rows_in(yy, p):
        arrived(s.ab.at[yy, near(p)], s.ayr.at[yy, near(p)])

    def spread_rows(p):
        if p:
            a_wait(p)
            z_start(a_copy, (q_second, q_third, [])[p - 1])
        for copy in ay_own(p):
            copy.start()

    def pass_rows(p):
        rows_in(down if p < 2 else up, p)
        ay_on(p).start()

    def rest_of_rows():
        for p in range(RING):
            rows_in(up if p < 2 else down, p)

    def far_rows():
        for p in range(RING):
            rows_in(far, p)

    z_start(a_copy, q_first)
    spread_rows(0)
    s.sl[z] = jnp.broadcast_to(to_row(picked(s.lf)), (8, HD))

    def x_copy(d):
        zz = lax.rem(z + d, RING)
        return send(s.sx, s.xb.at[z], s.xs.at[d], s.xr.at[z], across(zz))

    def pass_query():
        for d in (1, 2, 3):
            yy = lax.rem(y + d, RING)
            arrived(s.sb.at[yy], s.br.at[yy])
        total = s.sb[0].astype(F32)
        for yy in (1, 2, 3):
            total = total + s.sb[yy].astype(F32)
        s.sx[...] = total.astype(BF16)
        for d in range(RING):
            x_copy(d).start()

    def h_copies(d):
        zz = lax.rem(z + d, RING)
        copies = [
            send(s.hos, s.ho.at[z], s.hs.at[d], s.hr.at[z], across(zz)),
            send(s.hls, s.hl.at[z], s.hls_s.at[d], s.hlr.at[z], across(zz)),
        ]
        if d:
            copies.append(send(s.sl.at[z], s.sl.at[z], s.sls.at[d], s.slr.at[z], at_z(zz)))
        return copies

    def answer():
        for zz in range(RING):
            arrived(s.xb.at[zz], s.xr.at[zz])
        query = s.xb[0].astype(F32)
        for zz in (1, 2, 3):
            query = query + s.xb[zz].astype(F32)
        span = pl.ds(PRE, SPAN)
        scores = dot_nn(query.astype(BF16), s.kb[y, 0:HD, span]) * SCALE
        top = jnp.max(scores, axis=1, keepdims=True)
        weights = jnp.exp2(scores - top)
        total = jnp.sum(weights, axis=1, keepdims=True)
        s.hos[...] = (dot_nn(weights.astype(BF16), s.vb[y, span, :]) / total).astype(BF16)
        level = jnp.broadcast_to(top + log2(total), (QROWS, HD))
        s.hls[...] = jnp.broadcast_to(to_row(level), (8, HD))
        for d in range(RING):
            for copy in h_copies(d):
                copy.start()

    def h2_copies(d):
        yy = lax.rem(y + d, RING)
        return [
            send(s.ho2.at[y], s.ho2.at[y], s.h2s.at[d], s.h2r.at[y], at_y(yy)),
            send(s.hl2.at[y], s.hl2.at[y], s.hl2s.at[d], s.hl2r.at[y], at_y(yy)),
        ]

    def combine_z():
        for zz in range(RING):
            arrived(s.ho.at[zz], s.hr.at[zz])
            arrived(s.hl.at[zz], s.hlr.at[zz])
        for d in (1, 2, 3):
            zz = lax.rem(z + d, RING)
            arrived(s.sl.at[zz], s.slr.at[zz])
        out, level = merge([(s.ho[zz].astype(F32), to_column(s.hl[zz, 0:1, :], QROWS)) for zz in range(RING)])
        s.ho2[y] = out.astype(BF16)
        s.hl2[y, 0:8, :] = jnp.broadcast_to(to_row(jnp.broadcast_to(level, (QROWS, HD))), (8, HD))
        s.hl2[y, 8:16, :] = s.sl[0] + s.sl[1] + s.sl[2] + s.sl[3]
        for d in (1, 2, 3):
            for copy in h2_copies(d):
                copy.start()

    def combine_y():
        for d in (1, 2, 3):
            yy = lax.rem(y + d, RING)
            arrived(s.ho2.at[yy], s.h2r.at[yy])
            arrived(s.hl2.at[yy], s.hl2r.at[yy])
        out, level = merge([(s.ho2[yy].astype(F32), to_column(s.hl2[yy, 0:1, :], QROWS)) for yy in range(RING)])
        rows = s.hl2[0, 8:9, :] + s.hl2[1, 8:9, :] + s.hl2[2, 8:9, :] + s.hl2[3, 8:9, :]
        before = to_column(rows, QROWS)
        top = jnp.maximum(before, level)
        w_own, w_span = jnp.exp2(before - top), jnp.exp2(level - top)
        total = w_own + w_span
        keep = jnp.broadcast_to(w_own / total, (QROWS, HD))
        added = out * (w_span / total)
        for at in range(2):
            s.wt[pl.ds(at * QROWS, QROWS), :] = keep
            s.ot[pl.ds(at * QROWS, QROWS), :] = added

    def si_copy(j):
        return send(s.so.at[j], s.si.at[j], s.sis.at[j], s.sir.at[j], sibling)

    def project(j):
        yc = turned(j)
        count = RING * ROWS * STEPS
        row = yc * (RING * ROWS) + lax.shift_right_logical(iota((count, HD), 0), 2)
        hit = row == prow[0]
        for h in range(GQ):
            block = jnp.concatenate([s.ab[yc, zz, h] for zz in range(RING)], axis=0).astype(F32)
            keep = s.wt[pl.ds(h, 2 * STEPS, stride=GQ), :]
            added = s.ot[pl.ds(h, 2 * STEPS, stride=GQ), :]
            keep = jnp.concatenate([keep] * (count // (2 * STEPS)), axis=0)
            added = jnp.concatenate([added] * (count // (2 * STEPS)), axis=0)
            block = jnp.where(hit, block * keep + added, block)
            s.am[:, h * HD : (h + 1) * HD] = block.astype(BF16)
        s.pr[...] = dot_nn(s.am[...], s.wb[...])
        s.pm[j] = s.pr[pl.ds(pl.multiple_of(core * 128, 128), 128), :]
        s.so[j] = s.pr[pl.ds(pl.multiple_of((1 - core) * 128, 128), 128), :].astype(BF16)
        si_copy(j).start()

    def xi_copy(j):
        return send(s.xo.at[j], s.xi.at[x], s.xis.at[j], s.xir.at[x], at_x(turned(j)))

    def join(j):
        arrived(s.si.at[j], s.sir.at[j])
        total = s.pm[j] + s.si[j].astype(F32)

        @pl.when(turned(j) == x)
        def _():
            s.own[...] = total

        @pl.when(turned(j) != x)
        def _():
            s.xo[j] = total.astype(BF16)
            xi_copy(j).start()

    count = BLOCK // SPAN
    first_lane = jnp.where(iota((BLOCK, HD), 1) == 0, 1.0, 0.0).astype(BF16)
    ones = jnp.ones((KEYS, HD), BF16)

    def scores_of(at, b, held, peak):
        p, yc = lookup(PIECES, at), turned(lookup(CHUNKS, at))
        zq = near(p)
        late = (y * RING + zq) * SPAN - (yc * RING + z) * SPAN
        shape = (SPAN, SPAN)
        ahead = jnp.where(iota(shape, 1) - iota(shape, 0) <= late, 0.0, MASKED)
        ahead = jnp.concatenate([ahead] * count, axis=0)
        queries = jnp.concatenate([s.qb[zq, b * BLOCK : (b + 1) * BLOCK, :], first_lane], axis=1)
        scores = dot_nn(queries, s.kb[yc])
        highest = None
        for k in range(KEYS // HD):
            cols = slice(k * HD, (k + 1) * HD)
            part = scores[:, cols] * SCALE
            if k == PRE // HD:
                part = part + ahead
            held[:, cols] = part
            highest = part if highest is None else jnp.maximum(highest, part)
        peak[...] = jnp.broadcast_to(jnp.max(highest, axis=1, keepdims=True), (BLOCK, HD))

    def weigh(at, b, held, peak):
        p, yc = lookup(PIECES, at), turned(lookup(CHUNKS, at))
        rows = slice(b * BLOCK, (b + 1) * BLOCK)
        before = s.top[p, rows, :]
        after = jnp.maximum(before, peak[...])
        keep = jnp.exp2(before - after)
        packed = []
        for k in range(KEYS // HD):
            packed.append(jnp.exp2(held[:, k * HD : (k + 1) * HD] - after).astype(BF16))
        mixed = dot_nn(jnp.concatenate(packed, axis=1), jnp.concatenate([s.vb[yc], ones], axis=1))
        s.top[p, rows, :] = after
        s.tot[p, rows, :] = s.tot[p, rows, :] * keep + mixed[:, HD:]
        s.acc[p, rows, :] = s.acc[p, rows, :] * keep + mixed[:, :HD]

    def o_copies(p):
        return [
            send(s.os.at[p], s.orb.at[p], s.ops.at[p], s.opr.at[p], at_z(near(p))),
            send(s.ls.at[p], s.lrb.at[p], s.lps.at[p], s.lpr.at[p], at_z(near(p))),
        ]

    def each_head(one):
        def some(i, carry):
            for u in range(4):
                one(i * 4 + u)
            return carry

        lax.fori_loop(0, GQ // 4, some, 0)

    def ship(p):
        def one(h):
            rows = pl.ds(pl.multiple_of(h * SPAN, SPAN), SPAN)
            total = s.tot[p, rows, :]
            s.os[p, h] = (s.acc[p, rows, :] / total).astype(BF16)
            s.ls[p, pl.ds(h, 1), :] = to_row(s.top[p, rows, :] + log2(total))

        each_head(one)
        for copy in o_copies(p):
            copy.start()

    def settle():
        def one(h):
            rows = pl.ds(pl.multiple_of(h * SPAN, SPAN), SPAN)
            levels = [to_column(s.lrb[p, pl.ds(h, 1), :], SPAN) for p in (1, 2, 3)]
            top = s.top[0, rows, :]
            for level in levels:
                top = jnp.maximum(top, level)
            weight = jnp.exp2(s.top[0, rows, :] - top)
            total = s.tot[0, rows, :] * weight
            mixed = s.acc[0, rows, :] * weight
            for p, level in zip((1, 2, 3), levels):
                weight = jnp.exp2(level - top)
                total = total + weight
                mixed = mixed + s.orb[p, h].astype(F32) * weight
            out_p[:, pl.ds(pl.multiple_of(h * HD, HD), HD)] = (mixed / total).astype(BF16)

        each_head(one)

    def pass_keys():
        arrived(keys_of(down), s.kr.at[down])
        kv_on[0].start()

    def keys_near():
        arrived(s.vb.at[down], s.vr.at[down])
        arrived(keys_of(up), s.kr.at[up])

    def keys_far():
        arrived(keys_of(far), s.kr.at[far])
        arrived(s.vb.at[far], s.vr.at[far])

    def second_queries():
        q_wait(2)
        z_start(q_copy, q_third)

    actions = {
        0: [pass_query],
        1: [pass_keys],
        2: [keys_near],
        3: [second_queries, lambda: spread_rows(1)],
        4: [answer],
        5: [lambda: spread_rows(2), lambda: pass_rows(0)],
        6: [combine_z],
        7: [keys_far, lambda: pass_rows(1)],
        8: [lambda: spread_rows(3)],
        9: [lambda: q_wait(3)],
        10: [combine_y, lambda: pass_rows(2)],
        11: [lambda: pass_rows(3)],
        14: [rest_of_rows],
        16: [far_rows],
    }

    def prepare(i):
        for at, todo in actions.items():

            @pl.when(i == at)
            def _(todo=todo):
                for action in todo:
                    action()

        @pl.when((i == 12) | (i >= 15))
        def _():
            join(jnp.maximum(i - 14, 0))

        @pl.when((i == 11) | (i >= 14))
        def _():
            project(jnp.maximum(i - 13, 0))

    def step(i, carry):
        scores_of(i, 1, s.ts1, s.mx1)
        weigh(i, 0, s.ts0, s.mx0)
        prepare(i + 1)
        scores_of(jnp.minimum(i + 1, 15), 0, s.ts0, s.mx0)
        weigh(i, 1, s.ts1, s.mx1)
        p, k = lookup(PIECES, i), lookup(CHUNKS, i)

        @pl.when((k == 3) & (p > 0))
        def _():
            ship(p)

        return carry

    for action in actions.pop(0):
        action()
    scores_of(0, 0, s.ts0, s.mx0)
    lax.fori_loop(0, 16, step, 0)
    join(RING - 1)
    for p in (1, 2, 3):
        arrived(s.orb.at[p], s.opr.at[p])
        arrived(s.lrb.at[p], s.lpr.at[p])
    settle()

    total = s.own[...]
    for d in (1, 2, 3):
        xx = lax.rem(x + d, RING)
        arrived(s.xi.at[xx], s.xir.at[xx])
        total = total + s.xi[xx].astype(F32)
    for r in range(32):
        out_d[r] = total[r * STEPS : (r + 1) * STEPS, :].astype(BF16)

    for copy in kv_own + kv_on + [c for p in range(RING) for c in ay_own(p) + [ay_on(p)]]:
        copy.wait_send()
    for when, source, step_z, sem in q_first + q_second + q_third:

        @pl.when(when)
        def _(source=source, step_z=step_z, sem=sem):
            q_copy(source, step_z, sem).wait_send()
            a_copy(source, step_z, sem).wait_send()

    for d in range(RING):
        x_copy(d).wait_send()
        for copy in h_copies(d):
            copy.wait_send()
        if d:
            b_copy(d).wait_send()
            for copy in h2_copies(d):
                copy.wait_send()
            for copy in o_copies(d):
                copy.wait_send()
    for j in range(RING):
        si_copy(j).wait_send()

        @pl.when(turned(j) != x)
        def _(j=j):
            xi_copy(j).wait_send()


def shards(span_q, span_kv, prefix_kv, prefix_len, dec_q, dec_new_kv, dec_cache, cache_len, prompt_row, out_weight):
    vmem = pl.BlockSpec(memory_space=pltpu.VMEM)
    smem = pl.BlockSpec(memory_space=pltpu.SMEM)
    hbm = pl.BlockSpec(memory_space=pltpu.HBM)
    prefill, decode = pl.pallas_call(
        kernel,
        out_shape=(
            jax.ShapeDtypeStruct((SPAN, GQ * HD), BF16),
            jax.ShapeDtypeStruct((32, STEPS, COLS), BF16),
        ),
        in_specs=[smem] * 2 + [hbm] * 8,
        out_specs=(vmem, vmem),
        scratch_shapes=list(SCRATCH.values()),
        compiler_params=pltpu.CompilerParams(
            collective_id=0, has_side_effects=True, vmem_limit_bytes=VMEM_BYTES
        ),
        cost_estimate=pl.CostEstimate(flops=11_000_000_000, bytes_accessed=8_000_000, transcendentals=17_000_000),
    )(
        prefix_len,
        prompt_row,
        *[
            pltpu.with_memory_space_constraint(operand, pltpu.HBM)
            for operand in (
                cache_len,
                span_q[0],
                span_kv[0],
                prefix_kv[0],
                dec_q[0],
                dec_new_kv[0],
                dec_cache[0],
                out_weight,
            )
        ],
    )
    return prefill[None], decode[None]


def solution(mesh):
    placed = (
        P("grp", "ctx", "head"),
        P("grp", None, "ctx", "head"),
        P("grp", None, "ctx", "head"),
        P("grp"),
        P("grp", "ctx", None, "head"),
        P("grp", None, "ctx", None, "head"),
        P("grp", None, "ctx", None, "head"),
        P("grp", "ctx"),
        P("grp"),
        P("head", "ctx"),
    )
    return jax.shard_map(
        shards,
        mesh=mesh,
        in_specs=placed,
        out_specs=(P("grp", "ctx", "head"), P("grp", "head", None, "ctx")),
        check_vma=False,
    )
```

```python
import math

import jax
import jax.numpy as jnp
from jax import lax
from jax.experimental import pallas as pl
from jax.experimental.pallas import tpu as pltpu
from jax.sharding import PartitionSpec as P

HD = 128
GQ = 8
RING = 4
PRE = 896
SPAN = 128
KEYS = PRE + SPAN
ROWS = 16
STEPS = 4
SLOTS = 512
QROWS = STEPS * GQ
COLS = 512
MASKED = -1e30
LOG2E = math.log2(math.e)
SCALE = LOG2E / math.sqrt(HD)
MESH = pl.DeviceIdType.MESH
F32 = jnp.float32
BF16 = jnp.bfloat16
BLOCK = 512
VMEM_BYTES = 40 * 1024 * 1024

PIECES = (0, 2, 2, 2, 2, 3, 3, 3, 3, 1, 1, 1, 1, 0, 0, 0)
CHUNKS = (0, 0, 1, 2, 3, 0, 1, 2, 3, 0, 1, 2, 3, 1, 2, 3)


def dot_nt(a, b):
    return lax.dot_general(a, b, (((1,), (1,)), ((), ())), preferred_element_type=F32)


def dot_nn(a, b):
    return lax.dot_general(a, b, (((1,), (0,)), ((), ())), preferred_element_type=F32)


def log2(v):
    return jnp.log(v) * LOG2E


def iota(shape, axis):
    return lax.broadcasted_iota(jnp.int32, shape, axis)


def lookup(table, index):
    value = jnp.int32(table[0])
    for at, entry in enumerate(table[1:], 1):
        value = jnp.where(index == at, jnp.int32(entry), value)
    return value


def to_row(column):
    shape = column.shape
    return jnp.sum(jnp.where(iota(shape, 0) == iota(shape, 1), column, 0.0), axis=0, keepdims=True)


def to_column(row, count):
    shape = (count, HD)
    spread = jnp.broadcast_to(row, shape)
    return jnp.sum(jnp.where(iota(shape, 0) == iota(shape, 1), spread, 0.0), axis=1, keepdims=True)


def merge(parts):
    top = parts[0][1]
    for _, level in parts[1:]:
        top = jnp.maximum(top, level)
    weights = [jnp.exp2(level - top) for _, level in parts]
    total = weights[0]
    for w in weights[1:]:
        total = total + w
    mixed = parts[0][0] * weights[0]
    for (out, _), w in zip(parts[1:], weights[1:]):
        mixed = mixed + out * w
    return mixed / total, top + log2(total)


SCRATCH = {
    "kl": pltpu.VMEM((KEYS, HD), BF16),
    "kb": pltpu.VMEM((RING, 2 * HD, KEYS), BF16),
    "vb": pltpu.VMEM((RING, KEYS, HD), BF16),
    "qb": pltpu.VMEM((RING, GQ * SPAN, HD), BF16),
    "ts0": pltpu.VMEM((BLOCK, KEYS), F32),
    "ts1": pltpu.VMEM((BLOCK, KEYS), F32),
    "mx0": pltpu.VMEM((BLOCK, HD), F32),
    "mx1": pltpu.VMEM((BLOCK, HD), F32),
    "dq": pltpu.VMEM((ROWS, STEPS, GQ * HD), BF16),
    "nkv": pltpu.VMEM((2, ROWS, STEPS, HD), BF16),
    "acc": pltpu.VMEM((RING, GQ * SPAN, HD), F32),
    "top": pltpu.VMEM((RING, GQ * SPAN, HD), F32),
    "tot": pltpu.VMEM((RING, GQ * SPAN, HD), F32),
    "os": pltpu.VMEM((RING, GQ, SPAN, HD), BF16),
    "ls": pltpu.VMEM((RING, GQ, SPAN), F32),
    "orb": pltpu.VMEM((RING, GQ, SPAN, HD), BF16),
    "lrb": pltpu.VMEM((RING, GQ, SPAN), F32),
    "ck": pltpu.VMEM((ROWS, SLOTS, HD), BF16),
    "cv": pltpu.VMEM((ROWS, SLOTS, HD), BF16),
    "wb": pltpu.VMEM((GQ * HD, COLS), BF16),
    "qf": pltpu.VMEM((ROWS * QROWS, HD), F32),
    "kn": pltpu.VMEM((HD, HD), F32),
    "vn": pltpu.VMEM((HD, HD), F32),
    "of": pltpu.VMEM((ROWS * QROWS, HD), F32),
    "mf": pltpu.VMEM((ROWS * QROWS, HD), F32),
    "lf": pltpu.VMEM((ROWS * QROWS, HD), F32),
    "sb": pltpu.VMEM((RING, QROWS, HD), BF16),
    "sx": pltpu.VMEM((QROWS, HD), BF16),
    "xb": pltpu.VMEM((RING, QROWS, HD), BF16),
    "hos": pltpu.VMEM((QROWS, HD), BF16),
    "hls": pltpu.VMEM((8, HD), F32),
    "ho": pltpu.VMEM((RING, QROWS, HD), BF16),
    "hl": pltpu.VMEM((RING, 8, HD), F32),
    "sl": pltpu.VMEM((RING, 8, HD), F32),
    "ho2": pltpu.VMEM((RING, QROWS, HD), BF16),
    "hl2": pltpu.VMEM((RING, 16, HD), F32),
    "wt": pltpu.VMEM((2 * QROWS, HD), F32),
    "ot": pltpu.VMEM((2 * QROWS, HD), F32),
    "ab": pltpu.VMEM((RING, RING, GQ, ROWS * STEPS, HD), BF16),
    "am": pltpu.VMEM((RING * ROWS * STEPS, GQ * HD), BF16),
    "pr": pltpu.VMEM((RING * ROWS * STEPS, COLS), F32),
    "pm": pltpu.VMEM((RING, 128, COLS), F32),
    "so": pltpu.VMEM((RING, 128, COLS), BF16),
    "si": pltpu.VMEM((RING, 128, COLS), BF16),
    "xo": pltpu.VMEM((RING, 128, COLS), BF16),
    "xi": pltpu.VMEM((RING, 128, COLS), BF16),
    "own": pltpu.VMEM((128, COLS), F32),
    "clen": pltpu.SMEM((1, ROWS), jnp.int32),
    "loc": pltpu.SemaphoreType.DMA((18,)),
    "kvs": pltpu.SemaphoreType.DMA((6,)),
    "kr": pltpu.SemaphoreType.DMA((RING,)),
    "vr": pltpu.SemaphoreType.DMA((RING,)),
    "qs": pltpu.SemaphoreType.DMA((6,)),
    "qr": pltpu.SemaphoreType.DMA((RING,)),
    "bs": pltpu.SemaphoreType.DMA((RING,)),
    "br": pltpu.SemaphoreType.DMA((RING,)),
    "xs": pltpu.SemaphoreType.DMA((RING,)),
    "xr": pltpu.SemaphoreType.DMA((RING,)),
    "hs": pltpu.SemaphoreType.DMA((RING,)),
    "hr": pltpu.SemaphoreType.DMA((RING,)),
    "hls_s": pltpu.SemaphoreType.DMA((RING,)),
    "hlr": pltpu.SemaphoreType.DMA((RING,)),
    "sls": pltpu.SemaphoreType.DMA((RING,)),
    "slr": pltpu.SemaphoreType.DMA((RING,)),
    "h2s": pltpu.SemaphoreType.DMA((RING,)),
    "h2r": pltpu.SemaphoreType.DMA((RING,)),
    "hl2s": pltpu.SemaphoreType.DMA((RING,)),
    "hl2r": pltpu.SemaphoreType.DMA((RING,)),
    "as_": pltpu.SemaphoreType.DMA((6,)),
    "ar": pltpu.SemaphoreType.DMA((RING,)),
    "ays": pltpu.SemaphoreType.DMA((3 * RING,)),
    "ayr": pltpu.SemaphoreType.DMA((RING, RING)),
    "ops": pltpu.SemaphoreType.DMA((RING,)),
    "opr": pltpu.SemaphoreType.DMA((RING,)),
    "lps": pltpu.SemaphoreType.DMA((RING,)),
    "lpr": pltpu.SemaphoreType.DMA((RING,)),
    "sis": pltpu.SemaphoreType.DMA((RING,)),
    "sir": pltpu.SemaphoreType.DMA((RING,)),
    "xis": pltpu.SemaphoreType.DMA((RING,)),
    "xir": pltpu.SemaphoreType.DMA((RING,)),
}


class Names:
    pass


def kernel(plen, prow, clen_in, q_in, skv, pkv, dq, nkv, cache, w_in, out_p, out_d, *scratch):
    s = Names()
    for name, ref in zip(SCRATCH, scratch):
        setattr(s, name, ref)

    me = lax.axis_index("ctx")
    y, z = lax.div(me, RING), lax.rem(me, RING)
    head = lax.axis_index("head")
    x, core = lax.div(head, 2), lax.rem(head, 2)
    other = 1 - lax.axis_index("grp")

    def turned(j):
        return lax.rem(y + lax.div(j * (j + 1), 2), RING)

    def near(p):
        high = lax.rem(lax.div(z, 2) + lax.div(p, 2), 2)
        return 2 * high + lax.rem(z + p, 2)

    up, down, far = lax.rem(y + 1, RING), lax.rem(y + 3, RING), lax.rem(y + 2, RING)

    def at_y(yy):
        return {"ctx": yy * RING + z}

    def at_z(zz):
        return {"ctx": y * RING + zz}

    def across(zz):
        return {"ctx": y * RING + zz, "grp": other}

    def at_x(xx):
        return {"head": xx * 2 + core}

    sibling = {"head": x * 2 + 1 - core}

    def send(src, dst, ssem, rsem, device):
        return pltpu.make_async_remote_copy(
            src_ref=src, dst_ref=dst, send_sem=ssem, recv_sem=rsem, device_id=device, device_id_type=MESH
        )

    def arrived(dst, rsem):
        send(dst, dst, s.loc.at[0], rsem, sibling).wait_recv()

    pairs = [
        (pkv.at[0], s.kl.at[pl.ds(0, PRE)]),
        (skv.at[0], s.kl.at[pl.ds(PRE, SPAN)]),
        (pkv.at[1], s.vb.at[y, pl.ds(0, PRE)]),
        (skv.at[1], s.vb.at[y, pl.ds(PRE, SPAN)]),
    ]
    pairs += [(q_in.at[:, pl.ds(h * HD, HD)], s.qb.at[z, pl.ds(h * SPAN, SPAN)]) for h in range(GQ)]
    pairs += [(dq, s.dq), (nkv, s.nkv), (clen_in, s.clen), (cache.at[0], s.ck), (cache.at[1], s.cv), (w_in, s.wb)]
    loads = [pltpu.make_async_copy(src, dst, s.loc.at[at]) for at, (src, dst) in enumerate(pairs)]
    for load in loads:
        load.start()

    barrier = pltpu.get_barrier_semaphore()
    greeted = [at_y(lax.rem(y + d, RING)) for d in (1, 2, 3)] + [at_z(lax.rem(z + d, RING)) for d in (1, 2, 3)]
    greeted += [across(zz) for zz in range(RING)] + [sibling] + [at_x(lax.rem(x + d, RING)) for d in (1, 2, 3)]
    for device in greeted:
        pl.semaphore_signal(barrier, inc=1, device_id=device, device_id_type=MESH)

    def clear(p, carry):
        s.acc[p] = jnp.zeros((GQ * SPAN, HD), F32)
        s.tot[p] = jnp.zeros((GQ * SPAN, HD), F32)
        s.top[p] = jnp.full((GQ * SPAN, HD), MASKED, F32)
        slot = iota((HD, KEYS), 1)
        unused = ((p * RING + z) * PRE + slot >= plen[0]) & (slot < PRE) & (iota((HD, KEYS), 0) == 0)
        s.kb[p, HD : 2 * HD, :] = jnp.where(unused, MASKED, 0.0).astype(BF16)
        return carry

    lax.fori_loop(0, RING, clear, 0)


    for load in loads[2:12]:
        load.wait()
    pl.semaphore_wait(barrier, len(greeted))

    def keys_of(yy):
        return s.kb.at[yy, pl.ds(0, HD)]

    kv_own = [
        send(s.vb.at[y], s.vb.at[y], s.kvs.at[0], s.vr.at[y], at_y(up)),
        send(s.vb.at[y], s.vb.at[y], s.kvs.at[1], s.vr.at[y], at_y(down)),
        send(keys_of(y), keys_of(y), s.kvs.at[2], s.kr.at[y], at_y(up)),
        send(keys_of(y), keys_of(y), s.kvs.at[3], s.kr.at[y], at_y(down)),
    ]
    kv_on = [
        send(keys_of(down), keys_of(down), s.kvs.at[4], s.kr.at[down], at_y(up)),
        send(s.vb.at[up], s.vb.at[up], s.kvs.at[5], s.vr.at[up], at_y(down)),
    ]

    def q_copy(source, step, sem):
        return send(s.qb.at[source], s.qb.at[source], s.qs.at[sem], s.qr.at[source], at_z(z + step))

    def a_copy(source, step, sem):
        block = s.ab.at[y, source]
        return send(block, block, s.as_.at[sem], s.ar.at[source], at_z(z + step))

    q_first = [(z < 3, z, 1, 0), (z > 0, z, -1, 1)]
    q_second = [((z > 0) & (z < 3), z - 1, 1, 2), ((z > 0) & (z < 3), z + 1, -1, 3)]
    q_third = [(z == 2, z - 2, 1, 4), (z == 1, z + 2, -1, 5)]

    def z_start(copy, group):
        for when, source, step, sem in group:

            @pl.when(when)
            def _(source=source, step=step, sem=sem):
                copy(source, step, sem).start()

    def z_wait(block, sems, distance):
        @pl.when(z >= distance)
        def _():
            arrived(block(z - distance), sems.at[z - distance])

        @pl.when(z + distance < RING)
        def _():
            arrived(block(z + distance), sems.at[z + distance])

    def q_wait(distance):
        z_wait(lambda source: s.qb.at[source], s.qr, distance)

    def a_wait(distance):
        z_wait(lambda source: s.ab.at[y, source], s.ar, distance)

    def b_copy(d):
        return send(s.sb.at[y], s.sb.at[y], s.bs.at[d], s.br.at[y], at_y(lax.rem(y + d, RING)))

    for copy in kv_own[:2]:
        copy.start()
    z_start(q_copy, q_first)
    for load in loads[:2]:
        load.wait()
    s.kb[y, 0:HD, :] = s.kl[...].T
    for copy in kv_own[2:]:
        copy.start()

    for load in loads[12:15]:
        load.wait()
    for r in range(ROWS):
        row = s.dq[r].astype(F32)
        for h in range(GQ):
            s.qf[pl.ds(r * QROWS + h, STEPS, stride=GQ), :] = row[:, h * HD : (h + 1) * HD]
    s.kn[...] = jnp.zeros((HD, HD), F32)
    s.vn[...] = jnp.zeros((HD, HD), F32)
    for r in range(ROWS):
        s.kn[pl.ds(r * STEPS, STEPS), :] = s.nkv[0, r].astype(F32)
        s.vn[pl.ds(r * STEPS, STEPS), :] = s.nkv[1, r].astype(F32)

    def picked(ref):
        total = jnp.zeros((QROWS, HD), F32)
        for r in range(ROWS):
            mine = jnp.where(me * ROWS + r == prow[0], 1.0, 0.0)
            total = total + mine * ref[r * QROWS : (r + 1) * QROWS, :]
        return total

    s.sb[y] = picked(s.qf).astype(BF16)

    for d in (1, 2, 3):
        b_copy(d).start()

    lanes = (ROWS * QROWS, HD)
    at_row, at_key = iota(lanes, 0), iota(lanes, 1)
    same = lax.shift_right_logical(at_row, 5) == lax.shift_right_logical(at_key, 2)
    early = jnp.bitwise_and(at_key, 3) <= jnp.bitwise_and(lax.shift_right_logical(at_row, 3), 3)
    new = jnp.where(same & early, dot_nt(s.qf[...].astype(BF16), s.kn[...].astype(BF16)) * SCALE, MASKED)
    new_top = jnp.max(new, axis=1, keepdims=True)
    new_weights = jnp.exp2(new - new_top)
    s.mf[...] = jnp.broadcast_to(new_top, lanes)
    s.lf[...] = jnp.broadcast_to(jnp.sum(new_weights, axis=1, keepdims=True), lanes)
    s.of[...] = dot_nn(new_weights.astype(BF16), s.vn[...].astype(BF16))

    for load in loads[15:]:
        load.wait()

    def cached(r):
        rows = pl.ds(pl.multiple_of(r * QROWS, QROWS), QROWS)
        scores = dot_nt(s.qf[rows, :].astype(BF16), s.ck[r]) * SCALE
        scores = jnp.where(iota((QROWS, SLOTS), 1) < s.clen[0, r], scores, MASKED)
        before = s.mf[rows, :]
        after = jnp.maximum(before, jnp.max(scores, axis=1, keepdims=True))
        weights = jnp.exp2(scores - after[:, :1])
        keep = jnp.exp2(before - after)
        total = s.lf[rows, :] * keep + jnp.sum(weights, axis=1, keepdims=True)
        mixed = s.of[rows, :] * keep + dot_nn(weights.astype(BF16), s.cv[r])
        s.of[rows, :] = mixed / total
        s.lf[rows, :] = after + log2(total)

    def first_queries():
        q_wait(1)
        z_start(q_copy, q_second)

    def some_rows(i, carry):
        @pl.when(i == 1)
        def _():
            first_queries()
            arrived(s.vb.at[up], s.vr.at[up])
            kv_on[1].start()

        for u in range(8):
            cached(i * 8 + u)
        return carry

    lax.fori_loop(0, ROWS // 8, some_rows, 0)
    for h in range(GQ):
        s.ab[y, z, h] = s.of[pl.ds(h, ROWS * STEPS, stride=GQ), :].astype(BF16)

    def ay_copy(yy, p, sem, to):
        block = s.ab.at[yy, near(p)]
        return send(block, block, s.ays.at[sem], s.ayr.at[yy, near(p)], at_y(to))

    def ay_own(p):
        return [ay_copy(y, p, 3 * p, up), ay_copy(y, p, 3 * p + 1, down)]

    def ay_on(p):
        return ay_copy(down, p, 3 * p + 2, up) if p < 2 else ay_copy(up, p, 3 * p + 2, down)

    def rows_in(yy, p):
        arrived(s.ab.at[yy, near(p)], s.ayr.at[yy, near(p)])

    def spread_rows(p):
        if p:
            a_wait(p)
            z_start(a_copy, (q_second, q_third, [])[p - 1])
        for copy in ay_own(p):
            copy.start()

    def pass_rows(p):
        rows_in(down if p < 2 else up, p)
        ay_on(p).start()

    def rest_of_rows():
        for p in range(RING):
            rows_in(up if p < 2 else down, p)

    def far_rows():
        for p in range(RING):
            rows_in(far, p)

    z_start(a_copy, q_first)
    spread_rows(0)
    s.sl[z] = jnp.broadcast_to(to_row(picked(s.lf)), (8, HD))

    def x_copy(d):
        zz = lax.rem(z + d, RING)
        return send(s.sx, s.xb.at[z], s.xs.at[d], s.xr.at[z], across(zz))

    def pass_query():
        for d in (1, 2, 3):
            yy = lax.rem(y + d, RING)
            arrived(s.sb.at[yy], s.br.at[yy])
        total = s.sb[0].astype(F32)
        for yy in (1, 2, 3):
            total = total + s.sb[yy].astype(F32)
        s.sx[...] = total.astype(BF16)
        for d in range(RING):
            x_copy(d).start()

    def h_copies(d):
        zz = lax.rem(z + d, RING)
        copies = [
            send(s.hos, s.ho.at[z], s.hs.at[d], s.hr.at[z], across(zz)),
            send(s.hls, s.hl.at[z], s.hls_s.at[d], s.hlr.at[z], across(zz)),
        ]
        if d:
            copies.append(send(s.sl.at[z], s.sl.at[z], s.sls.at[d], s.slr.at[z], at_z(zz)))
        return copies

    def answer():
        for zz in range(RING):
            arrived(s.xb.at[zz], s.xr.at[zz])
        query = s.xb[0].astype(F32)
        for zz in (1, 2, 3):
            query = query + s.xb[zz].astype(F32)
        span = pl.ds(PRE, SPAN)
        scores = dot_nn(query.astype(BF16), s.kb[y, 0:HD, span]) * SCALE
        top = jnp.max(scores, axis=1, keepdims=True)
        weights = jnp.exp2(scores - top)
        total = jnp.sum(weights, axis=1, keepdims=True)
        s.hos[...] = (dot_nn(weights.astype(BF16), s.vb[y, span, :]) / total).astype(BF16)
        level = jnp.broadcast_to(top + log2(total), (QROWS, HD))
        s.hls[...] = jnp.broadcast_to(to_row(level), (8, HD))
        for d in range(RING):
            for copy in h_copies(d):
                copy.start()

    def h2_copies(d):
        yy = lax.rem(y + d, RING)
        return [
            send(s.ho2.at[y], s.ho2.at[y], s.h2s.at[d], s.h2r.at[y], at_y(yy)),
            send(s.hl2.at[y], s.hl2.at[y], s.hl2s.at[d], s.hl2r.at[y], at_y(yy)),
        ]

    def combine_z():
        for zz in range(RING):
            arrived(s.ho.at[zz], s.hr.at[zz])
            arrived(s.hl.at[zz], s.hlr.at[zz])
        for d in (1, 2, 3):
            zz = lax.rem(z + d, RING)
            arrived(s.sl.at[zz], s.slr.at[zz])
        out, level = merge([(s.ho[zz].astype(F32), to_column(s.hl[zz, 0:1, :], QROWS)) for zz in range(RING)])
        s.ho2[y] = out.astype(BF16)
        s.hl2[y, 0:8, :] = jnp.broadcast_to(to_row(jnp.broadcast_to(level, (QROWS, HD))), (8, HD))
        s.hl2[y, 8:16, :] = s.sl[0] + s.sl[1] + s.sl[2] + s.sl[3]
        for d in (1, 2, 3):
            for copy in h2_copies(d):
                copy.start()

    def combine_y():
        for d in (1, 2, 3):
            yy = lax.rem(y + d, RING)
            arrived(s.ho2.at[yy], s.h2r.at[yy])
            arrived(s.hl2.at[yy], s.hl2r.at[yy])
        out, level = merge([(s.ho2[yy].astype(F32), to_column(s.hl2[yy, 0:1, :], QROWS)) for yy in range(RING)])
        rows = s.hl2[0, 8:9, :] + s.hl2[1, 8:9, :] + s.hl2[2, 8:9, :] + s.hl2[3, 8:9, :]
        before = to_column(rows, QROWS)
        top = jnp.maximum(before, level)
        w_own, w_span = jnp.exp2(before - top), jnp.exp2(level - top)
        total = w_own + w_span
        keep = jnp.broadcast_to(w_own / total, (QROWS, HD))
        added = out * (w_span / total)
        for at in range(2):
            s.wt[pl.ds(at * QROWS, QROWS), :] = keep
            s.ot[pl.ds(at * QROWS, QROWS), :] = added

    def si_copy(j):
        return send(s.so.at[j], s.si.at[j], s.sis.at[j], s.sir.at[j], sibling)

    def project(j):
        yc = turned(j)
        count = RING * ROWS * STEPS
        row = yc * (RING * ROWS) + lax.shift_right_logical(iota((count, HD), 0), 2)
        hit = row == prow[0]
        for h in range(GQ):
            block = jnp.concatenate([s.ab[yc, zz, h] for zz in range(RING)], axis=0).astype(F32)
            keep = s.wt[pl.ds(h, 2 * STEPS, stride=GQ), :]
            added = s.ot[pl.ds(h, 2 * STEPS, stride=GQ), :]
            keep = jnp.concatenate([keep] * (count // (2 * STEPS)), axis=0)
            added = jnp.concatenate([added] * (count // (2 * STEPS)), axis=0)
            block = jnp.where(hit, block * keep + added, block)
            s.am[:, h * HD : (h + 1) * HD] = block.astype(BF16)
        s.pr[...] = dot_nn(s.am[...], s.wb[...])
        s.pm[j] = s.pr[pl.ds(pl.multiple_of(core * 128, 128), 128), :]
        s.so[j] = s.pr[pl.ds(pl.multiple_of((1 - core) * 128, 128), 128), :].astype(BF16)
        si_copy(j).start()

    def xi_copy(j):
        return send(s.xo.at[j], s.xi.at[x], s.xis.at[j], s.xir.at[x], at_x(turned(j)))

    def join(j):
        arrived(s.si.at[j], s.sir.at[j])
        total = s.pm[j] + s.si[j].astype(F32)

        @pl.when(turned(j) == x)
        def _():
            s.own[...] = total

        @pl.when(turned(j) != x)
        def _():
            s.xo[j] = total.astype(BF16)
            xi_copy(j).start()

    count = BLOCK // SPAN
    first_lane = jnp.where(iota((BLOCK, HD), 1) == 0, 1.0, 0.0).astype(BF16)
    ones = jnp.ones((KEYS, HD), BF16)

    def scores_of(at, b, held, peak):
        p, yc = lookup(PIECES, at), turned(lookup(CHUNKS, at))
        zq = near(p)
        late = (y * RING + zq) * SPAN - (yc * RING + z) * SPAN
        shape = (SPAN, SPAN)
        ahead = jnp.where(iota(shape, 1) - iota(shape, 0) <= late, 0.0, MASKED)
        ahead = jnp.concatenate([ahead] * count, axis=0)
        queries = jnp.concatenate([s.qb[zq, b * BLOCK : (b + 1) * BLOCK, :], first_lane], axis=1)
        scores = dot_nn(queries, s.kb[yc])
        highest = None
        for k in range(KEYS // HD):
            cols = slice(k * HD, (k + 1) * HD)
            part = scores[:, cols] * SCALE
            if k == PRE // HD:
                part = part + ahead
            held[:, cols] = part
            highest = part if highest is None else jnp.maximum(highest, part)
        peak[...] = jnp.broadcast_to(jnp.max(highest, axis=1, keepdims=True), (BLOCK, HD))

    def weigh(at, b, held, peak):
        p, yc = lookup(PIECES, at), turned(lookup(CHUNKS, at))
        rows = slice(b * BLOCK, (b + 1) * BLOCK)
        before = s.top[p, rows, :]
        after = jnp.maximum(before, peak[...])
        keep = jnp.exp2(before - after)
        packed = []
        for k in range(KEYS // HD):
            packed.append(jnp.exp2(held[:, k * HD : (k + 1) * HD] - after).astype(BF16))
        mixed = dot_nn(jnp.concatenate(packed, axis=1), jnp.concatenate([s.vb[yc], ones], axis=1))
        s.top[p, rows, :] = after
        s.tot[p, rows, :] = s.tot[p, rows, :] * keep + mixed[:, HD:]
        s.acc[p, rows, :] = s.acc[p, rows, :] * keep + mixed[:, :HD]

    def o_copies(p):
        return [
            send(s.os.at[p], s.orb.at[p], s.ops.at[p], s.opr.at[p], at_z(near(p))),
            send(s.ls.at[p], s.lrb.at[p], s.lps.at[p], s.lpr.at[p], at_z(near(p))),
        ]

    def each_head(one):
        def some(i, carry):
            for u in range(4):
                one(i * 4 + u)
            return carry

        lax.fori_loop(0, GQ // 4, some, 0)

    def ship(p):
        def one(h):
            rows = pl.ds(pl.multiple_of(h * SPAN, SPAN), SPAN)
            total = s.tot[p, rows, :]
            s.os[p, h] = (s.acc[p, rows, :] / total).astype(BF16)
            s.ls[p, pl.ds(h, 1), :] = to_row(s.top[p, rows, :] + log2(total))

        each_head(one)
        for copy in o_copies(p):
            copy.start()

    def settle():
        def one(h):
            rows = pl.ds(pl.multiple_of(h * SPAN, SPAN), SPAN)
            levels = [to_column(s.lrb[p, pl.ds(h, 1), :], SPAN) for p in (1, 2, 3)]
            top = s.top[0, rows, :]
            for level in levels:
                top = jnp.maximum(top, level)
            weight = jnp.exp2(s.top[0, rows, :] - top)
            total = s.tot[0, rows, :] * weight
            mixed = s.acc[0, rows, :] * weight
            for p, level in zip((1, 2, 3), levels):
                weight = jnp.exp2(level - top)
                total = total + weight
                mixed = mixed + s.orb[p, h].astype(F32) * weight
            out_p[:, pl.ds(pl.multiple_of(h * HD, HD), HD)] = (mixed / total).astype(BF16)

        each_head(one)

    def pass_keys():
        arrived(keys_of(down), s.kr.at[down])
        kv_on[0].start()

    def keys_near():
        arrived(s.vb.at[down], s.vr.at[down])
        arrived(keys_of(up), s.kr.at[up])

    def keys_far():
        arrived(keys_of(far), s.kr.at[far])
        arrived(s.vb.at[far], s.vr.at[far])

    def second_queries():
        q_wait(2)
        z_start(q_copy, q_third)

    actions = {
        0: [pass_query],
        1: [second_queries, pass_keys],
        2: [keys_near],
        3: [lambda: spread_rows(1), answer],
        4: [keys_far, lambda: pass_rows(0)],
        5: [lambda: q_wait(3), lambda: spread_rows(2)],
        6: [combine_z, lambda: pass_rows(1)],
        7: [lambda: spread_rows(3)],
        8: [combine_y, lambda: pass_rows(2)],
        9: [lambda: pass_rows(3)],
        13: [rest_of_rows],
        16: [far_rows],
    }

    def prepare(i):
        for at, todo in actions.items():

            @pl.when(i == at)
            def _(todo=todo):
                for action in todo:
                    action()

        @pl.when((i == 10) | (i == 14) | (i == 16))
        def _():
            join(lax.div(jnp.maximum(i - 12, 0), 2))

        @pl.when((i == 9) | (i == 13) | (i == 14) | (i == 16))
        def _():
            project(jnp.minimum(jnp.maximum(i - 12, 0), 3))

    def step(i, carry):
        scores_of(i, 1, s.ts1, s.mx1)
        weigh(i, 0, s.ts0, s.mx0)
        prepare(i + 1)
        scores_of(jnp.minimum(i + 1, 15), 0, s.ts0, s.mx0)
        weigh(i, 1, s.ts1, s.mx1)
        p, k = lookup(PIECES, i), lookup(CHUNKS, i)

        @pl.when((k == 3) & (p > 0))
        def _():
            ship(p)

        return carry

    for action in actions.pop(0):
        action()
    scores_of(0, 0, s.ts0, s.mx0)
    lax.fori_loop(0, 16, step, 0)
    join(RING - 1)
    for p in (1, 2, 3):
        arrived(s.orb.at[p], s.opr.at[p])
        arrived(s.lrb.at[p], s.lpr.at[p])
    settle()

    total = s.own[...]
    for d in (1, 2, 3):
        xx = lax.rem(x + d, RING)
        arrived(s.xi.at[xx], s.xir.at[xx])
        total = total + s.xi[xx].astype(F32)
    for r in range(32):
        out_d[r] = total[r * STEPS : (r + 1) * STEPS, :].astype(BF16)

    for copy in kv_own + kv_on + [c for p in range(RING) for c in ay_own(p) + [ay_on(p)]]:
        copy.wait_send()
    for when, source, step_z, sem in q_first + q_second + q_third:

        @pl.when(when)
        def _(source=source, step_z=step_z, sem=sem):
            q_copy(source, step_z, sem).wait_send()
            a_copy(source, step_z, sem).wait_send()

    for d in range(RING):
        x_copy(d).wait_send()
        for copy in h_copies(d):
            copy.wait_send()
        if d:
            b_copy(d).wait_send()
            for copy in h2_copies(d):
                copy.wait_send()
            for copy in o_copies(d):
                copy.wait_send()
    for j in range(RING):
        si_copy(j).wait_send()

        @pl.when(turned(j) != x)
        def _(j=j):
            xi_copy(j).wait_send()


def shards(span_q, span_kv, prefix_kv, prefix_len, dec_q, dec_new_kv, dec_cache, cache_len, prompt_row, out_weight):
    vmem = pl.BlockSpec(memory_space=pltpu.VMEM)
    smem = pl.BlockSpec(memory_space=pltpu.SMEM)
    hbm = pl.BlockSpec(memory_space=pltpu.HBM)
    prefill, decode = pl.pallas_call(
        kernel,
        out_shape=(
            jax.ShapeDtypeStruct((SPAN, GQ * HD), BF16),
            jax.ShapeDtypeStruct((32, STEPS, COLS), BF16),
        ),
        in_specs=[smem] * 2 + [hbm] * 8,
        out_specs=(vmem, vmem),
        scratch_shapes=list(SCRATCH.values()),
        compiler_params=pltpu.CompilerParams(
            collective_id=0, has_side_effects=True, vmem_limit_bytes=VMEM_BYTES
        ),
        cost_estimate=pl.CostEstimate(flops=11_000_000_000, bytes_accessed=8_000_000, transcendentals=17_000_000),
    )(
        prefix_len,
        prompt_row,
        *[
            pltpu.with_memory_space_constraint(operand, pltpu.HBM)
            for operand in (
                cache_len,
                span_q[0],
                span_kv[0],
                prefix_kv[0],
                dec_q[0],
                dec_new_kv[0],
                dec_cache[0],
                out_weight,
            )
        ],
    )
    return prefill[None], decode[None]


def solution(mesh):
    placed = (
        P("grp", "ctx", "head"),
        P("grp", None, "ctx", "head"),
        P("grp", None, "ctx", "head"),
        P("grp"),
        P("grp", "ctx", None, "head"),
        P("grp", None, "ctx", None, "head"),
        P("grp", None, "ctx", None, "head"),
        P("grp", "ctx"),
        P("grp"),
        P("head", "ctx"),
    )
    return jax.shard_map(
        shards,
        mesh=mesh,
        in_specs=placed,
        out_specs=(P("grp", "ctx", "head"), P("grp", "head", None, "ctx")),
        check_vma=False,
    )
```

```python
import math

import jax
import jax.numpy as jnp
from jax import lax
from jax.experimental import pallas as pl
from jax.experimental.pallas import tpu as pltpu
from jax.sharding import PartitionSpec as P

HD = 128
GQ = 8
RING = 4
PRE = 896
SPAN = 128
KEYS = PRE + SPAN
ROWS = 16
STEPS = 4
SLOTS = 512
QROWS = STEPS * GQ
COLS = 512
MASKED = -1e30
LOG2E = math.log2(math.e)
SCALE = LOG2E / math.sqrt(HD)
MESH = pl.DeviceIdType.MESH
F32 = jnp.float32
BF16 = jnp.bfloat16
BLOCK = 512
VMEM_BYTES = 40 * 1024 * 1024

PIECES = (0, 1, 2, 2, 2, 2, 3, 3, 3, 3, 1, 1, 1, 0, 0, 0)
CHUNKS = (0, 0, 0, 1, 2, 3, 0, 1, 2, 3, 1, 2, 3, 1, 2, 3)


def dot_nt(a, b):
    return lax.dot_general(a, b, (((1,), (1,)), ((), ())), preferred_element_type=F32)


def dot_nn(a, b):
    return lax.dot_general(a, b, (((1,), (0,)), ((), ())), preferred_element_type=F32)


def log2(v):
    return jnp.log(v) * LOG2E


def iota(shape, axis):
    return lax.broadcasted_iota(jnp.int32, shape, axis)


def lookup(table, index):
    value = jnp.int32(table[0])
    for at, entry in enumerate(table[1:], 1):
        value = jnp.where(index == at, jnp.int32(entry), value)
    return value


def to_row(column):
    shape = column.shape
    return jnp.sum(jnp.where(iota(shape, 0) == iota(shape, 1), column, 0.0), axis=0, keepdims=True)


def to_column(row, count):
    shape = (count, HD)
    spread = jnp.broadcast_to(row, shape)
    return jnp.sum(jnp.where(iota(shape, 0) == iota(shape, 1), spread, 0.0), axis=1, keepdims=True)


def merge(parts):
    top = parts[0][1]
    for _, level in parts[1:]:
        top = jnp.maximum(top, level)
    weights = [jnp.exp2(level - top) for _, level in parts]
    total = weights[0]
    for w in weights[1:]:
        total = total + w
    mixed = parts[0][0] * weights[0]
    for (out, _), w in zip(parts[1:], weights[1:]):
        mixed = mixed + out * w
    return mixed / total, top + log2(total)


SCRATCH = {
    "kl": pltpu.VMEM((KEYS, HD), BF16),
    "kb": pltpu.VMEM((RING, 2 * HD, KEYS), BF16),
    "vb": pltpu.VMEM((RING, KEYS, HD), BF16),
    "qb": pltpu.VMEM((RING, GQ * SPAN, HD), BF16),
    "ts0": pltpu.VMEM((BLOCK, KEYS), F32),
    "ts1": pltpu.VMEM((BLOCK, KEYS), F32),
    "mx0": pltpu.VMEM((BLOCK, HD), F32),
    "mx1": pltpu.VMEM((BLOCK, HD), F32),
    "dq": pltpu.VMEM((ROWS, STEPS, GQ * HD), BF16),
    "nkv": pltpu.VMEM((2, ROWS, STEPS, HD), BF16),
    "acc": pltpu.VMEM((RING, GQ * SPAN, HD), F32),
    "top": pltpu.VMEM((RING, GQ * SPAN, HD), F32),
    "tot": pltpu.VMEM((RING, GQ * SPAN, HD), F32),
    "os": pltpu.VMEM((RING, GQ, SPAN, HD), BF16),
    "ls": pltpu.VMEM((RING, GQ, SPAN), F32),
    "orb": pltpu.VMEM((RING, GQ, SPAN, HD), BF16),
    "lrb": pltpu.VMEM((RING, GQ, SPAN), F32),
    "ck": pltpu.VMEM((ROWS, SLOTS, HD), BF16),
    "cv": pltpu.VMEM((ROWS, SLOTS, HD), BF16),
    "wb": pltpu.VMEM((GQ * HD, COLS), BF16),
    "qf": pltpu.VMEM((ROWS * QROWS, HD), F32),
    "kn": pltpu.VMEM((HD, HD), F32),
    "vn": pltpu.VMEM((HD, HD), F32),
    "of": pltpu.VMEM((ROWS * QROWS, HD), F32),
    "mf": pltpu.VMEM((ROWS * QROWS, HD), F32),
    "lf": pltpu.VMEM((ROWS * QROWS, HD), F32),
    "sb": pltpu.VMEM((RING, QROWS, HD), BF16),
    "sx": pltpu.VMEM((QROWS, HD), BF16),
    "xb": pltpu.VMEM((RING, QROWS, HD), BF16),
    "hos": pltpu.VMEM((QROWS, HD), BF16),
    "hls": pltpu.VMEM((8, HD), F32),
    "ho": pltpu.VMEM((RING, QROWS, HD), BF16),
    "hl": pltpu.VMEM((RING, 8, HD), F32),
    "sl": pltpu.VMEM((RING, 8, HD), F32),
    "ho2": pltpu.VMEM((RING, QROWS, HD), BF16),
    "hl2": pltpu.VMEM((RING, 16, HD), F32),
    "wt": pltpu.VMEM((2 * QROWS, HD), F32),
    "ot": pltpu.VMEM((2 * QROWS, HD), F32),
    "ab": pltpu.VMEM((RING, RING, GQ, ROWS * STEPS, HD), BF16),
    "am": pltpu.VMEM((RING * ROWS * STEPS, GQ * HD), BF16),
    "pr": pltpu.VMEM((RING * ROWS * STEPS, COLS), F32),
    "pm": pltpu.VMEM((RING, 128, COLS), F32),
    "so": pltpu.VMEM((RING, 128, COLS), BF16),
    "si": pltpu.VMEM((RING, 128, COLS), BF16),
    "xo": pltpu.VMEM((RING, 128, COLS), BF16),
    "xi": pltpu.VMEM((RING, 128, COLS), BF16),
    "own": pltpu.VMEM((128, COLS), F32),
    "clen": pltpu.SMEM((1, ROWS), jnp.int32),
    "loc": pltpu.SemaphoreType.DMA((18,)),
    "kvs": pltpu.SemaphoreType.DMA((6,)),
    "kr": pltpu.SemaphoreType.DMA((RING,)),
    "vr": pltpu.SemaphoreType.DMA((RING,)),
    "qs": pltpu.SemaphoreType.DMA((6,)),
    "qr": pltpu.SemaphoreType.DMA((RING,)),
    "bs": pltpu.SemaphoreType.DMA((RING,)),
    "br": pltpu.SemaphoreType.DMA((RING,)),
    "xs": pltpu.SemaphoreType.DMA((RING,)),
    "xr": pltpu.SemaphoreType.DMA((RING,)),
    "hs": pltpu.SemaphoreType.DMA((RING,)),
    "hr": pltpu.SemaphoreType.DMA((RING,)),
    "hls_s": pltpu.SemaphoreType.DMA((RING,)),
    "hlr": pltpu.SemaphoreType.DMA((RING,)),
    "sls": pltpu.SemaphoreType.DMA((RING,)),
    "slr": pltpu.SemaphoreType.DMA((RING,)),
    "h2s": pltpu.SemaphoreType.DMA((RING,)),
    "h2r": pltpu.SemaphoreType.DMA((RING,)),
    "hl2s": pltpu.SemaphoreType.DMA((RING,)),
    "hl2r": pltpu.SemaphoreType.DMA((RING,)),
    "as_": pltpu.SemaphoreType.DMA((6,)),
    "ar": pltpu.SemaphoreType.DMA((RING,)),
    "ays": pltpu.SemaphoreType.DMA((3 * RING,)),
    "ayr": pltpu.SemaphoreType.DMA((RING, RING)),
    "ops": pltpu.SemaphoreType.DMA((RING,)),
    "opr": pltpu.SemaphoreType.DMA((RING,)),
    "lps": pltpu.SemaphoreType.DMA((RING,)),
    "lpr": pltpu.SemaphoreType.DMA((RING,)),
    "sis": pltpu.SemaphoreType.DMA((RING,)),
    "sir": pltpu.SemaphoreType.DMA((RING,)),
    "xis": pltpu.SemaphoreType.DMA((RING,)),
    "xir": pltpu.SemaphoreType.DMA((RING,)),
}


class Names:
    pass


def kernel(plen, prow, clen_in, q_in, skv, pkv, dq, nkv, cache, w_in, out_p, out_d, *scratch):
    s = Names()
    for name, ref in zip(SCRATCH, scratch):
        setattr(s, name, ref)

    me = lax.axis_index("ctx")
    y, z = lax.div(me, RING), lax.rem(me, RING)
    head = lax.axis_index("head")
    x, core = lax.div(head, 2), lax.rem(head, 2)
    other = 1 - lax.axis_index("grp")

    def turned(j):
        return lax.rem(y + lax.div(j * (j + 1), 2), RING)

    def near(p):
        high = lax.rem(lax.div(z, 2) + lax.div(p, 2), 2)
        return 2 * high + lax.rem(z + p, 2)

    up, down, far = lax.rem(y + 1, RING), lax.rem(y + 3, RING), lax.rem(y + 2, RING)

    def at_y(yy):
        return {"ctx": yy * RING + z}

    def at_z(zz):
        return {"ctx": y * RING + zz}

    def across(zz):
        return {"ctx": y * RING + zz, "grp": other}

    def at_x(xx):
        return {"head": xx * 2 + core}

    sibling = {"head": x * 2 + 1 - core}

    def send(src, dst, ssem, rsem, device):
        return pltpu.make_async_remote_copy(
            src_ref=src, dst_ref=dst, send_sem=ssem, recv_sem=rsem, device_id=device, device_id_type=MESH
        )

    def arrived(dst, rsem):
        send(dst, dst, s.loc.at[0], rsem, sibling).wait_recv()

    pairs = [
        (pkv.at[0], s.kl.at[pl.ds(0, PRE)]),
        (skv.at[0], s.kl.at[pl.ds(PRE, SPAN)]),
        (pkv.at[1], s.vb.at[y, pl.ds(0, PRE)]),
        (skv.at[1], s.vb.at[y, pl.ds(PRE, SPAN)]),
    ]
    pairs += [(q_in.at[:, pl.ds(h * HD, HD)], s.qb.at[z, pl.ds(h * SPAN, SPAN)]) for h in range(GQ)]
    pairs += [(dq, s.dq), (nkv, s.nkv), (clen_in, s.clen), (cache.at[0], s.ck), (cache.at[1], s.cv), (w_in, s.wb)]
    loads = [pltpu.make_async_copy(src, dst, s.loc.at[at]) for at, (src, dst) in enumerate(pairs)]
    for load in loads:
        load.start()

    barrier = pltpu.get_barrier_semaphore()
    greeted = [at_y(lax.rem(y + d, RING)) for d in (1, 2, 3)] + [at_z(lax.rem(z + d, RING)) for d in (1, 2, 3)]
    greeted += [across(zz) for zz in range(RING)] + [sibling] + [at_x(lax.rem(x + d, RING)) for d in (1, 2, 3)]
    for device in greeted:
        pl.semaphore_signal(barrier, inc=1, device_id=device, device_id_type=MESH)

    def clear(p, carry):
        s.acc[p] = jnp.zeros((GQ * SPAN, HD), F32)
        s.tot[p] = jnp.zeros((GQ * SPAN, HD), F32)
        s.top[p] = jnp.full((GQ * SPAN, HD), MASKED, F32)
        slot = iota((HD, KEYS), 1)
        unused = ((p * RING + z) * PRE + slot >= plen[0]) & (slot < PRE) & (iota((HD, KEYS), 0) == 0)
        s.kb[p, HD : 2 * HD, :] = jnp.where(unused, MASKED, 0.0).astype(BF16)
        return carry

    lax.fori_loop(0, RING, clear, 0)


    for load in loads[2:12]:
        load.wait()
    pl.semaphore_wait(barrier, len(greeted))

    def keys_of(yy):
        return s.kb.at[yy, pl.ds(0, HD)]

    kv_own = [
        send(s.vb.at[y], s.vb.at[y], s.kvs.at[0], s.vr.at[y], at_y(up)),
        send(s.vb.at[y], s.vb.at[y], s.kvs.at[1], s.vr.at[y], at_y(down)),
        send(keys_of(y), keys_of(y), s.kvs.at[2], s.kr.at[y], at_y(up)),
        send(keys_of(y), keys_of(y), s.kvs.at[3], s.kr.at[y], at_y(down)),
    ]
    kv_on = [
        send(keys_of(down), keys_of(down), s.kvs.at[4], s.kr.at[down], at_y(up)),
        send(s.vb.at[up], s.vb.at[up], s.kvs.at[5], s.vr.at[up], at_y(down)),
    ]

    def q_copy(source, step, sem):
        return send(s.qb.at[source], s.qb.at[source], s.qs.at[sem], s.qr.at[source], at_z(z + step))

    def a_copy(source, step, sem):
        block = s.ab.at[y, source]
        return send(block, block, s.as_.at[sem], s.ar.at[source], at_z(z + step))

    q_first = [(z < 3, z, 1, 0), (z > 0, z, -1, 1)]
    q_second = [((z > 0) & (z < 3), z - 1, 1, 2), ((z > 0) & (z < 3), z + 1, -1, 3)]
    q_third = [(z == 2, z - 2, 1, 4), (z == 1, z + 2, -1, 5)]

    def z_start(copy, group):
        for when, source, step, sem in group:

            @pl.when(when)
            def _(source=source, step=step, sem=sem):
                copy(source, step, sem).start()

    def z_wait(block, sems, distance):
        @pl.when(z >= distance)
        def _():
            arrived(block(z - distance), sems.at[z - distance])

        @pl.when(z + distance < RING)
        def _():
            arrived(block(z + distance), sems.at[z + distance])

    def q_wait(distance):
        z_wait(lambda source: s.qb.at[source], s.qr, distance)

    def a_wait(distance):
        z_wait(lambda source: s.ab.at[y, source], s.ar, distance)

    def b_copy(d):
        return send(s.sb.at[y], s.sb.at[y], s.bs.at[d], s.br.at[y], at_y(lax.rem(y + d, RING)))

    for copy in kv_own[:2]:
        copy.start()
    z_start(q_copy, q_first)
    for load in loads[:2]:
        load.wait()
    s.kb[y, 0:HD, :] = s.kl[...].T
    for copy in kv_own[2:]:
        copy.start()

    for load in loads[12:15]:
        load.wait()
    for r in range(ROWS):
        row = s.dq[r].astype(F32)
        for h in range(GQ):
            s.qf[pl.ds(r * QROWS + h, STEPS, stride=GQ), :] = row[:, h * HD : (h + 1) * HD]
    s.kn[...] = jnp.zeros((HD, HD), F32)
    s.vn[...] = jnp.zeros((HD, HD), F32)
    for r in range(ROWS):
        s.kn[pl.ds(r * STEPS, STEPS), :] = s.nkv[0, r].astype(F32)
        s.vn[pl.ds(r * STEPS, STEPS), :] = s.nkv[1, r].astype(F32)

    def picked(ref):
        total = jnp.zeros((QROWS, HD), F32)
        for r in range(ROWS):
            mine = jnp.where(me * ROWS + r == prow[0], 1.0, 0.0)
            total = total + mine * ref[r * QROWS : (r + 1) * QROWS, :]
        return total

    s.sb[y] = picked(s.qf).astype(BF16)

    for d in (1, 2, 3):
        b_copy(d).start()

    lanes = (ROWS * QROWS, HD)
    at_row, at_key = iota(lanes, 0), iota(lanes, 1)
    same = lax.shift_right_logical(at_row, 5) == lax.shift_right_logical(at_key, 2)
    early = jnp.bitwise_and(at_key, 3) <= jnp.bitwise_and(lax.shift_right_logical(at_row, 3), 3)
    new = jnp.where(same & early, dot_nt(s.qf[...].astype(BF16), s.kn[...].astype(BF16)) * SCALE, MASKED)
    new_top = jnp.max(new, axis=1, keepdims=True)
    new_weights = jnp.exp2(new - new_top)
    s.mf[...] = jnp.broadcast_to(new_top, lanes)
    s.lf[...] = jnp.broadcast_to(jnp.sum(new_weights, axis=1, keepdims=True), lanes)
    s.of[...] = dot_nn(new_weights.astype(BF16), s.vn[...].astype(BF16))

    for load in loads[15:]:
        load.wait()

    def cached(r):
        rows = pl.ds(pl.multiple_of(r * QROWS, QROWS), QROWS)
        scores = dot_nt(s.qf[rows, :].astype(BF16), s.ck[r]) * SCALE
        scores = jnp.where(iota((QROWS, SLOTS), 1) < s.clen[0, r], scores, MASKED)
        before = s.mf[rows, :]
        after = jnp.maximum(before, jnp.max(scores, axis=1, keepdims=True))
        weights = jnp.exp2(scores - after[:, :1])
        keep = jnp.exp2(before - after)
        total = s.lf[rows, :] * keep + jnp.sum(weights, axis=1, keepdims=True)
        mixed = s.of[rows, :] * keep + dot_nn(weights.astype(BF16), s.cv[r])
        s.of[rows, :] = mixed / total
        s.lf[rows, :] = after + log2(total)

    def first_queries():
        q_wait(1)
        z_start(q_copy, q_second)

    def some_rows(i, carry):
        for u in range(8):
            cached(i * 8 + u)
        return carry

    lax.fori_loop(0, ROWS // 8, some_rows, 0)
    for h in range(GQ):
        s.ab[y, z, h] = s.of[pl.ds(h, ROWS * STEPS, stride=GQ), :].astype(BF16)

    def ay_copy(yy, p, sem, to):
        block = s.ab.at[yy, near(p)]
        return send(block, block, s.ays.at[sem], s.ayr.at[yy, near(p)], at_y(to))

    def ay_own(p):
        return [ay_copy(y, p, 3 * p, up), ay_copy(y, p, 3 * p + 1, down)]

    def ay_on(p):
        return ay_copy(down, p, 3 * p + 2, up) if p < 2 else ay_copy(up, p, 3 * p + 2, down)

    def rows_in(yy, p):
        arrived(s.ab.at[yy, near(p)], s.ayr.at[yy, near(p)])

    def spread_rows(p):
        if p:
            a_wait(p)
            z_start(a_copy, (q_second, q_third, [])[p - 1])
        for copy in ay_own(p):
            copy.start()

    def pass_rows(p):
        rows_in(down if p < 2 else up, p)
        ay_on(p).start()

    def rest_of_rows():
        for p in range(RING):
            rows_in(up if p < 2 else down, p)

    def far_rows():
        for p in range(RING):
            rows_in(far, p)

    z_start(a_copy, q_first)
    spread_rows(0)
    s.sl[z] = jnp.broadcast_to(to_row(picked(s.lf)), (8, HD))

    def x_copy(d):
        zz = lax.rem(z + d, RING)
        return send(s.sx, s.xb.at[z], s.xs.at[d], s.xr.at[z], across(zz))

    def pass_query():
        for d in (1, 2, 3):
            yy = lax.rem(y + d, RING)
            arrived(s.sb.at[yy], s.br.at[yy])
        total = s.sb[0].astype(F32)
        for yy in (1, 2, 3):
            total = total + s.sb[yy].astype(F32)
        s.sx[...] = total.astype(BF16)
        for d in range(RING):
            x_copy(d).start()

    def h_copies(d):
        zz = lax.rem(z + d, RING)
        copies = [
            send(s.hos, s.ho.at[z], s.hs.at[d], s.hr.at[z], across(zz)),
            send(s.hls, s.hl.at[z], s.hls_s.at[d], s.hlr.at[z], across(zz)),
        ]
        if d:
            copies.append(send(s.sl.at[z], s.sl.at[z], s.sls.at[d], s.slr.at[z], at_z(zz)))
        return copies

    def answer():
        for zz in range(RING):
            arrived(s.xb.at[zz], s.xr.at[zz])
        query = s.xb[0].astype(F32)
        for zz in (1, 2, 3):
            query = query + s.xb[zz].astype(F32)
        span = pl.ds(PRE, SPAN)
        scores = dot_nn(query.astype(BF16), s.kb[y, 0:HD, span]) * SCALE
        top = jnp.max(scores, axis=1, keepdims=True)
        weights = jnp.exp2(scores - top)
        total = jnp.sum(weights, axis=1, keepdims=True)
        s.hos[...] = (dot_nn(weights.astype(BF16), s.vb[y, span, :]) / total).astype(BF16)
        level = jnp.broadcast_to(top + log2(total), (QROWS, HD))
        s.hls[...] = jnp.broadcast_to(to_row(level), (8, HD))
        for d in range(RING):
            for copy in h_copies(d):
                copy.start()

    def h2_copies(d):
        yy = lax.rem(y + d, RING)
        return [
            send(s.ho2.at[y], s.ho2.at[y], s.h2s.at[d], s.h2r.at[y], at_y(yy)),
            send(s.hl2.at[y], s.hl2.at[y], s.hl2s.at[d], s.hl2r.at[y], at_y(yy)),
        ]

    def combine_z():
        for zz in range(RING):
            arrived(s.ho.at[zz], s.hr.at[zz])
            arrived(s.hl.at[zz], s.hlr.at[zz])
        for d in (1, 2, 3):
            zz = lax.rem(z + d, RING)
            arrived(s.sl.at[zz], s.slr.at[zz])
        out, level = merge([(s.ho[zz].astype(F32), to_column(s.hl[zz, 0:1, :], QROWS)) for zz in range(RING)])
        s.ho2[y] = out.astype(BF16)
        s.hl2[y, 0:8, :] = jnp.broadcast_to(to_row(jnp.broadcast_to(level, (QROWS, HD))), (8, HD))
        s.hl2[y, 8:16, :] = s.sl[0] + s.sl[1] + s.sl[2] + s.sl[3]
        for d in (1, 2, 3):
            for copy in h2_copies(d):
                copy.start()

    def combine_y():
        for d in (1, 2, 3):
            yy = lax.rem(y + d, RING)
            arrived(s.ho2.at[yy], s.h2r.at[yy])
            arrived(s.hl2.at[yy], s.hl2r.at[yy])
        out, level = merge([(s.ho2[yy].astype(F32), to_column(s.hl2[yy, 0:1, :], QROWS)) for yy in range(RING)])
        rows = s.hl2[0, 8:9, :] + s.hl2[1, 8:9, :] + s.hl2[2, 8:9, :] + s.hl2[3, 8:9, :]
        before = to_column(rows, QROWS)
        top = jnp.maximum(before, level)
        w_own, w_span = jnp.exp2(before - top), jnp.exp2(level - top)
        total = w_own + w_span
        keep = jnp.broadcast_to(w_own / total, (QROWS, HD))
        added = out * (w_span / total)
        for at in range(2):
            s.wt[pl.ds(at * QROWS, QROWS), :] = keep
            s.ot[pl.ds(at * QROWS, QROWS), :] = added

    def si_copy(j):
        return send(s.so.at[j], s.si.at[j], s.sis.at[j], s.sir.at[j], sibling)

    def project(j):
        yc = turned(j)
        count = RING * ROWS * STEPS
        row = yc * (RING * ROWS) + lax.shift_right_logical(iota((count, HD), 0), 2)
        hit = row == prow[0]
        for h in range(GQ):
            block = jnp.concatenate([s.ab[yc, zz, h] for zz in range(RING)], axis=0).astype(F32)
            keep = s.wt[pl.ds(h, 2 * STEPS, stride=GQ), :]
            added = s.ot[pl.ds(h, 2 * STEPS, stride=GQ), :]
            keep = jnp.concatenate([keep] * (count // (2 * STEPS)), axis=0)
            added = jnp.concatenate([added] * (count // (2 * STEPS)), axis=0)
            block = jnp.where(hit, block * keep + added, block)
            s.am[:, h * HD : (h + 1) * HD] = block.astype(BF16)
        s.pr[...] = dot_nn(s.am[...], s.wb[...])
        s.pm[j] = s.pr[pl.ds(pl.multiple_of(core * 128, 128), 128), :]
        s.so[j] = s.pr[pl.ds(pl.multiple_of((1 - core) * 128, 128), 128), :].astype(BF16)
        si_copy(j).start()

    def xi_copy(j):
        return send(s.xo.at[j], s.xi.at[x], s.xis.at[j], s.xir.at[x], at_x(turned(j)))

    def join(j):
        arrived(s.si.at[j], s.sir.at[j])
        total = s.pm[j] + s.si[j].astype(F32)

        @pl.when(turned(j) == x)
        def _():
            s.own[...] = total

        @pl.when(turned(j) != x)
        def _():
            s.xo[j] = total.astype(BF16)
            xi_copy(j).start()

    count = BLOCK // SPAN
    first_lane = jnp.where(iota((BLOCK, HD), 1) == 0, 1.0, 0.0).astype(BF16)
    ones = jnp.ones((KEYS, HD), BF16)

    def scores_of(at, b, held, peak):
        p, yc = lookup(PIECES, at), turned(lookup(CHUNKS, at))
        zq = near(p)
        late = (y * RING + zq) * SPAN - (yc * RING + z) * SPAN
        shape = (SPAN, SPAN)
        ahead = jnp.where(iota(shape, 1) - iota(shape, 0) <= late, 0.0, MASKED)
        ahead = jnp.concatenate([ahead] * count, axis=0)
        queries = jnp.concatenate([s.qb[zq, b * BLOCK : (b + 1) * BLOCK, :], first_lane], axis=1)
        scores = dot_nn(queries, s.kb[yc])
        highest = None
        for k in range(KEYS // HD):
            cols = slice(k * HD, (k + 1) * HD)
            part = scores[:, cols] * SCALE
            if k == PRE // HD:
                part = part + ahead
            held[:, cols] = part
            highest = part if highest is None else jnp.maximum(highest, part)
        peak[...] = jnp.broadcast_to(jnp.max(highest, axis=1, keepdims=True), (BLOCK, HD))

    def weigh(at, b, held, peak):
        p, yc = lookup(PIECES, at), turned(lookup(CHUNKS, at))
        rows = slice(b * BLOCK, (b + 1) * BLOCK)
        before = s.top[p, rows, :]
        after = jnp.maximum(before, peak[...])
        keep = jnp.exp2(before - after)
        packed = []
        for k in range(KEYS // HD):
            packed.append(jnp.exp2(held[:, k * HD : (k + 1) * HD] - after).astype(BF16))
        mixed = dot_nn(jnp.concatenate(packed, axis=1), jnp.concatenate([s.vb[yc], ones], axis=1))
        s.top[p, rows, :] = after
        s.tot[p, rows, :] = s.tot[p, rows, :] * keep + mixed[:, HD:]
        s.acc[p, rows, :] = s.acc[p, rows, :] * keep + mixed[:, :HD]

    def o_copies(p):
        return [
            send(s.os.at[p], s.orb.at[p], s.ops.at[p], s.opr.at[p], at_z(near(p))),
            send(s.ls.at[p], s.lrb.at[p], s.lps.at[p], s.lpr.at[p], at_z(near(p))),
        ]

    def each_head(one):
        def some(i, carry):
            for u in range(4):
                one(i * 4 + u)
            return carry

        lax.fori_loop(0, GQ // 4, some, 0)

    def ship(p):
        def one(h):
            rows = pl.ds(pl.multiple_of(h * SPAN, SPAN), SPAN)
            total = s.tot[p, rows, :]
            s.os[p, h] = (s.acc[p, rows, :] / total).astype(BF16)
            s.ls[p, pl.ds(h, 1), :] = to_row(s.top[p, rows, :] + log2(total))

        each_head(one)
        for copy in o_copies(p):
            copy.start()

    def settle():
        def one(h):
            rows = pl.ds(pl.multiple_of(h * SPAN, SPAN), SPAN)
            levels = [to_column(s.lrb[p, pl.ds(h, 1), :], SPAN) for p in (1, 2, 3)]
            top = s.top[0, rows, :]
            for level in levels:
                top = jnp.maximum(top, level)
            weight = jnp.exp2(s.top[0, rows, :] - top)
            total = s.tot[0, rows, :] * weight
            mixed = s.acc[0, rows, :] * weight
            for p, level in zip((1, 2, 3), levels):
                weight = jnp.exp2(level - top)
                total = total + weight
                mixed = mixed + s.orb[p, h].astype(F32) * weight
            out_p[:, pl.ds(pl.multiple_of(h * HD, HD), HD)] = (mixed / total).astype(BF16)

        each_head(one)

    def pass_values():
        arrived(s.vb.at[up], s.vr.at[up])
        kv_on[1].start()

    def pass_keys():
        arrived(keys_of(down), s.kr.at[down])
        kv_on[0].start()

    def keys_near():
        arrived(s.vb.at[down], s.vr.at[down])
        arrived(keys_of(up), s.kr.at[up])

    def keys_far():
        arrived(keys_of(far), s.kr.at[far])
        arrived(s.vb.at[far], s.vr.at[far])

    def second_queries():
        q_wait(2)
        z_start(q_copy, q_third)

    actions = {
        1: [first_queries, pass_values],
        2: [pass_keys, second_queries, pass_query],
        3: [keys_near, lambda: spread_rows(1)],
        4: [answer],
        5: [keys_far, lambda: pass_rows(0)],
        6: [lambda: q_wait(3), lambda: spread_rows(2)],
        7: [combine_z, lambda: pass_rows(1)],
        8: [lambda: spread_rows(3)],
        9: [combine_y, lambda: pass_rows(2)],
        10: [lambda: pass_rows(3)],
        12: [rest_of_rows],
        14: [far_rows],
    }

    def prepare(i):
        for at, todo in actions.items():

            @pl.when(i == at)
            def _(todo=todo):
                for action in todo:
                    action()

        @pl.when((i == 11) | ((i >= 13) & (i < 16)))
        def _():
            join(jnp.maximum(i - 12, 0))

        @pl.when((i == 10) | ((i >= 12) & (i < 15)))
        def _():
            project(jnp.maximum(i - 11, 0))

    def step(i, carry):
        scores_of(i, 1, s.ts1, s.mx1)
        weigh(i, 0, s.ts0, s.mx0)
        prepare(i + 1)
        scores_of(jnp.minimum(i + 1, 15), 0, s.ts0, s.mx0)
        weigh(i, 1, s.ts1, s.mx1)
        p, k = lookup(PIECES, i), lookup(CHUNKS, i)

        @pl.when((k == 3) & (p > 0))
        def _():
            ship(p)

        return carry

    scores_of(0, 0, s.ts0, s.mx0)
    lax.fori_loop(0, 16, step, 0)
    for p in (1, 2, 3):
        arrived(s.orb.at[p], s.opr.at[p])
        arrived(s.lrb.at[p], s.lpr.at[p])
    settle()

    total = s.own[...]
    for d in (1, 2, 3):
        xx = lax.rem(x + d, RING)
        arrived(s.xi.at[xx], s.xir.at[xx])
        total = total + s.xi[xx].astype(F32)
    for r in range(32):
        out_d[r] = total[r * STEPS : (r + 1) * STEPS, :].astype(BF16)

    for copy in kv_own + kv_on + [c for p in range(RING) for c in ay_own(p) + [ay_on(p)]]:
        copy.wait_send()
    for when, source, step_z, sem in q_first + q_second + q_third:

        @pl.when(when)
        def _(source=source, step_z=step_z, sem=sem):
            q_copy(source, step_z, sem).wait_send()
            a_copy(source, step_z, sem).wait_send()

    for d in range(RING):
        x_copy(d).wait_send()
        for copy in h_copies(d):
            copy.wait_send()
        if d:
            b_copy(d).wait_send()
            for copy in h2_copies(d):
                copy.wait_send()
            for copy in o_copies(d):
                copy.wait_send()
    for j in range(RING):
        si_copy(j).wait_send()

        @pl.when(turned(j) != x)
        def _(j=j):
            xi_copy(j).wait_send()


def shards(span_q, span_kv, prefix_kv, prefix_len, dec_q, dec_new_kv, dec_cache, cache_len, prompt_row, out_weight):
    vmem = pl.BlockSpec(memory_space=pltpu.VMEM)
    smem = pl.BlockSpec(memory_space=pltpu.SMEM)
    hbm = pl.BlockSpec(memory_space=pltpu.HBM)
    prefill, decode = pl.pallas_call(
        kernel,
        out_shape=(
            jax.ShapeDtypeStruct((SPAN, GQ * HD), BF16),
            jax.ShapeDtypeStruct((32, STEPS, COLS), BF16),
        ),
        in_specs=[smem] * 2 + [hbm] * 8,
        out_specs=(vmem, vmem),
        scratch_shapes=list(SCRATCH.values()),
        compiler_params=pltpu.CompilerParams(
            collective_id=0, has_side_effects=True, vmem_limit_bytes=VMEM_BYTES
        ),
        cost_estimate=pl.CostEstimate(flops=11_000_000_000, bytes_accessed=8_000_000, transcendentals=17_000_000),
    )(
        prefix_len,
        prompt_row,
        *[
            pltpu.with_memory_space_constraint(operand, pltpu.HBM)
            for operand in (
                cache_len,
                span_q[0],
                span_kv[0],
                prefix_kv[0],
                dec_q[0],
                dec_new_kv[0],
                dec_cache[0],
                out_weight,
            )
        ],
    )
    return prefill[None], decode[None]


def solution(mesh):
    placed = (
        P("grp", "ctx", "head"),
        P("grp", None, "ctx", "head"),
        P("grp", None, "ctx", "head"),
        P("grp"),
        P("grp", "ctx", None, "head"),
        P("grp", None, "ctx", None, "head"),
        P("grp", None, "ctx", None, "head"),
        P("grp", "ctx"),
        P("grp"),
        P("head", "ctx"),
    )
    return jax.shard_map(
        shards,
        mesh=mesh,
        in_specs=placed,
        out_specs=(P("grp", "ctx", "head"), P("grp", "head", None, "ctx")),
        check_vma=False,
    )
```

```python
import math

import jax
import jax.numpy as jnp
from jax import lax
from jax.experimental import pallas as pl
from jax.experimental.pallas import tpu as pltpu
from jax.sharding import PartitionSpec as P

HD = 128
GQ = 8
RING = 4
PRE = 896
SPAN = 128
KEYS = PRE + SPAN
ROWS = 16
STEPS = 4
SLOTS = 512
QROWS = STEPS * GQ
COLS = 512
MASKED = -1e30
LOG2E = math.log2(math.e)
SCALE = LOG2E / math.sqrt(HD)
MESH = pl.DeviceIdType.MESH
F32 = jnp.float32
BF16 = jnp.bfloat16
BLOCK = 512
VMEM_BYTES = 40 * 1024 * 1024

def piece_of(i):
    return jnp.where(i < 2, i, jnp.where(i < 10, 2 + lax.div(i - 2, 4), 1 - lax.div(i - 10, 3)))


def chunk_of(i):
    return jnp.where(i < 2, 0, jnp.where(i < 10, lax.rem(i - 2, 4), 1 + lax.rem(i - 10, 3)))


def dot_nt(a, b):
    return lax.dot_general(a, b, (((1,), (1,)), ((), ())), preferred_element_type=F32)


def dot_nn(a, b):
    return lax.dot_general(a, b, (((1,), (0,)), ((), ())), preferred_element_type=F32)


def log2(v):
    return jnp.log(v) * LOG2E


def iota(shape, axis):
    return lax.broadcasted_iota(jnp.int32, shape, axis)


def to_row(column):
    shape = column.shape
    return jnp.sum(jnp.where(iota(shape, 0) == iota(shape, 1), column, 0.0), axis=0, keepdims=True)


def to_column(row, count):
    shape = (count, HD)
    spread = jnp.broadcast_to(row, shape)
    return jnp.sum(jnp.where(iota(shape, 0) == iota(shape, 1), spread, 0.0), axis=1, keepdims=True)


def merge(parts):
    top = parts[0][1]
    for _, level in parts[1:]:
        top = jnp.maximum(top, level)
    weights = [jnp.exp2(level - top) for _, level in parts]
    total = weights[0]
    for w in weights[1:]:
        total = total + w
    mixed = parts[0][0] * weights[0]
    for (out, _), w in zip(parts[1:], weights[1:]):
        mixed = mixed + out * w
    return mixed / total, top + log2(total)


SCRATCH = {
    "kl": pltpu.VMEM((KEYS, HD), BF16),
    "kb": pltpu.VMEM((RING, 2 * HD, KEYS), BF16),
    "vb": pltpu.VMEM((RING, KEYS, HD), BF16),
    "qb": pltpu.VMEM((RING, GQ * SPAN, HD), BF16),
    "ts0": pltpu.VMEM((BLOCK, KEYS), F32),
    "ts1": pltpu.VMEM((BLOCK, KEYS), F32),
    "mx0": pltpu.VMEM((BLOCK, HD), F32),
    "mx1": pltpu.VMEM((BLOCK, HD), F32),
    "dq": pltpu.VMEM((ROWS, STEPS, GQ * HD), BF16),
    "nkv": pltpu.VMEM((2, ROWS, STEPS, HD), BF16),
    "acc": pltpu.VMEM((RING, GQ * SPAN, HD), F32),
    "top": pltpu.VMEM((RING, GQ * SPAN, HD), F32),
    "tot": pltpu.VMEM((RING, GQ * SPAN, HD), F32),
    "os": pltpu.VMEM((RING, GQ, SPAN, HD), BF16),
    "ls": pltpu.VMEM((RING, GQ, SPAN), F32),
    "orb": pltpu.VMEM((RING, GQ, SPAN, HD), BF16),
    "lrb": pltpu.VMEM((RING, GQ, SPAN), F32),
    "ck": pltpu.VMEM((ROWS, SLOTS, HD), BF16),
    "cv": pltpu.VMEM((ROWS, SLOTS, HD), BF16),
    "wb": pltpu.VMEM((GQ * HD, COLS), BF16),
    "qf": pltpu.VMEM((ROWS * QROWS, HD), F32),
    "kn": pltpu.VMEM((HD, HD), F32),
    "vn": pltpu.VMEM((HD, HD), F32),
    "of": pltpu.VMEM((ROWS * QROWS, HD), F32),
    "mf": pltpu.VMEM((ROWS * QROWS, HD), F32),
    "lf": pltpu.VMEM((ROWS * QROWS, HD), F32),
    "sb": pltpu.VMEM((RING, QROWS, HD), BF16),
    "sx": pltpu.VMEM((QROWS, HD), BF16),
    "xb": pltpu.VMEM((RING, QROWS, HD), BF16),
    "hos": pltpu.VMEM((QROWS, HD), BF16),
    "hls": pltpu.VMEM((8, HD), F32),
    "ho": pltpu.VMEM((RING, QROWS, HD), BF16),
    "hl": pltpu.VMEM((RING, 8, HD), F32),
    "sl": pltpu.VMEM((RING, 8, HD), F32),
    "ho2": pltpu.VMEM((RING, QROWS, HD), BF16),
    "hl2": pltpu.VMEM((RING, 16, HD), F32),
    "wt": pltpu.VMEM((2 * QROWS, HD), F32),
    "ot": pltpu.VMEM((2 * QROWS, HD), F32),
    "ab": pltpu.VMEM((RING, RING, GQ, ROWS * STEPS, HD), BF16),
    "am": pltpu.VMEM((RING * ROWS * STEPS, GQ * HD), BF16),
    "pr": pltpu.VMEM((RING * ROWS * STEPS, COLS), F32),
    "pm": pltpu.VMEM((RING, 128, COLS), F32),
    "so": pltpu.VMEM((RING, 128, COLS), BF16),
    "si": pltpu.VMEM((RING, 128, COLS), BF16),
    "xo": pltpu.VMEM((RING, 128, COLS), BF16),
    "xi": pltpu.VMEM((RING, 128, COLS), BF16),
    "own": pltpu.VMEM((128, COLS), F32),
    "clen": pltpu.SMEM((1, ROWS), jnp.int32),
    "loc": pltpu.SemaphoreType.DMA((18,)),
    "kvs": pltpu.SemaphoreType.DMA((6,)),
    "kr": pltpu.SemaphoreType.DMA((RING,)),
    "vr": pltpu.SemaphoreType.DMA((RING,)),
    "qs": pltpu.SemaphoreType.DMA((6,)),
    "qr": pltpu.SemaphoreType.DMA((RING,)),
    "bs": pltpu.SemaphoreType.DMA((RING,)),
    "br": pltpu.SemaphoreType.DMA((RING,)),
    "xs": pltpu.SemaphoreType.DMA((RING,)),
    "xr": pltpu.SemaphoreType.DMA((RING,)),
    "hs": pltpu.SemaphoreType.DMA((RING,)),
    "hr": pltpu.SemaphoreType.DMA((RING,)),
    "hls_s": pltpu.SemaphoreType.DMA((RING,)),
    "hlr": pltpu.SemaphoreType.DMA((RING,)),
    "sls": pltpu.SemaphoreType.DMA((RING,)),
    "slr": pltpu.SemaphoreType.DMA((RING,)),
    "h2s": pltpu.SemaphoreType.DMA((RING,)),
    "h2r": pltpu.SemaphoreType.DMA((RING,)),
    "hl2s": pltpu.SemaphoreType.DMA((RING,)),
    "hl2r": pltpu.SemaphoreType.DMA((RING,)),
    "as_": pltpu.SemaphoreType.DMA((6,)),
    "ar": pltpu.SemaphoreType.DMA((RING,)),
    "ays": pltpu.SemaphoreType.DMA((3 * RING,)),
    "ayr": pltpu.SemaphoreType.DMA((RING, RING)),
    "ops": pltpu.SemaphoreType.DMA((RING,)),
    "opr": pltpu.SemaphoreType.DMA((RING,)),
    "lps": pltpu.SemaphoreType.DMA((RING,)),
    "lpr": pltpu.SemaphoreType.DMA((RING,)),
    "sis": pltpu.SemaphoreType.DMA((RING,)),
    "sir": pltpu.SemaphoreType.DMA((RING,)),
    "xis": pltpu.SemaphoreType.DMA((RING,)),
    "xir": pltpu.SemaphoreType.DMA((RING,)),
}


class Names:
    pass


def kernel(plen, prow, clen_in, q_in, skv, pkv, dq, nkv, cache, w_in, out_p, out_d, *scratch):
    s = Names()
    for name, ref in zip(SCRATCH, scratch):
        setattr(s, name, ref)

    me = lax.axis_index("ctx")
    y, z = lax.div(me, RING), lax.rem(me, RING)
    head = lax.axis_index("head")
    x, core = lax.div(head, 2), lax.rem(head, 2)
    other = 1 - lax.axis_index("grp")

    def turned(j):
        return lax.rem(y + lax.div(j * (j + 1), 2), RING)

    def near(p):
        high = lax.rem(lax.div(z, 2) + lax.div(p, 2), 2)
        return 2 * high + lax.rem(z + p, 2)

    up, down, far = lax.rem(y + 1, RING), lax.rem(y + 3, RING), lax.rem(y + 2, RING)

    def at_y(yy):
        return {"ctx": yy * RING + z}

    def at_z(zz):
        return {"ctx": y * RING + zz}

    def across(zz):
        return {"ctx": y * RING + zz, "grp": other}

    def at_x(xx):
        return {"head": xx * 2 + core}

    sibling = {"head": x * 2 + 1 - core}

    def send(src, dst, ssem, rsem, device):
        return pltpu.make_async_remote_copy(
            src_ref=src, dst_ref=dst, send_sem=ssem, recv_sem=rsem, device_id=device, device_id_type=MESH
        )

    def arrived(dst, rsem):
        send(dst, dst, s.loc.at[0], rsem, sibling).wait_recv()

    pairs = [
        (pkv.at[0], s.kl.at[pl.ds(0, PRE)]),
        (skv.at[0], s.kl.at[pl.ds(PRE, SPAN)]),
        (pkv.at[1], s.vb.at[y, pl.ds(0, PRE)]),
        (skv.at[1], s.vb.at[y, pl.ds(PRE, SPAN)]),
    ]
    pairs += [(q_in.at[:, pl.ds(h * HD, HD)], s.qb.at[z, pl.ds(h * SPAN, SPAN)]) for h in range(GQ)]
    pairs += [(dq, s.dq), (nkv, s.nkv), (clen_in, s.clen), (cache.at[0], s.ck), (cache.at[1], s.cv), (w_in, s.wb)]
    loads = [pltpu.make_async_copy(src, dst, s.loc.at[at]) for at, (src, dst) in enumerate(pairs)]
    for load in loads:
        load.start()

    barrier = pltpu.get_barrier_semaphore()
    greeted = [at_y(lax.rem(y + d, RING)) for d in (1, 2, 3)] + [at_z(lax.rem(z + d, RING)) for d in (1, 2, 3)]
    greeted += [across(zz) for zz in range(RING)] + [sibling] + [at_x(lax.rem(x + d, RING)) for d in (1, 2, 3)]
    for device in greeted:
        pl.semaphore_signal(barrier, inc=1, device_id=device, device_id_type=MESH)

    def clear(p, carry):
        s.acc[p] = jnp.zeros((GQ * SPAN, HD), F32)
        s.tot[p] = jnp.zeros((GQ * SPAN, HD), F32)
        s.top[p] = jnp.full((GQ * SPAN, HD), MASKED, F32)
        slot = iota((HD, KEYS), 1)
        unused = ((p * RING + z) * PRE + slot >= plen[0]) & (slot < PRE) & (iota((HD, KEYS), 0) == 0)
        s.kb[p, HD : 2 * HD, :] = jnp.where(unused, MASKED, 0.0).astype(BF16)
        return carry

    lax.fori_loop(0, RING, clear, 0)


    for load in loads[2:12]:
        load.wait()
    pl.semaphore_wait(barrier, len(greeted))

    def keys_of(yy):
        return s.kb.at[yy, pl.ds(0, HD)]

    kv_own = [
        send(s.vb.at[y], s.vb.at[y], s.kvs.at[0], s.vr.at[y], at_y(up)),
        send(s.vb.at[y], s.vb.at[y], s.kvs.at[1], s.vr.at[y], at_y(down)),
        send(keys_of(y), keys_of(y), s.kvs.at[2], s.kr.at[y], at_y(up)),
        send(keys_of(y), keys_of(y), s.kvs.at[3], s.kr.at[y], at_y(down)),
    ]
    kv_on = [
        send(keys_of(down), keys_of(down), s.kvs.at[4], s.kr.at[down], at_y(up)),
        send(s.vb.at[up], s.vb.at[up], s.kvs.at[5], s.vr.at[up], at_y(down)),
    ]

    def q_copy(source, step, sem):
        return send(s.qb.at[source], s.qb.at[source], s.qs.at[sem], s.qr.at[source], at_z(z + step))

    def a_copy(source, step, sem):
        block = s.ab.at[y, source]
        return send(block, block, s.as_.at[sem], s.ar.at[source], at_z(z + step))

    q_first = [(z < 3, z, 1, 0), (z > 0, z, -1, 1)]
    q_second = [((z > 0) & (z < 3), z - 1, 1, 2), ((z > 0) & (z < 3), z + 1, -1, 3)]
    q_third = [(z == 2, z - 2, 1, 4), (z == 1, z + 2, -1, 5)]

    def z_start(copy, group):
        for when, source, step, sem in group:

            @pl.when(when)
            def _(source=source, step=step, sem=sem):
                copy(source, step, sem).start()

    def z_wait(block, sems, distance):
        @pl.when(z >= distance)
        def _():
            arrived(block(z - distance), sems.at[z - distance])

        @pl.when(z + distance < RING)
        def _():
            arrived(block(z + distance), sems.at[z + distance])

    def q_wait(distance):
        z_wait(lambda source: s.qb.at[source], s.qr, distance)

    def a_wait(distance):
        z_wait(lambda source: s.ab.at[y, source], s.ar, distance)

    def b_copy(d):
        return send(s.sb.at[y], s.sb.at[y], s.bs.at[d], s.br.at[y], at_y(lax.rem(y + d, RING)))

    for copy in kv_own[:2]:
        copy.start()
    z_start(q_copy, q_first)
    for load in loads[:2]:
        load.wait()
    s.kb[y, 0:HD, :] = s.kl[...].T
    for copy in kv_own[2:]:
        copy.start()

    for load in loads[12:15]:
        load.wait()
    for r in range(ROWS):
        row = s.dq[r].astype(F32)
        for h in range(GQ):
            s.qf[pl.ds(r * QROWS + h, STEPS, stride=GQ), :] = row[:, h * HD : (h + 1) * HD]
    s.kn[...] = jnp.zeros((HD, HD), F32)
    s.vn[...] = jnp.zeros((HD, HD), F32)
    for r in range(ROWS):
        s.kn[pl.ds(r * STEPS, STEPS), :] = s.nkv[0, r].astype(F32)
        s.vn[pl.ds(r * STEPS, STEPS), :] = s.nkv[1, r].astype(F32)

    def picked(ref):
        total = jnp.zeros((QROWS, HD), F32)
        for r in range(ROWS):
            mine = jnp.where(me * ROWS + r == prow[0], 1.0, 0.0)
            total = total + mine * ref[r * QROWS : (r + 1) * QROWS, :]
        return total

    s.sb[y] = picked(s.qf).astype(BF16)

    for d in (1, 2, 3):
        b_copy(d).start()

    lanes = (ROWS * QROWS, HD)
    at_row, at_key = iota(lanes, 0), iota(lanes, 1)
    same = lax.shift_right_logical(at_row, 5) == lax.shift_right_logical(at_key, 2)
    early = jnp.bitwise_and(at_key, 3) <= jnp.bitwise_and(lax.shift_right_logical(at_row, 3), 3)
    new = jnp.where(same & early, dot_nt(s.qf[...].astype(BF16), s.kn[...].astype(BF16)) * SCALE, MASKED)
    new_top = jnp.max(new, axis=1, keepdims=True)
    new_weights = jnp.exp2(new - new_top)
    s.mf[...] = jnp.broadcast_to(new_top, lanes)
    s.lf[...] = jnp.broadcast_to(jnp.sum(new_weights, axis=1, keepdims=True), lanes)
    s.of[...] = dot_nn(new_weights.astype(BF16), s.vn[...].astype(BF16))

    for load in loads[15:]:
        load.wait()

    def cached(r):
        rows = pl.ds(pl.multiple_of(r * QROWS, QROWS), QROWS)
        scores = dot_nt(s.qf[rows, :].astype(BF16), s.ck[r]) * SCALE
        scores = jnp.where(iota((QROWS, SLOTS), 1) < s.clen[0, r], scores, MASKED)
        before = s.mf[rows, :]
        after = jnp.maximum(before, jnp.max(scores, axis=1, keepdims=True))
        weights = jnp.exp2(scores - after[:, :1])
        keep = jnp.exp2(before - after)
        total = s.lf[rows, :] * keep + jnp.sum(weights, axis=1, keepdims=True)
        mixed = s.of[rows, :] * keep + dot_nn(weights.astype(BF16), s.cv[r])
        s.of[rows, :] = mixed / total
        s.lf[rows, :] = after + log2(total)

    def first_queries():
        q_wait(1)
        z_start(q_copy, q_second)

    def some_rows(i, carry):
        for u in range(8):
            cached(i * 8 + u)
        return carry

    lax.fori_loop(0, ROWS // 8, some_rows, 0)
    for h in range(GQ):
        s.ab[y, z, h] = s.of[pl.ds(h, ROWS * STEPS, stride=GQ), :].astype(BF16)

    def ay_copy(yy, p, sem, to):
        block = s.ab.at[yy, near(p)]
        return send(block, block, s.ays.at[sem], s.ayr.at[yy, near(p)], at_y(to))

    def ay_own(p):
        return [ay_copy(y, p, 3 * p, up), ay_copy(y, p, 3 * p + 1, down)]

    def ay_on(p):
        return ay_copy(down, p, 3 * p + 2, up) if p < 2 else ay_copy(up, p, 3 * p + 2, down)

    def rows_in(yy, p):
        arrived(s.ab.at[yy, near(p)], s.ayr.at[yy, near(p)])

    def spread_rows(p):
        if p:
            a_wait(p)
            z_start(a_copy, (q_second, q_third, [])[p - 1])
        for copy in ay_own(p):
            copy.start()

    def pass_rows(p):
        rows_in(down if p < 2 else up, p)
        ay_on(p).start()

    def rest_of_rows():
        for p in range(RING):
            rows_in(up if p < 2 else down, p)

    def far_rows():
        for p in range(RING):
            rows_in(far, p)

    z_start(a_copy, q_first)
    spread_rows(0)
    s.sl[z] = jnp.broadcast_to(to_row(picked(s.lf)), (8, HD))

    def x_copy(d):
        zz = lax.rem(z + d, RING)
        return send(s.sx, s.xb.at[z], s.xs.at[d], s.xr.at[z], across(zz))

    def pass_query():
        for d in (1, 2, 3):
            yy = lax.rem(y + d, RING)
            arrived(s.sb.at[yy], s.br.at[yy])
        total = s.sb[0].astype(F32)
        for yy in (1, 2, 3):
            total = total + s.sb[yy].astype(F32)
        s.sx[...] = total.astype(BF16)
        for d in range(RING):
            x_copy(d).start()

    def h_copies(d):
        zz = lax.rem(z + d, RING)
        copies = [
            send(s.hos, s.ho.at[z], s.hs.at[d], s.hr.at[z], across(zz)),
            send(s.hls, s.hl.at[z], s.hls_s.at[d], s.hlr.at[z], across(zz)),
        ]
        if d:
            copies.append(send(s.sl.at[z], s.sl.at[z], s.sls.at[d], s.slr.at[z], at_z(zz)))
        return copies

    def answer():
        for zz in range(RING):
            arrived(s.xb.at[zz], s.xr.at[zz])
        query = s.xb[0].astype(F32)
        for zz in (1, 2, 3):
            query = query + s.xb[zz].astype(F32)
        span = pl.ds(PRE, SPAN)
        scores = dot_nn(query.astype(BF16), s.kb[y, 0:HD, span]) * SCALE
        top = jnp.max(scores, axis=1, keepdims=True)
        weights = jnp.exp2(scores - top)
        total = jnp.sum(weights, axis=1, keepdims=True)
        s.hos[...] = (dot_nn(weights.astype(BF16), s.vb[y, span, :]) / total).astype(BF16)
        level = jnp.broadcast_to(top + log2(total), (QROWS, HD))
        s.hls[...] = jnp.broadcast_to(to_row(level), (8, HD))
        for d in range(RING):
            for copy in h_copies(d):
                copy.start()

    def h2_copies(d):
        yy = lax.rem(y + d, RING)
        return [
            send(s.ho2.at[y], s.ho2.at[y], s.h2s.at[d], s.h2r.at[y], at_y(yy)),
            send(s.hl2.at[y], s.hl2.at[y], s.hl2s.at[d], s.hl2r.at[y], at_y(yy)),
        ]

    def combine_z():
        for zz in range(RING):
            arrived(s.ho.at[zz], s.hr.at[zz])
            arrived(s.hl.at[zz], s.hlr.at[zz])
        for d in (1, 2, 3):
            zz = lax.rem(z + d, RING)
            arrived(s.sl.at[zz], s.slr.at[zz])
        out, level = merge([(s.ho[zz].astype(F32), to_column(s.hl[zz, 0:1, :], QROWS)) for zz in range(RING)])
        s.ho2[y] = out.astype(BF16)
        s.hl2[y, 0:8, :] = jnp.broadcast_to(to_row(jnp.broadcast_to(level, (QROWS, HD))), (8, HD))
        s.hl2[y, 8:16, :] = s.sl[0] + s.sl[1] + s.sl[2] + s.sl[3]
        for d in (1, 2, 3):
            for copy in h2_copies(d):
                copy.start()

    def combine_y():
        for d in (1, 2, 3):
            yy = lax.rem(y + d, RING)
            arrived(s.ho2.at[yy], s.h2r.at[yy])
            arrived(s.hl2.at[yy], s.hl2r.at[yy])
        out, level = merge([(s.ho2[yy].astype(F32), to_column(s.hl2[yy, 0:1, :], QROWS)) for yy in range(RING)])
        rows = s.hl2[0, 8:9, :] + s.hl2[1, 8:9, :] + s.hl2[2, 8:9, :] + s.hl2[3, 8:9, :]
        before = to_column(rows, QROWS)
        top = jnp.maximum(before, level)
        w_own, w_span = jnp.exp2(before - top), jnp.exp2(level - top)
        total = w_own + w_span
        keep = jnp.broadcast_to(w_own / total, (QROWS, HD))
        added = out * (w_span / total)
        for at in range(2):
            s.wt[pl.ds(at * QROWS, QROWS), :] = keep
            s.ot[pl.ds(at * QROWS, QROWS), :] = added

    def si_copy(j):
        return send(s.so.at[j], s.si.at[j], s.sis.at[j], s.sir.at[j], sibling)

    def project(j):
        yc = turned(j)
        count = RING * ROWS * STEPS
        row = yc * (RING * ROWS) + lax.shift_right_logical(iota((count, HD), 0), 2)
        hit = row == prow[0]
        for h in range(GQ):
            block = jnp.concatenate([s.ab[yc, zz, h] for zz in range(RING)], axis=0).astype(F32)
            keep = s.wt[pl.ds(h, 2 * STEPS, stride=GQ), :]
            added = s.ot[pl.ds(h, 2 * STEPS, stride=GQ), :]
            keep = jnp.concatenate([keep] * (count // (2 * STEPS)), axis=0)
            added = jnp.concatenate([added] * (count // (2 * STEPS)), axis=0)
            block = jnp.where(hit, block * keep + added, block)
            s.am[:, h * HD : (h + 1) * HD] = block.astype(BF16)
        s.pr[...] = dot_nn(s.am[...], s.wb[...])
        s.pm[j] = s.pr[pl.ds(pl.multiple_of(core * 128, 128), 128), :]
        s.so[j] = s.pr[pl.ds(pl.multiple_of((1 - core) * 128, 128), 128), :].astype(BF16)
        si_copy(j).start()

    def xi_copy(j):
        return send(s.xo.at[j], s.xi.at[x], s.xis.at[j], s.xir.at[x], at_x(turned(j)))

    def join(j):
        arrived(s.si.at[j], s.sir.at[j])
        total = s.pm[j] + s.si[j].astype(F32)

        @pl.when(turned(j) == x)
        def _():
            s.own[...] = total

        @pl.when(turned(j) != x)
        def _():
            s.xo[j] = total.astype(BF16)
            xi_copy(j).start()

    count = BLOCK // SPAN
    first_lane = jnp.where(iota((BLOCK, HD), 1) == 0, 1.0, 0.0).astype(BF16)
    ones = jnp.ones((KEYS, HD), BF16)

    def scores_of(at, b, held, peak):
        p, yc = piece_of(at), turned(chunk_of(at))
        zq = near(p)
        late = (y * RING + zq) * SPAN - (yc * RING + z) * SPAN
        shape = (SPAN, SPAN)
        ahead = jnp.where(iota(shape, 1) - iota(shape, 0) <= late, 0.0, MASKED)
        ahead = jnp.concatenate([ahead] * count, axis=0)
        queries = jnp.concatenate([s.qb[zq, b * BLOCK : (b + 1) * BLOCK, :], first_lane], axis=1)
        scores = dot_nn(queries, s.kb[yc])
        highest = None
        for k in range(KEYS // HD):
            cols = slice(k * HD, (k + 1) * HD)
            part = scores[:, cols] * SCALE
            if k == PRE // HD:
                part = part + ahead
            held[:, cols] = part
            highest = part if highest is None else jnp.maximum(highest, part)
        peak[...] = jnp.broadcast_to(jnp.max(highest, axis=1, keepdims=True), (BLOCK, HD))

    def weigh(at, b, held, peak):
        p, yc = piece_of(at), turned(chunk_of(at))
        rows = slice(b * BLOCK, (b + 1) * BLOCK)
        before = s.top[p, rows, :]
        after = jnp.maximum(before, peak[...])
        keep = jnp.exp2(before - after)
        packed = []
        for k in range(KEYS // HD):
            packed.append(jnp.exp2(held[:, k * HD : (k + 1) * HD] - after).astype(BF16))
        mixed = dot_nn(jnp.concatenate(packed, axis=1), jnp.concatenate([s.vb[yc], ones], axis=1))
        s.top[p, rows, :] = after
        s.tot[p, rows, :] = s.tot[p, rows, :] * keep + mixed[:, HD:]
        s.acc[p, rows, :] = s.acc[p, rows, :] * keep + mixed[:, :HD]

    def o_copies(p):
        return [
            send(s.os.at[p], s.orb.at[p], s.ops.at[p], s.opr.at[p], at_z(near(p))),
            send(s.ls.at[p], s.lrb.at[p], s.lps.at[p], s.lpr.at[p], at_z(near(p))),
        ]

    def each_head(one):
        def some(i, carry):
            for u in range(4):
                one(i * 4 + u)
            return carry

        lax.fori_loop(0, GQ // 4, some, 0)

    def ship(p):
        def one(h):
            rows = pl.ds(pl.multiple_of(h * SPAN, SPAN), SPAN)
            total = s.tot[p, rows, :]
            s.os[p, h] = (s.acc[p, rows, :] / total).astype(BF16)
            s.ls[p, pl.ds(h, 1), :] = to_row(s.top[p, rows, :] + log2(total))

        each_head(one)
        for copy in o_copies(p):
            copy.start()

    def settle():
        def one(h):
            rows = pl.ds(pl.multiple_of(h * SPAN, SPAN), SPAN)
            levels = [to_column(s.lrb[p, pl.ds(h, 1), :], SPAN) for p in (1, 2, 3)]
            top = s.top[0, rows, :]
            for level in levels:
                top = jnp.maximum(top, level)
            weight = jnp.exp2(s.top[0, rows, :] - top)
            total = s.tot[0, rows, :] * weight
            mixed = s.acc[0, rows, :] * weight
            for p, level in zip((1, 2, 3), levels):
                weight = jnp.exp2(level - top)
                total = total + weight
                mixed = mixed + s.orb[p, h].astype(F32) * weight
            out_p[:, pl.ds(pl.multiple_of(h * HD, HD), HD)] = (mixed / total).astype(BF16)

        each_head(one)

    def pass_values():
        arrived(s.vb.at[up], s.vr.at[up])
        kv_on[1].start()

    def pass_keys():
        arrived(keys_of(down), s.kr.at[down])
        kv_on[0].start()

    def keys_near():
        arrived(s.vb.at[down], s.vr.at[down])
        arrived(keys_of(up), s.kr.at[up])

    def keys_far():
        arrived(keys_of(far), s.kr.at[far])
        arrived(s.vb.at[far], s.vr.at[far])

    def second_queries():
        q_wait(2)
        z_start(q_copy, q_third)

    actions = {
        1: [first_queries, pass_values],
        2: [pass_keys, second_queries, pass_query],
        3: [keys_near, lambda: spread_rows(1)],
        4: [answer],
        5: [keys_far, lambda: pass_rows(0)],
        6: [lambda: q_wait(3), lambda: spread_rows(2)],
        7: [combine_z, lambda: pass_rows(1)],
        8: [lambda: spread_rows(3)],
        9: [combine_y, lambda: pass_rows(2)],
        10: [lambda: pass_rows(3)],
        12: [rest_of_rows],
        14: [far_rows],
    }

    def prepare(i):
        for at, todo in actions.items():

            @pl.when(i == at)
            def _(todo=todo):
                for action in todo:
                    action()

        @pl.when((i == 11) | ((i >= 13) & (i < 16)))
        def _():
            join(jnp.maximum(i - 12, 0))

        @pl.when((i == 10) | ((i >= 12) & (i < 15)))
        def _():
            project(jnp.maximum(i - 11, 0))

    def step(i, carry):
        scores_of(i, 1, s.ts1, s.mx1)
        weigh(i, 0, s.ts0, s.mx0)
        prepare(i + 1)
        scores_of(jnp.minimum(i + 1, 15), 0, s.ts0, s.mx0)
        weigh(i, 1, s.ts1, s.mx1)
        p, k = piece_of(i), chunk_of(i)

        @pl.when((k == 3) & (p > 0))
        def _():
            ship(p)

        return carry

    scores_of(jnp.int32(0), 0, s.ts0, s.mx0)
    lax.fori_loop(0, 16, step, 0)
    for p in (1, 2, 3):
        arrived(s.orb.at[p], s.opr.at[p])
        arrived(s.lrb.at[p], s.lpr.at[p])
    settle()

    total = s.own[...]
    for d in (1, 2, 3):
        xx = lax.rem(x + d, RING)
        arrived(s.xi.at[xx], s.xir.at[xx])
        total = total + s.xi[xx].astype(F32)
    for r in range(32):
        out_d[r] = total[r * STEPS : (r + 1) * STEPS, :].astype(BF16)

    for copy in kv_own + kv_on + [c for p in range(RING) for c in ay_own(p) + [ay_on(p)]]:
        copy.wait_send()
    for when, source, step_z, sem in q_first + q_second + q_third:

        @pl.when(when)
        def _(source=source, step_z=step_z, sem=sem):
            q_copy(source, step_z, sem).wait_send()
            a_copy(source, step_z, sem).wait_send()

    for d in range(RING):
        x_copy(d).wait_send()
        for copy in h_copies(d):
            copy.wait_send()
        if d:
            b_copy(d).wait_send()
            for copy in h2_copies(d):
                copy.wait_send()
            for copy in o_copies(d):
                copy.wait_send()
    for j in range(RING):
        si_copy(j).wait_send()

        @pl.when(turned(j) != x)
        def _(j=j):
            xi_copy(j).wait_send()


def shards(span_q, span_kv, prefix_kv, prefix_len, dec_q, dec_new_kv, dec_cache, cache_len, prompt_row, out_weight):
    vmem = pl.BlockSpec(memory_space=pltpu.VMEM)
    smem = pl.BlockSpec(memory_space=pltpu.SMEM)
    hbm = pl.BlockSpec(memory_space=pltpu.HBM)
    prefill, decode = pl.pallas_call(
        kernel,
        out_shape=(
            jax.ShapeDtypeStruct((SPAN, GQ * HD), BF16),
            jax.ShapeDtypeStruct((32, STEPS, COLS), BF16),
        ),
        in_specs=[smem] * 2 + [hbm] * 8,
        out_specs=(vmem, vmem),
        scratch_shapes=list(SCRATCH.values()),
        compiler_params=pltpu.CompilerParams(
            collective_id=0, has_side_effects=True, vmem_limit_bytes=VMEM_BYTES
        ),
        cost_estimate=pl.CostEstimate(flops=11_000_000_000, bytes_accessed=8_000_000, transcendentals=17_000_000),
    )(
        prefix_len,
        prompt_row,
        *[
            pltpu.with_memory_space_constraint(operand, pltpu.HBM)
            for operand in (
                cache_len,
                span_q[0],
                span_kv[0],
                prefix_kv[0],
                dec_q[0],
                dec_new_kv[0],
                dec_cache[0],
                out_weight,
            )
        ],
    )
    return prefill[None], decode[None]


def solution(mesh):
    placed = (
        P("grp", "ctx", "head"),
        P("grp", None, "ctx", "head"),
        P("grp", None, "ctx", "head"),
        P("grp"),
        P("grp", "ctx", None, "head"),
        P("grp", None, "ctx", None, "head"),
        P("grp", None, "ctx", None, "head"),
        P("grp", "ctx"),
        P("grp"),
        P("head", "ctx"),
    )
    return jax.shard_map(
        shards,
        mesh=mesh,
        in_specs=placed,
        out_specs=(P("grp", "ctx", "head"), P("grp", "head", None, "ctx")),
        check_vma=False,
    )
```

```python
import math

import jax
import jax.numpy as jnp
from jax import lax
from jax.experimental import pallas as pl
from jax.experimental.pallas import tpu as pltpu
from jax.sharding import PartitionSpec as P

HD = 128
GQ = 8
RING = 4
PRE = 896
SPAN = 128
KEYS = PRE + SPAN
ROWS = 16
STEPS = 4
SLOTS = 512
QROWS = STEPS * GQ
COLS = 512
MASKED = -1e30
LOG2E = math.log2(math.e)
SCALE = LOG2E / math.sqrt(HD)
MESH = pl.DeviceIdType.MESH
F32 = jnp.float32
BF16 = jnp.bfloat16
BLOCK = 512
VMEM_BYTES = 40 * 1024 * 1024

def piece_of(i):
    return jnp.where(i < 2, i, jnp.where(i < 10, 2 + lax.div(i - 2, 4), 1 - lax.div(i - 10, 3)))


def chunk_of(i):
    return jnp.where(i < 2, 0, jnp.where(i < 10, lax.rem(i - 2, 4), 1 + lax.rem(i - 10, 3)))


def dot_nt(a, b):
    return lax.dot_general(a, b, (((1,), (1,)), ((), ())), preferred_element_type=F32)


def dot_nn(a, b):
    return lax.dot_general(a, b, (((1,), (0,)), ((), ())), preferred_element_type=F32)


def log2(v):
    return jnp.log(v) * LOG2E


def iota(shape, axis):
    return lax.broadcasted_iota(jnp.int32, shape, axis)


def to_row(column):
    shape = column.shape
    return jnp.sum(jnp.where(iota(shape, 0) == iota(shape, 1), column, 0.0), axis=0, keepdims=True)


def to_column(row, count):
    shape = (count, HD)
    spread = jnp.broadcast_to(row, shape)
    return jnp.sum(jnp.where(iota(shape, 0) == iota(shape, 1), spread, 0.0), axis=1, keepdims=True)


def merge(parts):
    top = parts[0][1]
    for _, level in parts[1:]:
        top = jnp.maximum(top, level)
    weights = [jnp.exp2(level - top) for _, level in parts]
    total = weights[0]
    for w in weights[1:]:
        total = total + w
    mixed = parts[0][0] * weights[0]
    for (out, _), w in zip(parts[1:], weights[1:]):
        mixed = mixed + out * w
    return mixed / total, top + log2(total)


SCRATCH = {
    "kl": pltpu.VMEM((KEYS, HD), BF16),
    "kb": pltpu.VMEM((RING, 2 * HD, KEYS), BF16),
    "vb": pltpu.VMEM((RING, KEYS, HD), BF16),
    "qb": pltpu.VMEM((RING, GQ * SPAN, HD), BF16),
    "ts0": pltpu.VMEM((BLOCK, KEYS), F32),
    "ts1": pltpu.VMEM((BLOCK, KEYS), F32),
    "kp": pltpu.VMEM((BLOCK, HD), F32),
    "pk": pltpu.VMEM((BLOCK, KEYS), BF16),
    "ahead": pltpu.VMEM((SPAN, SPAN), F32),
    "dq": pltpu.VMEM((ROWS, STEPS, GQ * HD), BF16),
    "nkv": pltpu.VMEM((2, ROWS, STEPS, HD), BF16),
    "acc": pltpu.VMEM((RING, GQ * SPAN, HD), F32),
    "top": pltpu.VMEM((RING, GQ * SPAN, HD), F32),
    "tot": pltpu.VMEM((RING, GQ * SPAN, HD), F32),
    "os": pltpu.VMEM((RING, GQ, SPAN, HD), BF16),
    "ls": pltpu.VMEM((RING, GQ, SPAN), F32),
    "orb": pltpu.VMEM((RING, GQ, SPAN, HD), BF16),
    "lrb": pltpu.VMEM((RING, GQ, SPAN), F32),
    "ck": pltpu.VMEM((ROWS, SLOTS, HD), BF16),
    "cv": pltpu.VMEM((ROWS, SLOTS, HD), BF16),
    "wb": pltpu.VMEM((GQ * HD, COLS), BF16),
    "qf": pltpu.VMEM((ROWS * QROWS, HD), F32),
    "kn": pltpu.VMEM((HD, HD), F32),
    "vn": pltpu.VMEM((HD, HD), F32),
    "of": pltpu.VMEM((ROWS * QROWS, HD), F32),
    "mf": pltpu.VMEM((ROWS * QROWS, HD), F32),
    "lf": pltpu.VMEM((ROWS * QROWS, HD), F32),
    "sb": pltpu.VMEM((RING, QROWS, HD), BF16),
    "sx": pltpu.VMEM((QROWS, HD), BF16),
    "xb": pltpu.VMEM((RING, QROWS, HD), BF16),
    "hos": pltpu.VMEM((QROWS, HD), BF16),
    "hls": pltpu.VMEM((8, HD), F32),
    "ho": pltpu.VMEM((RING, QROWS, HD), BF16),
    "hl": pltpu.VMEM((RING, 8, HD), F32),
    "sl": pltpu.VMEM((RING, 8, HD), F32),
    "ho2": pltpu.VMEM((RING, QROWS, HD), BF16),
    "hl2": pltpu.VMEM((RING, 16, HD), F32),
    "wt": pltpu.VMEM((2 * QROWS, HD), F32),
    "ot": pltpu.VMEM((2 * QROWS, HD), F32),
    "ab": pltpu.VMEM((RING, RING, GQ, ROWS * STEPS, HD), BF16),
    "am": pltpu.VMEM((RING * ROWS * STEPS, GQ * HD), BF16),
    "pr": pltpu.VMEM((RING * ROWS * STEPS, COLS), F32),
    "pm": pltpu.VMEM((RING, 128, COLS), F32),
    "so": pltpu.VMEM((RING, 128, COLS), BF16),
    "si": pltpu.VMEM((RING, 128, COLS), BF16),
    "xo": pltpu.VMEM((RING, 128, COLS), BF16),
    "xi": pltpu.VMEM((RING, 128, COLS), BF16),
    "own": pltpu.VMEM((128, COLS), F32),
    "clen": pltpu.SMEM((1, ROWS), jnp.int32),
    "loc": pltpu.SemaphoreType.DMA((18,)),
    "kvs": pltpu.SemaphoreType.DMA((6,)),
    "kr": pltpu.SemaphoreType.DMA((RING,)),
    "vr": pltpu.SemaphoreType.DMA((RING,)),
    "qs": pltpu.SemaphoreType.DMA((6,)),
    "qr": pltpu.SemaphoreType.DMA((RING,)),
    "bs": pltpu.SemaphoreType.DMA((RING,)),
    "br": pltpu.SemaphoreType.DMA((RING,)),
    "xs": pltpu.SemaphoreType.DMA((RING,)),
    "xr": pltpu.SemaphoreType.DMA((RING,)),
    "hs": pltpu.SemaphoreType.DMA((RING,)),
    "hr": pltpu.SemaphoreType.DMA((RING,)),
    "hls_s": pltpu.SemaphoreType.DMA((RING,)),
    "hlr": pltpu.SemaphoreType.DMA((RING,)),
    "sls": pltpu.SemaphoreType.DMA((RING,)),
    "slr": pltpu.SemaphoreType.DMA((RING,)),
    "h2s": pltpu.SemaphoreType.DMA((RING,)),
    "h2r": pltpu.SemaphoreType.DMA((RING,)),
    "hl2s": pltpu.SemaphoreType.DMA((RING,)),
    "hl2r": pltpu.SemaphoreType.DMA((RING,)),
    "as_": pltpu.SemaphoreType.DMA((6,)),
    "ar": pltpu.SemaphoreType.DMA((RING,)),
    "ays": pltpu.SemaphoreType.DMA((3 * RING,)),
    "ayr": pltpu.SemaphoreType.DMA((RING, RING)),
    "ops": pltpu.SemaphoreType.DMA((RING,)),
    "opr": pltpu.SemaphoreType.DMA((RING,)),
    "lps": pltpu.SemaphoreType.DMA((RING,)),
    "lpr": pltpu.SemaphoreType.DMA((RING,)),
    "sis": pltpu.SemaphoreType.DMA((RING,)),
    "sir": pltpu.SemaphoreType.DMA((RING,)),
    "xis": pltpu.SemaphoreType.DMA((RING,)),
    "xir": pltpu.SemaphoreType.DMA((RING,)),
}


class Names:
    pass


def kernel(plen, prow, clen_in, q_in, skv, pkv, dq, nkv, cache, w_in, out_p, out_d, *scratch):
    s = Names()
    for name, ref in zip(SCRATCH, scratch):
        setattr(s, name, ref)

    me = lax.axis_index("ctx")
    y, z = lax.div(me, RING), lax.rem(me, RING)
    head = lax.axis_index("head")
    x, core = lax.div(head, 2), lax.rem(head, 2)
    other = 1 - lax.axis_index("grp")

    def turned(j):
        return lax.rem(y + lax.div(j * (j + 1), 2), RING)

    def near(p):
        high = lax.rem(lax.div(z, 2) + lax.div(p, 2), 2)
        return 2 * high + lax.rem(z + p, 2)

    up, down, far = lax.rem(y + 1, RING), lax.rem(y + 3, RING), lax.rem(y + 2, RING)

    def at_y(yy):
        return {"ctx": yy * RING + z}

    def at_z(zz):
        return {"ctx": y * RING + zz}

    def across(zz):
        return {"ctx": y * RING + zz, "grp": other}

    def at_x(xx):
        return {"head": xx * 2 + core}

    sibling = {"head": x * 2 + 1 - core}

    def send(src, dst, ssem, rsem, device):
        return pltpu.make_async_remote_copy(
            src_ref=src, dst_ref=dst, send_sem=ssem, recv_sem=rsem, device_id=device, device_id_type=MESH
        )

    def arrived(dst, rsem):
        send(dst, dst, s.loc.at[0], rsem, sibling).wait_recv()

    pairs = [
        (pkv.at[0], s.kl.at[pl.ds(0, PRE)]),
        (skv.at[0], s.kl.at[pl.ds(PRE, SPAN)]),
        (pkv.at[1], s.vb.at[y, pl.ds(0, PRE)]),
        (skv.at[1], s.vb.at[y, pl.ds(PRE, SPAN)]),
    ]
    pairs += [(q_in.at[:, pl.ds(h * HD, HD)], s.qb.at[z, pl.ds(h * SPAN, SPAN)]) for h in range(GQ)]
    pairs += [(dq, s.dq), (nkv, s.nkv), (clen_in, s.clen), (cache.at[0], s.ck), (cache.at[1], s.cv), (w_in, s.wb)]
    loads = [pltpu.make_async_copy(src, dst, s.loc.at[at]) for at, (src, dst) in enumerate(pairs)]
    for load in loads:
        load.start()

    barrier = pltpu.get_barrier_semaphore()
    greeted = [at_y(lax.rem(y + d, RING)) for d in (1, 2, 3)] + [at_z(lax.rem(z + d, RING)) for d in (1, 2, 3)]
    greeted += [across(zz) for zz in range(RING)] + [sibling] + [at_x(lax.rem(x + d, RING)) for d in (1, 2, 3)]
    for device in greeted:
        pl.semaphore_signal(barrier, inc=1, device_id=device, device_id_type=MESH)

    def clear(p, carry):
        s.acc[p] = jnp.zeros((GQ * SPAN, HD), F32)
        s.tot[p] = jnp.zeros((GQ * SPAN, HD), F32)
        s.top[p] = jnp.full((GQ * SPAN, HD), MASKED, F32)
        slot = iota((HD, KEYS), 1)
        unused = ((p * RING + z) * PRE + slot >= plen[0]) & (slot < PRE) & (iota((HD, KEYS), 0) == 0)
        s.kb[p, HD : 2 * HD, :] = jnp.where(unused, MASKED, 0.0).astype(BF16)
        return carry

    lax.fori_loop(0, RING, clear, 0)


    for load in loads[2:12]:
        load.wait()
    pl.semaphore_wait(barrier, len(greeted))

    def keys_of(yy):
        return s.kb.at[yy, pl.ds(0, HD)]

    kv_own = [
        send(s.vb.at[y], s.vb.at[y], s.kvs.at[0], s.vr.at[y], at_y(up)),
        send(s.vb.at[y], s.vb.at[y], s.kvs.at[1], s.vr.at[y], at_y(down)),
        send(keys_of(y), keys_of(y), s.kvs.at[2], s.kr.at[y], at_y(up)),
        send(keys_of(y), keys_of(y), s.kvs.at[3], s.kr.at[y], at_y(down)),
    ]
    kv_on = [
        send(keys_of(down), keys_of(down), s.kvs.at[4], s.kr.at[down], at_y(up)),
        send(s.vb.at[up], s.vb.at[up], s.kvs.at[5], s.vr.at[up], at_y(down)),
    ]

    def q_copy(source, step, sem):
        return send(s.qb.at[source], s.qb.at[source], s.qs.at[sem], s.qr.at[source], at_z(z + step))

    def a_copy(source, step, sem):
        block = s.ab.at[y, source]
        return send(block, block, s.as_.at[sem], s.ar.at[source], at_z(z + step))

    q_first = [(z < 3, z, 1, 0), (z > 0, z, -1, 1)]
    q_second = [((z > 0) & (z < 3), z - 1, 1, 2), ((z > 0) & (z < 3), z + 1, -1, 3)]
    q_third = [(z == 2, z - 2, 1, 4), (z == 1, z + 2, -1, 5)]

    def z_start(copy, group):
        for when, source, step, sem in group:

            @pl.when(when)
            def _(source=source, step=step, sem=sem):
                copy(source, step, sem).start()

    def z_wait(block, sems, distance):
        @pl.when(z >= distance)
        def _():
            arrived(block(z - distance), sems.at[z - distance])

        @pl.when(z + distance < RING)
        def _():
            arrived(block(z + distance), sems.at[z + distance])

    def q_wait(distance):
        z_wait(lambda source: s.qb.at[source], s.qr, distance)

    def a_wait(distance):
        z_wait(lambda source: s.ab.at[y, source], s.ar, distance)

    def b_copy(d):
        return send(s.sb.at[y], s.sb.at[y], s.bs.at[d], s.br.at[y], at_y(lax.rem(y + d, RING)))

    for copy in kv_own[:2]:
        copy.start()
    z_start(q_copy, q_first)
    for load in loads[:2]:
        load.wait()
    s.kb[y, 0:HD, :] = s.kl[...].T
    for copy in kv_own[2:]:
        copy.start()

    for load in loads[12:15]:
        load.wait()
    for r in range(ROWS):
        row = s.dq[r].astype(F32)
        for h in range(GQ):
            s.qf[pl.ds(r * QROWS + h, STEPS, stride=GQ), :] = row[:, h * HD : (h + 1) * HD]
    s.kn[...] = jnp.zeros((HD, HD), F32)
    s.vn[...] = jnp.zeros((HD, HD), F32)
    for r in range(ROWS):
        s.kn[pl.ds(r * STEPS, STEPS), :] = s.nkv[0, r].astype(F32)
        s.vn[pl.ds(r * STEPS, STEPS), :] = s.nkv[1, r].astype(F32)

    def picked(ref):
        total = jnp.zeros((QROWS, HD), F32)
        for r in range(ROWS):
            mine = jnp.where(me * ROWS + r == prow[0], 1.0, 0.0)
            total = total + mine * ref[r * QROWS : (r + 1) * QROWS, :]
        return total

    s.sb[y] = picked(s.qf).astype(BF16)

    for d in (1, 2, 3):
        b_copy(d).start()

    lanes = (ROWS * QROWS, HD)
    at_row, at_key = iota(lanes, 0), iota(lanes, 1)
    same = lax.shift_right_logical(at_row, 5) == lax.shift_right_logical(at_key, 2)
    early = jnp.bitwise_and(at_key, 3) <= jnp.bitwise_and(lax.shift_right_logical(at_row, 3), 3)
    new = jnp.where(same & early, dot_nt(s.qf[...].astype(BF16), s.kn[...].astype(BF16)) * SCALE, MASKED)
    new_top = jnp.max(new, axis=1, keepdims=True)
    new_weights = jnp.exp2(new - new_top)
    s.mf[...] = jnp.broadcast_to(new_top, lanes)
    s.lf[...] = jnp.broadcast_to(jnp.sum(new_weights, axis=1, keepdims=True), lanes)
    s.of[...] = dot_nn(new_weights.astype(BF16), s.vn[...].astype(BF16))

    for load in loads[15:]:
        load.wait()

    def cached(r):
        rows = pl.ds(pl.multiple_of(r * QROWS, QROWS), QROWS)
        scores = dot_nt(s.qf[rows, :].astype(BF16), s.ck[r]) * SCALE
        scores = jnp.where(iota((QROWS, SLOTS), 1) < s.clen[0, r], scores, MASKED)
        before = s.mf[rows, :]
        after = jnp.maximum(before, jnp.max(scores, axis=1, keepdims=True))
        weights = jnp.exp2(scores - after[:, :1])
        keep = jnp.exp2(before - after)
        total = s.lf[rows, :] * keep + jnp.sum(weights, axis=1, keepdims=True)
        mixed = s.of[rows, :] * keep + dot_nn(weights.astype(BF16), s.cv[r])
        s.of[rows, :] = mixed / total
        s.lf[rows, :] = after + log2(total)

    def first_queries():
        q_wait(1)
        z_start(q_copy, q_second)

    def some_rows(i, carry):
        for u in range(8):
            cached(i * 8 + u)
        return carry

    lax.fori_loop(0, ROWS // 8, some_rows, 0)
    for h in range(GQ):
        s.ab[y, z, h] = s.of[pl.ds(h, ROWS * STEPS, stride=GQ), :].astype(BF16)

    def ay_copy(yy, p, sem, to):
        block = s.ab.at[yy, near(p)]
        return send(block, block, s.ays.at[sem], s.ayr.at[yy, near(p)], at_y(to))

    def ay_own(p):
        return [ay_copy(y, p, 3 * p, up), ay_copy(y, p, 3 * p + 1, down)]

    def ay_on(p):
        return ay_copy(down, p, 3 * p + 2, up) if p < 2 else ay_copy(up, p, 3 * p + 2, down)

    def rows_in(yy, p):
        arrived(s.ab.at[yy, near(p)], s.ayr.at[yy, near(p)])

    def spread_rows(p):
        if p:
            a_wait(p)
            z_start(a_copy, (q_second, q_third, [])[p - 1])
        for copy in ay_own(p):
            copy.start()

    def pass_rows(p):
        rows_in(down if p < 2 else up, p)
        ay_on(p).start()

    def rest_of_rows():
        for p in range(RING):
            rows_in(up if p < 2 else down, p)

    def far_rows():
        for p in range(RING):
            rows_in(far, p)

    z_start(a_copy, q_first)
    spread_rows(0)
    s.sl[z] = jnp.broadcast_to(to_row(picked(s.lf)), (8, HD))

    def x_copy(d):
        zz = lax.rem(z + d, RING)
        return send(s.sx, s.xb.at[z], s.xs.at[d], s.xr.at[z], across(zz))

    def pass_query():
        for d in (1, 2, 3):
            yy = lax.rem(y + d, RING)
            arrived(s.sb.at[yy], s.br.at[yy])
        total = s.sb[0].astype(F32)
        for yy in (1, 2, 3):
            total = total + s.sb[yy].astype(F32)
        s.sx[...] = total.astype(BF16)
        for d in range(RING):
            x_copy(d).start()

    def h_copies(d):
        zz = lax.rem(z + d, RING)
        copies = [
            send(s.hos, s.ho.at[z], s.hs.at[d], s.hr.at[z], across(zz)),
            send(s.hls, s.hl.at[z], s.hls_s.at[d], s.hlr.at[z], across(zz)),
        ]
        if d:
            copies.append(send(s.sl.at[z], s.sl.at[z], s.sls.at[d], s.slr.at[z], at_z(zz)))
        return copies

    def answer():
        for zz in range(RING):
            arrived(s.xb.at[zz], s.xr.at[zz])
        query = s.xb[0].astype(F32)
        for zz in (1, 2, 3):
            query = query + s.xb[zz].astype(F32)
        span = pl.ds(PRE, SPAN)
        scores = dot_nn(query.astype(BF16), s.kb[y, 0:HD, span]) * SCALE
        top = jnp.max(scores, axis=1, keepdims=True)
        weights = jnp.exp2(scores - top)
        total = jnp.sum(weights, axis=1, keepdims=True)
        s.hos[...] = (dot_nn(weights.astype(BF16), s.vb[y, span, :]) / total).astype(BF16)
        level = jnp.broadcast_to(top + log2(total), (QROWS, HD))
        s.hls[...] = jnp.broadcast_to(to_row(level), (8, HD))
        for d in range(RING):
            for copy in h_copies(d):
                copy.start()

    def h2_copies(d):
        yy = lax.rem(y + d, RING)
        return [
            send(s.ho2.at[y], s.ho2.at[y], s.h2s.at[d], s.h2r.at[y], at_y(yy)),
            send(s.hl2.at[y], s.hl2.at[y], s.hl2s.at[d], s.hl2r.at[y], at_y(yy)),
        ]

    def combine_z():
        for zz in range(RING):
            arrived(s.ho.at[zz], s.hr.at[zz])
            arrived(s.hl.at[zz], s.hlr.at[zz])
        for d in (1, 2, 3):
            zz = lax.rem(z + d, RING)
            arrived(s.sl.at[zz], s.slr.at[zz])
        out, level = merge([(s.ho[zz].astype(F32), to_column(s.hl[zz, 0:1, :], QROWS)) for zz in range(RING)])
        s.ho2[y] = out.astype(BF16)
        s.hl2[y, 0:8, :] = jnp.broadcast_to(to_row(jnp.broadcast_to(level, (QROWS, HD))), (8, HD))
        s.hl2[y, 8:16, :] = s.sl[0] + s.sl[1] + s.sl[2] + s.sl[3]
        for d in (1, 2, 3):
            for copy in h2_copies(d):
                copy.start()

    def combine_y():
        for d in (1, 2, 3):
            yy = lax.rem(y + d, RING)
            arrived(s.ho2.at[yy], s.h2r.at[yy])
            arrived(s.hl2.at[yy], s.hl2r.at[yy])
        out, level = merge([(s.ho2[yy].astype(F32), to_column(s.hl2[yy, 0:1, :], QROWS)) for yy in range(RING)])
        rows = s.hl2[0, 8:9, :] + s.hl2[1, 8:9, :] + s.hl2[2, 8:9, :] + s.hl2[3, 8:9, :]
        before = to_column(rows, QROWS)
        top = jnp.maximum(before, level)
        w_own, w_span = jnp.exp2(before - top), jnp.exp2(level - top)
        total = w_own + w_span
        keep = jnp.broadcast_to(w_own / total, (QROWS, HD))
        added = out * (w_span / total)
        for at in range(2):
            s.wt[pl.ds(at * QROWS, QROWS), :] = keep
            s.ot[pl.ds(at * QROWS, QROWS), :] = added

    def si_copy(j):
        return send(s.so.at[j], s.si.at[j], s.sis.at[j], s.sir.at[j], sibling)

    def project(j):
        yc = turned(j)
        count = RING * ROWS * STEPS
        row = yc * (RING * ROWS) + lax.shift_right_logical(iota((count, HD), 0), 2)
        hit = row == prow[0]
        for h in range(GQ):
            block = jnp.concatenate([s.ab[yc, zz, h] for zz in range(RING)], axis=0).astype(F32)
            keep = s.wt[pl.ds(h, 2 * STEPS, stride=GQ), :]
            added = s.ot[pl.ds(h, 2 * STEPS, stride=GQ), :]
            keep = jnp.concatenate([keep] * (count // (2 * STEPS)), axis=0)
            added = jnp.concatenate([added] * (count // (2 * STEPS)), axis=0)
            block = jnp.where(hit, block * keep + added, block)
            s.am[:, h * HD : (h + 1) * HD] = block.astype(BF16)
        s.pr[...] = dot_nn(s.am[...], s.wb[...])
        s.pm[j] = s.pr[pl.ds(pl.multiple_of(core * 128, 128), 128), :]
        s.so[j] = s.pr[pl.ds(pl.multiple_of((1 - core) * 128, 128), 128), :].astype(BF16)
        si_copy(j).start()

    def xi_copy(j):
        return send(s.xo.at[j], s.xi.at[x], s.xis.at[j], s.xir.at[x], at_x(turned(j)))

    def join(j):
        arrived(s.si.at[j], s.sir.at[j])
        total = s.pm[j] + s.si[j].astype(F32)

        @pl.when(turned(j) == x)
        def _():
            s.own[...] = total

        @pl.when(turned(j) != x)
        def _():
            s.xo[j] = total.astype(BF16)
            xi_copy(j).start()

    first_lane = jnp.where(iota((BLOCK, HD), 1) == 0, 1.0, 0.0).astype(BF16)
    ones = jnp.ones((KEYS, HD), BF16)

    def scores_of(at, b, held):
        p, yc = piece_of(at), turned(chunk_of(at))
        queries = jnp.concatenate([s.qb[near(p), b * BLOCK : (b + 1) * BLOCK, :], first_lane], axis=1)
        held[...] = dot_nn(queries, s.kb[yc])

    def weigh(at, b, held):
        p, yc = piece_of(at), turned(chunk_of(at))
        late = (y * RING + near(p)) * SPAN - (yc * RING + z) * SPAN
        shape = (SPAN, SPAN)
        s.ahead[...] = jnp.where(iota(shape, 1) - iota(shape, 0) <= late, 0.0, MASKED)
        for i in range(0, BLOCK, 32):
            mine = slice(i, i + 32)
            rows = slice(b * BLOCK + i, b * BLOCK + i + 32)
            tiles = [held[mine, k * HD : (k + 1) * HD] for k in range(KEYS // HD)]
            tiles[-1] = tiles[-1] + s.ahead[i % SPAN : i % SPAN + 32, :]
            highest = tiles[0]
            for part in tiles[1:]:
                highest = jnp.maximum(highest, part)
            before = s.top[p, rows, :]
            after = jnp.maximum(before, jnp.max(highest, axis=1, keepdims=True))
            s.top[p, rows, :] = after
            s.kp[mine, :] = jnp.exp2((before - after) * SCALE)
            for k, part in enumerate(tiles):
                s.pk[mine, k * HD : (k + 1) * HD] = jnp.exp2((part - after) * SCALE).astype(BF16)
        rows = slice(b * BLOCK, (b + 1) * BLOCK)
        mixed = dot_nn(s.pk[...], jnp.concatenate([s.vb[yc], ones], axis=1))
        s.tot[p, rows, :] = s.tot[p, rows, :] * s.kp[...] + mixed[:, HD:]
        s.acc[p, rows, :] = s.acc[p, rows, :] * s.kp[...] + mixed[:, :HD]

    def o_copies(p):
        return [
            send(s.os.at[p], s.orb.at[p], s.ops.at[p], s.opr.at[p], at_z(near(p))),
            send(s.ls.at[p], s.lrb.at[p], s.lps.at[p], s.lpr.at[p], at_z(near(p))),
        ]

    def each_head(one):
        def some(i, carry):
            for u in range(4):
                one(i * 4 + u)
            return carry

        lax.fori_loop(0, GQ // 4, some, 0)

    def ship(p):
        def one(h):
            rows = pl.ds(pl.multiple_of(h * SPAN, SPAN), SPAN)
            total = s.tot[p, rows, :]
            s.os[p, h] = (s.acc[p, rows, :] / total).astype(BF16)
            s.ls[p, pl.ds(h, 1), :] = to_row(s.top[p, rows, :] * SCALE + log2(total))

        each_head(one)
        for copy in o_copies(p):
            copy.start()

    def settle():
        def one(h):
            rows = pl.ds(pl.multiple_of(h * SPAN, SPAN), SPAN)
            levels = [to_column(s.lrb[p, pl.ds(h, 1), :], SPAN) for p in (1, 2, 3)]
            own = s.top[0, rows, :] * SCALE
            top = own
            for level in levels:
                top = jnp.maximum(top, level)
            weight = jnp.exp2(own - top)
            total = s.tot[0, rows, :] * weight
            mixed = s.acc[0, rows, :] * weight
            for p, level in zip((1, 2, 3), levels):
                weight = jnp.exp2(level - top)
                total = total + weight
                mixed = mixed + s.orb[p, h].astype(F32) * weight
            out_p[:, pl.ds(pl.multiple_of(h * HD, HD), HD)] = (mixed / total).astype(BF16)

        each_head(one)

    def pass_values():
        arrived(s.vb.at[up], s.vr.at[up])
        kv_on[1].start()

    def pass_keys():
        arrived(keys_of(down), s.kr.at[down])
        kv_on[0].start()

    def keys_near():
        arrived(s.vb.at[down], s.vr.at[down])
        arrived(keys_of(up), s.kr.at[up])

    def keys_far():
        arrived(keys_of(far), s.kr.at[far])
        arrived(s.vb.at[far], s.vr.at[far])

    def second_queries():
        q_wait(2)
        z_start(q_copy, q_third)

    actions = {
        1: [first_queries, pass_values],
        2: [pass_keys, second_queries, pass_query],
        3: [keys_near, lambda: spread_rows(1)],
        4: [answer],
        5: [keys_far, lambda: pass_rows(0)],
        6: [lambda: q_wait(3), lambda: spread_rows(2)],
        7: [combine_z, lambda: pass_rows(1)],
        8: [lambda: spread_rows(3)],
        9: [combine_y, lambda: pass_rows(2)],
        10: [lambda: pass_rows(3)],
        12: [rest_of_rows],
        14: [far_rows],
    }

    def prepare(i):
        for at, todo in actions.items():

            @pl.when(i == at)
            def _(todo=todo):
                for action in todo:
                    action()

        @pl.when((i == 11) | ((i >= 13) & (i < 16)))
        def _():
            join(jnp.maximum(i - 12, 0))

        @pl.when((i == 10) | ((i >= 12) & (i < 15)))
        def _():
            project(jnp.maximum(i - 11, 0))

    def step(i, carry):
        scores_of(i, 1, s.ts1)
        weigh(i, 0, s.ts0)
        prepare(i + 1)
        scores_of(jnp.minimum(i + 1, 15), 0, s.ts0)
        weigh(i, 1, s.ts1)
        p, k = piece_of(i), chunk_of(i)

        @pl.when((k == 3) & (p > 0))
        def _():
            ship(p)

        return carry

    scores_of(jnp.int32(0), 0, s.ts0)
    lax.fori_loop(0, 16, step, 0)
    for p in (1, 2, 3):
        arrived(s.orb.at[p], s.opr.at[p])
        arrived(s.lrb.at[p], s.lpr.at[p])
    settle()

    total = s.own[...]
    for d in (1, 2, 3):
        xx = lax.rem(x + d, RING)
        arrived(s.xi.at[xx], s.xir.at[xx])
        total = total + s.xi[xx].astype(F32)
    for r in range(32):
        out_d[r] = total[r * STEPS : (r + 1) * STEPS, :].astype(BF16)

    for copy in kv_own + kv_on + [c for p in range(RING) for c in ay_own(p) + [ay_on(p)]]:
        copy.wait_send()
    for when, source, step_z, sem in q_first + q_second + q_third:

        @pl.when(when)
        def _(source=source, step_z=step_z, sem=sem):
            q_copy(source, step_z, sem).wait_send()
            a_copy(source, step_z, sem).wait_send()

    for d in range(RING):
        x_copy(d).wait_send()
        for copy in h_copies(d):
            copy.wait_send()
        if d:
            b_copy(d).wait_send()
            for copy in h2_copies(d):
                copy.wait_send()
            for copy in o_copies(d):
                copy.wait_send()
    for j in range(RING):
        si_copy(j).wait_send()

        @pl.when(turned(j) != x)
        def _(j=j):
            xi_copy(j).wait_send()


def shards(span_q, span_kv, prefix_kv, prefix_len, dec_q, dec_new_kv, dec_cache, cache_len, prompt_row, out_weight):
    vmem = pl.BlockSpec(memory_space=pltpu.VMEM)
    smem = pl.BlockSpec(memory_space=pltpu.SMEM)
    hbm = pl.BlockSpec(memory_space=pltpu.HBM)
    prefill, decode = pl.pallas_call(
        kernel,
        out_shape=(
            jax.ShapeDtypeStruct((SPAN, GQ * HD), BF16),
            jax.ShapeDtypeStruct((32, STEPS, COLS), BF16),
        ),
        in_specs=[smem] * 2 + [hbm] * 8,
        out_specs=(vmem, vmem),
        scratch_shapes=list(SCRATCH.values()),
        compiler_params=pltpu.CompilerParams(
            collective_id=0, has_side_effects=True, vmem_limit_bytes=VMEM_BYTES
        ),
        cost_estimate=pl.CostEstimate(flops=11_000_000_000, bytes_accessed=8_000_000, transcendentals=17_000_000),
    )(
        prefix_len,
        prompt_row,
        *[
            pltpu.with_memory_space_constraint(operand, pltpu.HBM)
            for operand in (
                cache_len,
                span_q[0],
                span_kv[0],
                prefix_kv[0],
                dec_q[0],
                dec_new_kv[0],
                dec_cache[0],
                out_weight,
            )
        ],
    )
    return prefill[None], decode[None]


def solution(mesh):
    placed = (
        P("grp", "ctx", "head"),
        P("grp", None, "ctx", "head"),
        P("grp", None, "ctx", "head"),
        P("grp"),
        P("grp", "ctx", None, "head"),
        P("grp", None, "ctx", None, "head"),
        P("grp", None, "ctx", None, "head"),
        P("grp", "ctx"),
        P("grp"),
        P("head", "ctx"),
    )
    return jax.shard_map(
        shards,
        mesh=mesh,
        in_specs=placed,
        out_specs=(P("grp", "ctx", "head"), P("grp", "head", None, "ctx")),
        check_vma=False,
    )
```
